128 devices in a mesh: ctx: 8 (over x, z_lo), fsdp: 16 (over z_hi, y, core).
Axes of the slice: x: 4, y: 4, z: 4 (z_hi: 2, z_lo: 2; z = z_hi * 2 + z_lo), core: 2. Of those that a mesh axis runs over, the one named last changes fastest.
Arguments:
- tokens: bfloat16 [16, 2048, 640], P('fsdp', 'ctx'), may hold values from -6 to 6
- cotangent: bfloat16 [16, 2048, 640], P('fsdp', 'ctx'), may hold values from -6 to 6
- starts: int32 [16], P('fsdp'), may hold values from 1 to 255
- qkv_weight: float32 [640, 1536], P(('ctx', 'fsdp')), may hold values from -0.25 to 0.25
- qkv_first: float32 [640, 1536], P(('ctx', 'fsdp')), may hold values from -34.393674 to 34.393674
- qkv_second: float32 [640, 1536], P(('ctx', 'fsdp')), may hold values from 1726.8736 to 6881.28
- out_weight: float32 [1024, 640], P(('ctx', 'fsdp')), may hold values from -2 to 2
- out_first: float32 [1024, 640], P(('ctx', 'fsdp')), may hold values from -3.04 to 3.04
- out_second: float32 [1024, 640], P(('ctx', 'fsdp')), may hold values from 13.4912 to 53.76
- gate_up_weight: float32 [640, 4096], P(('ctx', 'fsdp')), may hold values from -0.25 to 0.25
- gate_up_first: float32 [640, 4096], P(('ctx', 'fsdp')), may hold values from -12.16 to 12.16
- gate_up_second: float32 [640, 4096], P(('ctx', 'fsdp')), may hold values from 215.8592 to 860.16
- down_weight: float32 [2048, 640], P(('ctx', 'fsdp')), may hold values from -0.125 to 0.125
- down_first: float32 [2048, 640], P(('ctx', 'fsdp')), may hold values from -19.85659 to 19.85659
- down_second: float32 [2048, 640], P(('ctx', 'fsdp')), may hold values from 575.5894 to 2293.62
- norm_gains: float32 [2, 640], P(None, ('ctx', 'fsdp')), may hold values from 0.25 to 1.75
- gains_first: float32 [2, 640], P(None, ('ctx', 'fsdp')), may hold values from -34.393674 to 34.393674
- gains_second: float32 [2, 640], P(None, ('ctx', 'fsdp')), may hold values from 1726.8736 to 6881.28
Outputs:
- layer_out: float32 [16, 2048, 640], P('fsdp', 'ctx')
- input_grad: float32 [16, 2048, 640], P('fsdp', 'ctx')
- next_qkv: float32 [640, 1536], P(('ctx', 'fsdp'))
- next_qkv_first: float32 [640, 1536], P(('ctx', 'fsdp'))
- next_qkv_second: float32 [640, 1536], P(('ctx', 'fsdp'))
- next_out: float32 [1024, 640], P(('ctx', 'fsdp'))
- next_out_first: float32 [1024, 640], P(('ctx', 'fsdp'))
- next_out_second: float32 [1024, 640], P(('ctx', 'fsdp'))
- next_gate_up: float32 [640, 4096], P(('ctx', 'fsdp'))
- next_gate_up_first: float32 [640, 4096], P(('ctx', 'fsdp'))
- next_gate_up_second: float32 [640, 4096], P(('ctx', 'fsdp'))
- next_down: float32 [2048, 640], P(('ctx', 'fsdp'))
- next_down_first: float32 [2048, 640], P(('ctx', 'fsdp'))
- next_down_second: float32 [2048, 640], P(('ctx', 'fsdp'))
- next_gains: float32 [2, 640], P(None, ('ctx', 'fsdp'))
- next_gains_first: float32 [2, 640], P(None, ('ctx', 'fsdp'))
- next_gains_second: float32 [2, 640], P(None, ('ctx', 'fsdp'))
The draws below stay inside these ranges and needn't reach their ends.
All inputs are finite; a program needn't handle non-finite values.
Results may differ from the reference program's by a relative error of at most 0.034.
Values may be sent and summed in bfloat16 or wider, within the bound.
A program may use at most 128 MiB of HBM per device.

```python
import math
import jax
import jax.numpy as jnp
from jax import lax

D = 640
HEADS = 4
HEAD = 256
FF = 2048
WINDOW = 512
STEP = 10
TOK_DEV = 256
QW = 1024
OUT_FAN = 8
LENGTH = 2048
ROWS = 16
TOKENS = 32768


def first_moment(key, dims_shape, square):
    uniform_draw = jax.random.uniform(key, dims_shape, jnp.float32, -1.0, 1.0)
    return uniform_draw * (0.19 * math.sqrt(square))


def second_moment(key, dims_shape, square):
    uniform_draw = jax.random.uniform(key, dims_shape, jnp.float32, math.log(0.0527), math.log(0.21))
    return jnp.exp(uniform_draw) * square


def draw_qkv_first(key, part):
    key = jax.random.fold_in(key, 11)
    return first_moment(key, (D, QW + 2 * HEAD), TOKENS)


def draw_qkv_second(key, part):
    key = jax.random.fold_in(key, 12)
    return second_moment(key, (D, QW + 2 * HEAD), TOKENS)


def draw_out_first(key, part):
    key = jax.random.fold_in(key, 13)
    return first_moment(key, (QW, D), TOKENS * 4 // WINDOW)


def draw_out_second(key, part):
    key = jax.random.fold_in(key, 14)
    return second_moment(key, (QW, D), TOKENS * 4 // WINDOW)


def draw_gate_up_first(key, part):
    key = jax.random.fold_in(key, 15)
    return first_moment(key, (D, 2 * FF), TOKENS // 8)


def draw_gate_up_second(key, part):
    key = jax.random.fold_in(key, 16)
    return second_moment(key, (D, 2 * FF), TOKENS // 8)


def draw_down_first(key, part):
    key = jax.random.fold_in(key, 17)
    return first_moment(key, (FF, D), TOKENS // 3)


def draw_down_second(key, part):
    key = jax.random.fold_in(key, 18)
    return second_moment(key, (FF, D), TOKENS // 3)


def draw_gains_first(key, part):
    key = jax.random.fold_in(key, 19)
    return first_moment(key, (2, D), TOKENS)


def draw_gains_second(key, part):
    key = jax.random.fold_in(key, 20)
    return second_moment(key, (2, D), TOKENS)


def with_ends(values, stream_key, smallest, high):
    dims = values.shape
    spot = [jax.random.randint(jax.random.fold_in(stream_key, axis), (), 0, dims[axis]) for axis in range(len(dims))]
    values = values.at[tuple(spot)].set(smallest)
    longest = dims.index(max(dims))
    spot[longest] = (spot[longest] + 1) % dims[longest]
    return values.at[tuple(spot)].set(high)


def block_scale(key, extent, split, smallest, largest):
    level = 1.0
    for position, blocks in split:
        draws = jax.random.uniform(jax.random.fold_in(jax.random.fold_in(key, 6), position), (blocks,), jnp.float32, smallest / len(split), largest / len(split))
        level = level * jnp.repeat(jnp.exp(draws), extent[position] // blocks).reshape((-1,) + (1,) * (len(extent) - 1 - position))
    return level


def scatter_about(stream_key, extent, scale, most, cuts=(), kind=jnp.bfloat16):
    array = jax.random.normal(stream_key, extent, jnp.float32) * scale
    if len(cuts) > 0:
        array = block_scale(stream_key, extent, cuts, -0.22, 0.18) * array
    return jnp.clip(array, min=-most, max=most).astype(kind)


def setup_inputs(seed: int = 0) -> dict:
    key_of = jax.random.split(jax.random.key(seed), 19)
    tokens = scatter_about(key_of[0], (ROWS, LENGTH, D), 1.0, 6.0, ((0, 16), (1, 8)))
    cotangent = scatter_about(key_of[1], (ROWS, LENGTH, D), 1.0, 6.0, ((0, 16), (1, 8)))
    starts = with_ends(jax.random.randint(key_of[2], (ROWS,), 1, TOK_DEV), jax.random.fold_in(key_of[2], 1), 1, TOK_DEV - 1).astype(jnp.int32)
    qkv_weight = scatter_about(key_of[3], (D, QW + 2 * HEAD), D ** -0.5, 0.25, ((0, 128),), jnp.float32)
    qkv_first = draw_qkv_first(jax.random.fold_in(key_of[18], 71), 0)
    qkv_second = draw_qkv_second(jax.random.fold_in(key_of[18], 71), 0)
    out_weight = scatter_about(key_of[6], (QW, D), OUT_FAN ** -0.5, 2.0, ((0, 128),), jnp.float32)
    out_first = draw_out_first(jax.random.fold_in(key_of[18], 71), 0)
    out_second = draw_out_second(jax.random.fold_in(key_of[18], 71), 0)
    gate_up_weight = scatter_about(key_of[9], (D, 2 * FF), D ** -0.5, 0.25, ((0, 128),), jnp.float32)
    gate_up_first = draw_gate_up_first(jax.random.fold_in(key_of[18], 71), 0)
    gate_up_second = draw_gate_up_second(jax.random.fold_in(key_of[18], 71), 0)
    down_weight = scatter_about(key_of[12], (FF, D), FF ** -0.5, 0.125, ((0, 128),), jnp.float32)
    down_first = draw_down_first(jax.random.fold_in(key_of[18], 71), 0)
    down_second = draw_down_second(jax.random.fold_in(key_of[18], 71), 0)
    norm_gains = jnp.clip(1.0 + 0.15 * jax.random.normal(key_of[15], (2, D), jnp.float32), 0.25, 1.75)
    gains_first = draw_gains_first(jax.random.fold_in(key_of[18], 71), 0)
    gains_second = draw_gains_second(jax.random.fold_in(key_of[18], 71), 0)
    return {"tokens": tokens, "cotangent": cotangent, "starts": starts, "qkv_weight": qkv_weight, "qkv_first": qkv_first, "qkv_second": qkv_second, "out_weight": out_weight, "out_first": out_first, "out_second": out_second, "gate_up_weight": gate_up_weight, "gate_up_first": gate_up_first, "gate_up_second": gate_up_second, "down_weight": down_weight, "down_first": down_first, "down_second": down_second, "norm_gains": norm_gains, "gains_first": gains_first, "gains_second": gains_second}


@jax.custom_vjp
def low(v):
    return lax.optimization_barrier(v.astype(jnp.bfloat16)).astype(jnp.float32)

@jax.custom_vjp
def low_back(v):
    return v

def low_keep(v):
    return (low(v), None)

def low_pass(kept, grad):
    return (grad,)

def back_keep(v):
    return (v, None)

def back_low(kept, grad):
    return (low(grad),)
low.defvjp(low_keep, low_pass)
low_back.defvjp(back_keep, back_low)
exact_mode = lax.Precision.HIGHEST
eps_norm = 1e-06
beta_one = 0.9
beta_two = 0.95
eps_adam = 1e-08
weight_decay = 0.1
masked_score = -1e+30

def matmul(left, right):
    return jnp.dot(left, right, precision=exact_mode, preferred_element_type=jnp.float32)

def normed(field, gain_row):
    return field * lax.rsqrt(lax.optimization_barrier(jnp.mean(field * field, axis=-1, keepdims=True)) + eps_norm) * gain_row

def rotated(field, cos_table, sin_table):
    half_width = field.shape[-1] // 2
    first_half = field[..., :half_width]
    second_half = field[..., half_width:]
    return jnp.concatenate([first_half * cos_table - second_half * sin_table, second_half * cos_table + first_half * sin_table], axis=-1)

def forward(inputs, qkv_matrix, out_matrix, gate_up_matrix, down_matrix, gain_rows, boundary):
    length = inputs.shape[0]
    places = jnp.arange(length, dtype=jnp.int32)
    documents = (places >= boundary).astype(jnp.int32)
    half_width = HEAD // 2
    frequency = 10000.0 ** (-(2.0 * jnp.arange(half_width, dtype=jnp.float32)) / HEAD)
    angles = places.astype(jnp.float32)[:, None] * frequency[None, :]
    cos_table = jnp.cos(angles)
    sin_table = jnp.sin(angles)
    gains_low = low(gain_rows)
    first_normed = low(normed(inputs, gains_low[0]))
    projected = low_back(matmul(first_normed, low(qkv_matrix)))
    queries = projected[:, :QW].reshape(length, HEADS, HEAD)
    queries = low(rotated(queries, cos_table[:, None, :], sin_table[:, None, :]) * HEAD ** (-0.5))
    key_rows = low(rotated(projected[:, QW:QW + HEAD], cos_table, sin_table))
    value_rows = low(projected[:, QW + HEAD:])
    scores = low_back(jnp.einsum('qhd,kd->hqk', queries, key_rows, precision=exact_mode))
    distance = places[:, None] - places[None, :]
    allowed = (distance >= 0) & (distance < WINDOW) & (documents[:, None] == documents[None, :])
    scores = jnp.where(allowed[None], scores, masked_score)
    row_max = lax.optimization_barrier(jnp.max(scores, axis=-1, keepdims=True))
    exp_scores = jnp.exp(scores - row_max)
    soft_weights = low(exp_scores / lax.optimization_barrier(jnp.sum(exp_scores, axis=-1, keepdims=True)))
    mixed_heads = jnp.einsum('hqk,kd->qhd', soft_weights, value_rows, precision=exact_mode)
    mixed_heads = low_back(low(mixed_heads.reshape(length, QW)))
    first_out = inputs + low_back(matmul(mixed_heads, low(out_matrix)))
    second_normed = low(normed(first_out, gains_low[1]))
    gate_up = low_back(matmul(second_normed, low(gate_up_matrix)))
    hidden = low(jax.nn.gelu(gate_up[:, :FF], approximate=True) * gate_up[:, FF:])
    return first_out + low_back(matmul(hidden, low(down_matrix)))

def adamw(master, first_state, second_state, gradient, rate, decay_rate):
    first_next = beta_one * first_state + (1.0 - beta_one) * gradient
    second_next = beta_two * second_state + (1.0 - beta_two) * gradient * gradient
    first_fixed = first_next / (1.0 - beta_one ** STEP)
    second_fixed = second_next / (1.0 - beta_two ** STEP)
    master_next = master - rate * (first_fixed / (jnp.sqrt(second_fixed) + eps_adam) + decay_rate * master)
    return (master_next, first_next, second_next)

def reference(tokens, cotangent, starts, qkv_weight, qkv_first, qkv_second, out_weight, out_first, out_second, gate_up_weight, gate_up_first, gate_up_second, down_weight, down_first, down_second, norm_gains, gains_first, gains_second):
    masters = (qkv_weight, out_weight, gate_up_weight, down_weight, norm_gains)

    def row_step(running, row_data):
        row_tokens, row_pulled, boundary = row_data

        def wrapped(inputs, qkv_matrix, out_matrix, gate_up_matrix, down_matrix, gain_rows):
            return forward(inputs, qkv_matrix, out_matrix, gate_up_matrix, down_matrix, gain_rows, boundary)
        result, pull = jax.vjp(wrapped, row_tokens.astype(jnp.float32), *masters)
        grads = pull(row_pulled.astype(jnp.float32))
        running = tuple((earlier + latest for earlier, latest in zip(running, grads[1:])))
        return (running, (result, grads[0]))
    zeros = tuple((jnp.zeros_like(master) for master in masters))
    sums, (layer_out, input_grad) = lax.scan(row_step, zeros, (tokens, cotangent, starts))
    qkv_new = adamw(qkv_weight, qkv_first, qkv_second, sums[0], 1.5 * D ** (-0.5), weight_decay)
    out_new = adamw(out_weight, out_first, out_second, sums[1], 1.5 * OUT_FAN ** (-0.5), weight_decay)
    gate_up_new = adamw(gate_up_weight, gate_up_first, gate_up_second, sums[2], 1.5 * D ** (-0.5), weight_decay)
    down_new = adamw(down_weight, down_first, down_second, sums[3], 1.5 * FF ** (-0.5), weight_decay)
    gains_new = adamw(norm_gains, gains_first, gains_second, sums[4], 0.5, 0.0)
    return (layer_out, input_grad, qkv_new[0], qkv_new[1], qkv_new[2], out_new[0], out_new[1], out_new[2], gate_up_new[0], gate_up_new[1], gate_up_new[2], down_new[0], down_new[1], down_new[2], gains_new[0], gains_new[1], gains_new[2])
```

```python
import functools

import jax
import jax.numpy as jnp
import numpy as np
from jax import lax
from jax.experimental import pallas as pl
from jax.experimental.pallas import tpu as pltpu
from jax.sharding import PartitionSpec as P

D = 640
HEADS = 4
HEAD = 256
FF = 2048
WINDOW = 512
STEP = 10
QW = 1024
OUT_FAN = 8
TOK = 256
LENGTH = 2048

eps_norm = 1e-06
beta_one = 0.9
beta_two = 0.95
eps_adam = 1e-08
weight_decay = 0.1
masked_score = -1e30

MESH = pl.DeviceIdType.MESH
BF = jnp.bfloat16
F32 = jnp.float32


class Place:
    def __init__(self):
        self.ctx = lax.axis_index("ctx")
        self.fsdp = lax.axis_index("fsdp")
        self.x = lax.div(self.ctx, 2)
        self.zl = lax.rem(self.ctx, 2)
        self.zh = lax.div(self.fsdp, 8)
        self.y = lax.div(lax.rem(self.fsdp, 8), 2)
        self.k = lax.rem(self.fsdp, 2)
        self.z = 2 * self.zh + self.zl


def device(x, y, z, k):
    return (2 * x + lax.rem(z, 2), 8 * lax.div(z, 2) + 2 * y + k)


def around(a, b):
    return lax.rem(a + b, 4)


def plane_chip(me, last, j):
    a, b = lax.rem(j, 4), lax.div(j, 4)
    if last == XA:
        return me.x, around(me.y, a), around(me.z, b)
    if last == YA:
        return around(me.x, a), me.y, around(me.z, b)
    return around(me.x, a), around(me.y, b), me.z


def line_chip(me, last, j):
    if last == XA:
        return around(me.x, j), me.y, me.z
    if last == YA:
        return me.x, around(me.y, j), me.z
    return me.x, me.y, around(me.z, j)


def along(me, last):
    return (me.x, me.y, me.z)[last]


def in_plane(last, x, y, z):
    if last == XA:
        return lax.rem(z, 2) * 8 + lax.div(z, 2) * 4 + y
    if last == YA:
        return 4 * x + z
    return 4 * x + y


def rows(start, size):
    return pl.ds(pl.multiple_of(start, 16), size)


def feature_order(last):
    order = np.zeros(D, np.int64)
    for x in range(4):
        for y in range(4):
            for z in range(4):
                for k in range(2):
                    dev = x * 32 + (z % 2) * 16 + (z // 2) * 8 + y * 2 + k
                    b, p = (y, 4 * x + z) if last == YA else (z, 4 * x + y)
                    for r in range(5):
                        order[b * 160 + k * 80 + p * 5 + r] = 5 * dev + r
    return order


def constants():
    orders = np.zeros((2, D, D), np.float32)
    for n, last in enumerate((YA, ZA)):
        orders[n, feature_order(last), np.arange(D)] = 1.0
    pick5 = np.zeros((3, 160, 512), np.float32)
    for g in range(3):
        for s in range(32):
            for r in range(5):
                pick5[g, s * 5 + r, s * 16 + g * 5 + r] = 1.0
    pick8 = np.zeros((2, 128, 256), np.float32)
    for g in range(2):
        for s in range(16):
            for r in range(8):
                pick8[g, s * 8 + r, s * 16 + g * 8 + r] = 1.0
    half = HEAD // 2
    frequency = np.float32(10000.0) ** (
        -(np.float32(2.0) * np.arange(half, dtype=np.float32)) / np.float32(HEAD)
    )
    angles = np.arange(LENGTH, dtype=np.float32)[:, None] * frequency.astype(np.float32)[None, :]
    rope = np.stack([np.cos(angles.astype(np.float64)), np.sin(angles.astype(np.float64))])
    return (
        jnp.asarray(orders, BF),
        jnp.asarray(pick5, BF),
        jnp.asarray(pick8, BF),
        jnp.asarray(rope.astype(np.float32)),
    )


def dot(a, b):
    return lax.dot_general(a, b, (((1,), (0,)), ((), ())), preferred_element_type=F32)


def dot_nt(a, b):
    return lax.dot_general(a, b, (((1,), (1,)), ((), ())), preferred_element_type=F32)


def dot_tn(a, b):
    return lax.dot_general(a, b, (((0,), (0,)), ((), ())), preferred_element_type=F32)


def rotate(u, cos, sin):
    a, b = u[:, :128], u[:, 128:]
    return jnp.concatenate([a * cos - b * sin, b * cos + a * sin], axis=1)


def column(row):
    n = row.shape[1]
    i = lax.broadcasted_iota(jnp.int32, (n, n), 0)
    j = lax.broadcasted_iota(jnp.int32, (n, n), 1)
    wide = jnp.broadcast_to(row.astype(BF).astype(F32), (n, n))
    return jnp.sum(jnp.where(i == j, wide, 0.0), axis=1, keepdims=True)


class Bag(dict):
    __getattr__ = dict.__getitem__


def scratch_list():
    def v(*shape, kind=BF):
        return pltpu.VMEM(shape, kind)

    qkv = [
        Bag(
            pk=v(16, 256),
            st=v(256, 256),
            w=v(640, 512),
            g=v(640, 512),
            r0=v(320, 512),
            gs=v(320, 512),
            r1=v(240, 512),
            gp=v(256, 256),
            r2=v(256, 256),
        )
        for n in range(3)
    ]
    out = Bag(
        pk=v(16, 384),
        st=v(256, 384),
        w=v(1024, 640),
        g=v(1024, 640),
        r0=v(512, 640),
        gs=v(512, 640),
        r1=v(384, 640),
        gp=v(256, 384),
        r2=v(256, 384),
    )
    gate_up = [
        Bag(
            pk=v(32, 384),
            st=v(512, 384),
            w=v(640, 1024),
            g=v(640, 1024),
            r1=v(480, 1024),
            gp=v(512, 384),
            r2=v(512, 384),
        )
        for n in range(2)
    ]
    down = Bag(
        pk=v(16, 640),
        w=v(1024, 640),
        g=v(1024, 640),
        r1=v(768, 640),
        gp=v(256, 640),
        r2=v(256, 640),
    )
    return Bag(
        part=qkv + [out] + gate_up + [down],
        xin=v(TOK, D),
        cin=v(TOK, D),
        orders=v(2, D, D),
        pick5=v(3, 160, 512),
        pick8=v(2, 128, 256),
        rope=v(2, TOK, 128, kind=F32),
        pad=v(16, 384, kind=F32),
        xn=v(3, TOK, D),
        qs=v(HEADS * TOK, HEAD),
        kv=v(3 * TOK, 2 * HEAD),
        bias=v(TOK, 3 * TOK, kind=F32),
        probs=v(HEADS * TOK, 3 * TOK),
        ds=v(HEADS * TOK, 3 * TOK),
        mixed=v(TOK, QW),
        dmix=v(HEADS * TOK, HEAD),
        x1=v(TOK, D, kind=F32),
        x2=v(2 * TOK, D),
        x2z=v(2 * TOK, D),
        dy2=v(2 * TOK, D),
        outp=v(2 * TOK, D, kind=F32),
        ex=v(2 * TOK, D, kind=F32),
        ez=v(2 * TOK, D, kind=F32),
        osend=v(TOK, D),
        orecv=v(TOK, D),
        esend=v(TOK, D),
        erecv=v(TOK, D),
        dx1=v(TOK, D, kind=F32),
        dq=v(TOK, 1536),
        dkv=v(TOK, 2 * HEAD, kind=F32),
        kvsend=v(2 * TOK, 2 * HEAD),
        kvrecv=v(2 * TOK, 2 * HEAD),
    )


def leaves(tree):
    if isinstance(tree, dict):
        return [leaf for branch in tree.values() for leaf in leaves(branch)]
    if isinstance(tree, list):
        return [leaf for branch in tree for leaf in leaves(branch)]
    return [tree]


def refill(tree, values):
    if isinstance(tree, dict):
        return Bag({key: refill(branch, values) for key, branch in tree.items()})
    if isinstance(tree, list):
        return [refill(branch, values) for branch in tree]
    return next(values)


OUT, GATE, UP, DOWN = 3, 4, 5, 6
A, B, C, DD, E, FR = range(6)
DY, X2, EE, OO, KV, DKV = range(7, 13)
XA, YA, ZA = range(3)
LAST = (XA, YA, ZA, XA, XA, ZA, YA)


SEMS = 64


def wait_for(ref, sem):
    pltpu.make_async_copy(ref, ref, sem).wait()


def step_kernel(shape, *refs):
    (tok, cot, starts, wq, wo, wgu, wd, gains, orders_h, pick5_h, pick8_h, rope_h) = refs[:12]
    (lo, ig, sq0, sq1, sq2, so, sg, su, sd) = refs[12:21]
    s = refill(shape, iter(refs[21:-3]))
    local, sent, came = refs[-3:]
    me = Place()
    sems = {}

    def sem_of(name):
        return sems.setdefault(name, len(sems))

    def remote(src, dst, name, target):
        n = sem_of(name)
        pltpu.make_async_remote_copy(
            src_ref=src,
            dst_ref=dst,
            send_sem=sent.at[n],
            recv_sem=came.at[n],
            device_id=target,
            device_id_type=MESH,
        ).start()

    def own_copy(src, dst, name):
        pltpu.make_async_copy(src, dst, came.at[sem_of(name)]).start()

    def arrived(ref, name):
        wait_for(ref, came.at[sem_of(name)])

    def left(ref, name):
        wait_for(ref, sent.at[sem_of(name)])

    sibling = device(me.x, me.y, me.z, 1 - me.k)

    fetch = [
        (tok.at[0], s.xin),
        (orders_h, s.orders),
        (pick5_h, s.pick5),
        (pick8_h, s.pick8),
        (rope_h.at[:, pl.ds(pl.multiple_of(me.ctx * TOK, TOK), TOK), :], s.rope),
        (cot.at[0], s.cin),
        (cot.at[0], s.dy2.at[pl.ds(0, TOK)]),
    ]
    fetches = [pltpu.make_async_copy(a, b, local.at[n]) for n, (a, b) in enumerate(fetch)]
    for one in fetches:
        one.start()

    barrier = pltpu.get_barrier_semaphore()

    def greet(j, carry):
        for last in range(3):
            chip = plane_chip(me, last, j)
            for core in range(2):
                pl.semaphore_signal(barrier, inc=1, device_id=device(*chip, core), device_id_type=MESH)
        return carry

    lax.fori_loop(1, 16, greet, 0)
    pl.semaphore_signal(barrier, inc=1, device_id=sibling, device_id_type=MESH)

    pad = s.pad
    pad[...] = jnp.zeros((16, 384), F32)
    wqb = wq[...].astype(BF).astype(F32) * column(gains[0:1, :])
    for n in range(3):
        for g in range(2):
            pad[5 * g : 5 * g + 5, 0:256] = wqb[:, n * 512 + g * 256 : n * 512 + g * 256 + 256]
        s.part[n].pk[...] = pad[:, 0:256].astype(BF)
    gain = column(gains[1:2, :])
    for n, name in enumerate((GATE, UP)):
        for c in range(2):
            for t in range(8):
                g, i = t // 3, t % 3
                base = n * FF + (t // 2) * 512 + c * 256 + (t % 2) * 128
                pad[5 * g : 5 * g + 5, i * 128 : i * 128 + 128] = (
                    wgu[:, base : base + 128].astype(BF).astype(F32) * gain
                )
            pad[10:15, 256:384] = jnp.zeros((5, 128), F32)
            s.part[name].pk[c * 16 : c * 16 + 16, :] = pad[...].astype(BF)
    pad[0:8, :] = wo[:, 0:384]
    pad[8:16, 0:256] = wo[:, 384:640]
    pad[8:16, 256:384] = jnp.zeros((8, 128), F32)
    s.part[OUT].pk[...] = pad[...].astype(BF)
    s.part[DOWN].pk[...] = wd[...].astype(BF)

    pl.semaphore_wait(barrier, 91)

    def spread_same(last, src, dst, name):
        slot = in_plane(last, me.x, me.y, me.z)
        place = dst.at[rows(slot * 16, 16)]
        own_copy(src, place, name)

        def send(j, carry):
            remote(src, place, name, device(*plane_chip(me, last, j), me.k))
            return carry

        lax.fori_loop(1, 16, send, 0)

    def spread_low(last, src, place, name):
        def send(j, carry):
            remote(src, place, name, device(*plane_chip(me, last, j), me.zl))
            return carry

        lax.fori_loop(1, 16, send, 0)

        @pl.when(me.zl == me.k)
        def _():
            own_copy(src, place, name)

        @pl.when(me.zl != me.k)
        def _():
            remote(src, place, name, sibling)

    def spread_both(last, src, slot, dst, name):
        place = dst.at[rows(slot * 16, 16)]

        def send(j, carry):
            for core in range(2):
                remote(
                    src.at[pl.ds(core * 16, 16)],
                    place,
                    name,
                    device(*plane_chip(me, last, j), core),
                )
            return carry

        lax.fori_loop(1, 16, send, 0)
        own_copy(src.at[rows(me.k * 16, 16)], place, name)
        remote(src.at[rows((1 - me.k) * 16, 16)], place, name, sibling)

    low_slot = (me.zh * 4 + me.y) * 2 + me.k
    spread_same(ZA, s.part[2].pk, s.part[2].st, (2, A))
    spread_same(YA, s.part[1].pk, s.part[1].st, (1, A))
    spread_low(XA, s.part[0].pk, s.part[0].st.at[rows(low_slot * 16, 16)], (0, A))

    fetches[0].wait()
    fetches[1].wait()
    x = s.xin[...].astype(F32)
    r0 = lax.rsqrt(jnp.mean(x * x, axis=1, keepdims=True) + eps_norm)
    xn = (x * r0).astype(BF)
    s.xn[0] = xn
    s.xn[1] = dot(xn, s.orders[0]).astype(BF)
    s.xn[2] = dot(xn, s.orders[1]).astype(BF)
    for n in range(2, len(fetches)):
        fetches[n].wait()
    remote(s.cin, s.dy2.at[pl.ds(TOK, TOK)], DY, sibling)

    def pass_on(last, ref, name, place, size):
        for j in range(1, 4):
            remote(
                ref.at[rows(place, size)],
                ref.at[rows(place, size)],
                name,
                device(*line_chip(me, last, j), me.k),
            )

    for n in (2, 1, 0):
        last = LAST[n]
        arrived(s.part[n].st, (n, A))
        place = along(me, last) * 160 + me.k * 80
        st = s.part[n].st[...]
        w = s.part[n].w
        for g in range(2):
            w[rows(place, 80), g * 256 : g * 256 + 256] = dot(
                s.pick5[g, 0:80, 0:256], st
            ).astype(BF)
        pass_on(last, w, (n, B), place, 80)

    spread_low(XA, s.part[OUT].pk, s.part[OUT].st.at[rows(low_slot * 16, 16)], (OUT, A))
    spread_both(XA, s.part[GATE].pk, in_plane(XA, me.x, me.y, me.z) * 2 + me.k, s.part[GATE].st, (GATE, A))
    spread_both(ZA, s.part[UP].pk, me.k * 16 + in_plane(ZA, me.x, me.y, me.z), s.part[UP].st, (UP, A))
    down_row = me.x * 256 + me.zh * 128 + me.y * 32 + me.k * 16
    spread_low(YA, s.part[DOWN].pk, s.part[DOWN].w.at[rows(down_row, 16)], (DOWN, A))

    def to_sibling(ref, name, size, place):
        for b in range(4):
            remote(
                ref.at[rows(b * 2 * size + place, size)],
                ref.at[rows(b * 2 * size + place, size)],
                name,
                sibling,
            )

    for n in (2, 1, 0):
        arrived(s.part[n].w.at[pl.ds(0, 240)], (n, B))
        to_sibling(s.part[n].w, (n, C), 80, me.k * 80)

    kv = s.kv
    cos = s.rope[0]
    sin = s.rope[1]
    arrived(s.part[2].w.at[pl.ds(0, 320)], (2, C))
    own = dot(s.xn[2], s.part[2].w[...])
    kv[0:TOK, 0:HEAD] = rotate(own[:, 0:HEAD], cos, sin).astype(BF)
    kv[0:TOK, HEAD:] = own[:, HEAD:].astype(BF)
    for back in (1, 2):

        @pl.when(me.ctx + back < 8)
        def _():
            remote(
                kv.at[pl.ds(0, TOK)],
                kv.at[pl.ds(back * TOK, TOK)],
                (KV, back),
                (me.ctx + back, me.fsdp),
            )

        @pl.when(me.ctx < back)
        def _():
            kv[back * TOK : back * TOK + TOK, :] = jnp.zeros((TOK, 2 * HEAD), BF)

    for n in (1, 0):
        arrived(s.part[n].w.at[pl.ds(0, 320)], (n, C))
        part = dot(s.xn[n], s.part[n].w[...])
        for i in range(2):
            h = 2 * n + i
            s.qs[h * TOK : h * TOK + TOK, :] = (
                rotate(part[:, i * HEAD : i * HEAD + HEAD], cos, sin) * HEAD**-0.5
            ).astype(BF)

    boundary = starts[0]
    qi = lax.broadcasted_iota(jnp.int32, (TOK, TOK), 0)
    kj = lax.broadcasted_iota(jnp.int32, (TOK, TOK), 1)
    query_place = me.ctx * TOK + qi
    query_doc = (query_place >= boundary).astype(jnp.int32)
    for back in range(3):
        key_place = (me.ctx - back) * TOK + kj
        gap = query_place - key_place
        key_doc = (key_place >= boundary).astype(jnp.int32)
        allowed = (gap >= 0) & (gap < WINDOW) & (key_place >= 0) & (query_doc == key_doc)
        s.bias[:, back * TOK : back * TOK + TOK] = jnp.where(allowed, 0.0, masked_score)

    def unpack5(name, last):
        arrived(s.part[name].st, (name, A))
        place = along(me, last) * 160
        st = s.part[name].st[...]
        for g in range(3):
            width = 384 if g < 2 else 256
            s.part[name].w[rows(place, 160), g * 384 : g * 384 + width] = dot(
                s.pick5[g], st[:, 0:width]
            ).astype(BF)
        pass_on(last, s.part[name].w, (name, B), place, 160)

    arrived(s.part[OUT].st, (OUT, A))
    st = s.part[OUT].st[...]
    place = me.x * 256 + me.k * 128
    s.part[OUT].w[rows(place, 128), 0:384] = dot(s.pick8[0], st).astype(BF)
    s.part[OUT].w[rows(place, 128), 384:640] = dot(s.pick8[1], st[:, 0:256]).astype(BF)
    pass_on(XA, s.part[OUT].w, (OUT, B), place, 128)
    unpack5(GATE, XA)
    unpack5(UP, ZA)
    arrived(s.part[DOWN].w.at[pl.ds(0, 256)], (DOWN, A))
    for piece in range(8):
        pass_on(YA, s.part[DOWN].w, (DOWN, B), piece * 128 + me.y * 32, 32)

    for back in (1, 2):

        @pl.when(me.ctx >= back)
        def _():
            arrived(kv.at[pl.ds(back * TOK, TOK)], (KV, back))

    def head_forward(h, carry):
        hs = pl.ds(pl.multiple_of(h * TOK, TOK), TOK)
        scores = dot_nt(s.qs[hs, :], kv[:, 0:HEAD]) + s.bias[...]
        top = jnp.max(scores, axis=1, keepdims=True)
        e = jnp.exp(scores - top)
        p = (e * (1.0 / jnp.sum(e, axis=1, keepdims=True))).astype(BF)
        s.probs[hs, :] = p
        s.mixed[:, hs] = dot(p, kv[:, HEAD:]).astype(BF)
        return carry

    lax.fori_loop(0, HEADS, head_forward, 0)

    arrived(s.part[OUT].w.at[pl.ds(0, 384)], (OUT, B))
    to_sibling(s.part[OUT].w, (OUT, C), 128, me.k * 128)
    arrived(s.part[OUT].w.at[pl.ds(0, 512)], (OUT, C))
    x1 = x + dot(s.mixed[...], s.part[OUT].w[...])
    s.x1[...] = x1
    r1 = lax.rsqrt(jnp.mean(x1 * x1, axis=1, keepdims=True) + eps_norm)
    s.x2[0:TOK, :] = (x1 * r1).astype(BF)
    remote(s.x2.at[pl.ds(0, TOK)], s.x2.at[pl.ds(TOK, TOK)], X2, sibling)
    arrived(s.dy2.at[pl.ds(TOK, TOK)], DY)
    s.outp[...] = jnp.zeros((2 * TOK, D), F32)
    s.ex[...] = jnp.zeros((2 * TOK, D), F32)
    s.ez[...] = jnp.zeros((2 * TOK, D), F32)
    s.x2z[0:TOK, :] = dot(s.x2[0:TOK, :], s.orders[1]).astype(BF)
    arrived(s.x2.at[pl.ds(TOK, TOK)], X2)
    s.x2z[TOK:, :] = dot(s.x2[TOK:, :], s.orders[1]).astype(BF)
    arrived(s.part[GATE].w.at[pl.ds(0, 480)], (GATE, B))
    arrived(s.part[UP].w.at[pl.ds(0, 480)], (UP, B))
    arrived(s.part[DOWN].w.at[pl.ds(0, 768)], (DOWN, B))

    root = 0.7978845608028654

    def hidden_step(t, carry):
        ts = pl.ds(pl.multiple_of(t * 256, 256), 256)
        gate = dot(s.x2[...], s.part[GATE].w[:, ts])
        up = dot(s.x2z[...], s.part[UP].w[:, ts])
        d_hidden = dot_nt(s.dy2[...], s.part[DOWN].w[ts, :])
        square = gate * gate
        th = jnp.tanh(root * gate * (1.0 + 0.044715 * square))
        half = 0.5 * (1.0 + th)
        act = gate * half
        slope = half + 0.5 * gate * (1.0 - th * th) * (root * (1.0 + 0.134145 * square))
        hidden = (act * up).astype(BF)
        d_gate = (d_hidden * up * slope).astype(BF)
        d_up = (d_hidden * act).astype(BF)
        s.part[DOWN].g[ts, :] = dot_tn(hidden, s.dy2[...]).astype(BF)
        s.outp[...] += dot(hidden, s.part[DOWN].w[ts, :])
        s.part[GATE].g[:, ts] = dot_tn(s.x2[...], d_gate).astype(BF)
        s.ex[...] += dot_nt(d_gate, s.part[GATE].w[:, ts])
        s.part[UP].g[:, ts] = dot_tn(s.x2z[...], d_up).astype(BF)
        s.ez[...] += dot_nt(d_up, s.part[UP].w[:, ts])
        return carry

    lax.fori_loop(0, 4, hidden_step, 0)

    def gather_line(last, src, size, name):
        for j in range(1, 4):
            b = around(along(me, last), j)
            remote(
                src.at[rows(b * size, size)],
                s.part[name].r1.at[pl.ds((j - 1) * size, size)],
                (name, E),
                device(*line_chip(me, last, j), me.k),
            )

    other = s.ex[TOK:, :] + dot_nt(s.ez[TOK:, :].astype(BF), s.orders[1])
    s.esend[...] = other.astype(BF)
    remote(s.esend, s.erecv, EE, sibling)
    s.osend[...] = s.outp[TOK:, :].astype(BF)
    remote(s.osend, s.orecv, OO, sibling)

    for j in range(1, 4):
        b = around(me.y, j)
        for piece in range(8):
            remote(
                s.part[DOWN].g.at[rows(piece * 128 + b * 32, 32)],
                s.part[DOWN].r1.at[pl.ds((j - 1) * 256 + piece * 32, 32)],
                (DOWN, E),
                device(*line_chip(me, YA, j), me.k),
            )
    gather_line(XA, s.part[GATE].g, 160, GATE)
    gather_line(ZA, s.part[UP].g, 160, UP)

    e1 = s.ex[0:TOK, :] + dot_nt(s.ez[0:TOK, :].astype(BF), s.orders[1])
    arrived(s.erecv, EE)
    e1 = e1 + s.erecv[...].astype(F32)
    x1 = s.x1[...]
    r1 = lax.rsqrt(jnp.mean(x1 * x1, axis=1, keepdims=True) + eps_norm)
    dx1 = (
        s.cin[...].astype(F32)
        + r1 * e1
        - x1 * (r1 * r1 * r1 * jnp.mean(x1 * e1, axis=1, keepdims=True))
    )
    s.dx1[...] = dx1
    da = dx1.astype(BF)

    def head_out(h, carry):
        hs = pl.ds(pl.multiple_of(h * TOK, TOK), TOK)
        dmix = dot_nt(da, s.part[OUT].w[hs, :]).astype(BF)
        s.dmix[hs, :] = dmix
        d_probs = dot_nt(dmix, kv[:, HEAD:])
        p = s.probs[hs, :].astype(F32)
        center = jnp.sum(p * d_probs, axis=1, keepdims=True)
        s.ds[hs, :] = (p * (d_probs - center)).astype(BF)
        return carry

    lax.fori_loop(0, HEADS, head_out, 0)

    for back in (2, 1):
        bs = slice(back * TOK, back * TOK + TOK)
        to = slice((back - 1) * TOK, back * TOK)
        s.kvsend[to, 0:HEAD] = dot_tn(s.ds[:, bs], s.qs[...]).astype(BF)
        s.kvsend[to, HEAD:] = dot_tn(s.probs[:, bs], s.dmix[...]).astype(BF)

        @pl.when(me.ctx >= back)
        def _():
            remote(
                s.kvsend.at[pl.ds((back - 1) * TOK, TOK)],
                s.kvrecv.at[pl.ds((back - 1) * TOK, TOK)],
                (DKV, back),
                (me.ctx - back, me.fsdp),
            )

        @pl.when(me.ctx + back >= 8)
        def _():
            s.kvrecv[to, :] = jnp.zeros((TOK, 2 * HEAD), BF)

    def head_out_grad(h, carry):
        hs = pl.ds(pl.multiple_of(h * TOK, TOK), TOK)
        s.part[OUT].g[hs, :] = dot_tn(s.mixed[:, hs], da).astype(BF)
        dq = dot(s.ds[hs, :], kv[:, 0:HEAD]) * HEAD**-0.5
        s.dq[:, hs] = rotate(dq, cos, -sin).astype(BF)
        return carry

    lax.fori_loop(0, HEADS, head_out_grad, 0)

    def swap_halves(src, size, name):
        for b in range(4):
            remote(
                src.at[rows(b * 2 * size + (1 - me.k) * size, size)],
                s.part[name].r0.at[pl.ds(b * size, size)],
                (name, DD),
                sibling,
            )

    swap_halves(s.part[OUT].g, 128, OUT)
    for n in (0, 1):
        s.part[n].g[...] = dot_tn(s.xn[n], s.dq[:, n * 512 : n * 512 + 512]).astype(BF)
        swap_halves(s.part[n].g, 80, n)
    s.dkv[:, 0:HEAD] = dot_tn(s.ds[:, 0:TOK], s.qs[...])
    s.dkv[:, HEAD:] = dot_tn(s.probs[:, 0:TOK], s.dmix[...])

    def merge_halves(name, size, last):
        arrived(s.part[name].r0, (name, DD))
        for b in range(4):
            s.part[name].gs[b * size : b * size + size, :] = (
                s.part[name].g[rows(b * 2 * size + me.k * size, size), :].astype(F32)
                + s.part[name].r0[b * size : b * size + size, :].astype(F32)
            ).astype(BF)
        gather_line(last, s.part[name].gs, size, name)

    merge_halves(OUT, 128, XA)
    merge_halves(0, 80, XA)
    merge_halves(1, 80, YA)

    for back in (2, 1):

        @pl.when(me.ctx + back < 8)
        def _():
            arrived(s.kvrecv.at[pl.ds((back - 1) * TOK, TOK)], (DKV, back))

    dkv = (
        s.dkv[...]
        + s.kvrecv[0:TOK, :].astype(F32)
        + s.kvrecv[TOK : 2 * TOK, :].astype(F32)
    )
    s.dq[:, 1024:1280] = rotate(dkv[:, 0:HEAD], cos, -sin).astype(BF)
    s.dq[:, 1280:1536] = dkv[:, HEAD:].astype(BF)
    s.part[2].g[...] = dot_tn(s.xn[2], s.dq[:, 1024:1536]).astype(BF)
    swap_halves(s.part[2].g, 80, 2)

    def line_sum(name, own, size):
        arrived(s.part[name].r1, (name, E))
        total = own.astype(F32)
        for j in range(3):
            total = total + s.part[name].r1[j * size : j * size + size, :].astype(F32)
        return total.astype(BF)

    def collect_both(name, last):
        total = line_sum(name, s.part[name].g[rows(along(me, last) * 160, 160), :], 160)
        gp = s.part[name].gp
        gp[:, 0:256] = (
            dot_tn(s.pick5[0], total[:, 0:256])
            + dot_tn(s.pick5[1], total[:, 384:640])
            + dot_tn(s.pick5[2], total[:, 768:1024])
        ).astype(BF)
        gp[:, 256:384] = (
            dot_tn(s.pick5[0], total[:, 256:384]) + dot_tn(s.pick5[1], total[:, 640:768])
        ).astype(BF)
        home = s.part[name].r2.at[rows((me.k * 16 + in_plane(last, me.x, me.y, me.z)) * 16, 16)]

        def slot_of(chip, core):
            place = in_plane(last, *chip)
            return place * 2 + core if last == XA else core * 16 + place

        def send(j, carry):
            chip = plane_chip(me, last, j)
            for core in range(2):
                remote(
                    gp.at[rows(slot_of(chip, core) * 16, 16)],
                    home,
                    (name, FR),
                    device(*chip, core),
                )
            return carry

        lax.fori_loop(1, 16, send, 0)
        here = (me.x, me.y, me.z)
        own_copy(gp.at[rows(slot_of(here, me.k) * 16, 16)], home, (name, FR))
        remote(gp.at[rows(slot_of(here, 1 - me.k) * 16, 16)], home, (name, FR), sibling)

    def collect_low(last, src, dst, name, slot_chip):
        home = dst.at[rows(in_plane(last, me.x, me.y, me.z) * 16, 16)]

        def send(i, carry):
            q = lax.rem(i + me.fsdp, 16)
            x, y, z, core = slot_chip(q)
            is_me = (x == me.x) & (y == me.y) & (z == me.z) & (core == me.k)

            @pl.when(is_me)
            def _():
                own_copy(src.at[rows(q * 16, 16)], home, name)

            @pl.when(jnp.logical_not(is_me))
            def _():
                remote(src.at[rows(q * 16, 16)], home, name, device(x, y, z, core))

            return carry

        lax.fori_loop(0, 16, send, 0)

    def collect_same(last, src, dst, name):
        home = dst.at[rows(in_plane(last, me.x, me.y, me.z) * 16, 16)]
        own_copy(src.at[rows(in_plane(last, me.x, me.y, me.z) * 16, 16)], home, name)

        def send(j, carry):
            chip = plane_chip(me, last, j)
            remote(src.at[rows(in_plane(last, *chip) * 16, 16)], home, name, device(*chip, me.k))
            return carry

        lax.fori_loop(1, 16, send, 0)

    def low_chip_x(q):
        return me.x, lax.rem(lax.div(q, 2), 4), 2 * lax.div(q, 8) + me.k, lax.rem(q, 2)

    def low_chip_y(q):
        return lax.div(q, 4), me.y, 2 * lax.rem(lax.div(q, 2), 2) + me.k, lax.rem(q, 2)

    arrived(s.part[DOWN].r1, (DOWN, E))
    for piece in range(8):
        total = s.part[DOWN].g[rows(piece * 128 + me.y * 32, 32), :].astype(F32)
        for j in range(3):
            total = total + s.part[DOWN].r1[j * 256 + piece * 32 : j * 256 + piece * 32 + 32, :].astype(F32)
        s.part[DOWN].gp[piece * 32 : piece * 32 + 32, :] = total.astype(BF)
    collect_low(YA, s.part[DOWN].gp, s.part[DOWN].r2, (DOWN, FR), low_chip_y)
    collect_both(GATE, XA)
    collect_both(UP, ZA)

    total = line_sum(OUT, s.part[OUT].gs[rows(me.x * 128, 128), :], 128)
    s.part[OUT].gp[:, 0:256] = (
        dot_tn(s.pick8[0], total[:, 0:256]) + dot_tn(s.pick8[1], total[:, 384:640])
    ).astype(BF)
    s.part[OUT].gp[:, 256:384] = dot_tn(s.pick8[0], total[:, 256:384]).astype(BF)
    collect_low(XA, s.part[OUT].gp, s.part[OUT].r2, (OUT, FR), low_chip_x)

    merge_halves(2, 80, ZA)

    def collect_qkv(n):
        last = LAST[n]
        name = n
        total = line_sum(name, s.part[name].gs[rows(along(me, last) * 80, 80), :], 80)
        s.part[name].gp[...] = (
            dot_tn(s.pick5[0, 0:80, 0:256], total[:, 0:256])
            + dot_tn(s.pick5[1, 0:80, 0:256], total[:, 256:512])
        ).astype(BF)
        if n == 0:
            collect_low(XA, s.part[0].gp, s.part[0].r2, (0, FR), low_chip_x)
        else:
            collect_same(last, s.part[name].gp, s.part[name].r2, (name, FR))

    collect_qkv(0)
    collect_qkv(1)

    e0 = dot_nt(s.dq[:, 0:512], s.part[0].w[...])
    for n in (1, 2):
        part = dot_nt(s.dq[:, n * 512 : n * 512 + 512], s.part[n].w[...])
        e0 = e0 + dot_nt(part.astype(BF), s.orders[n - 1])
    x = s.xin[...].astype(F32)
    r0 = lax.rsqrt(jnp.mean(x * x, axis=1, keepdims=True) + eps_norm)
    ig[...] = s.dx1[...] + r0 * e0 - x * (r0 * r0 * r0 * jnp.mean(x * e0, axis=1, keepdims=True))
    arrived(s.orecv, OO)
    lo[...] = s.x1[...] + s.outp[0:TOK, :] + s.orecv[...].astype(F32)

    collect_qkv(2)

    def plane_sum(name, out, first):
        total = s.part[name].r2[first * 16 : first * 16 + 16, :].astype(F32)
        for p in range(1, 16):
            total = total + s.part[name].r2[(first + p) * 16 : (first + p) * 16 + 16, :].astype(F32)
        out[first : first + 16, :] = total

    arrived(s.part[DOWN].r2, (DOWN, FR))
    plane_sum(DOWN, sd, 0)
    for name, out in ((GATE, sg), (UP, su)):
        arrived(s.part[name].r2, (name, FR))
        plane_sum(name, out, 0)
        plane_sum(name, out, 16)
    arrived(s.part[OUT].r2, (OUT, FR))
    plane_sum(OUT, so, 0)
    for n, out in ((0, sq0), (1, sq1), (2, sq2)):
        arrived(s.part[n].r2, (n, FR))
        plane_sum(n, out, 0)

    def left_low(ref, name, size):
        @pl.when(me.zl == me.k)
        def _():
            left(ref.at[pl.ds(0, 15 * size)], name)

        @pl.when(me.zl != me.k)
        def _():
            left(ref.at[pl.ds(0, 16 * size)], name)

    left(s.part[2].st.at[pl.ds(0, 240)], (2, A))
    left(s.part[1].st.at[pl.ds(0, 240)], (1, A))
    left_low(s.part[0].st, (0, A), 16)
    left_low(s.part[OUT].st, (OUT, A), 16)
    left_low(s.part[DOWN].w, (DOWN, A), 16)
    for name in (GATE, UP):
        left(s.part[name].st.at[pl.ds(0, 31 * 16)], (name, A))
        left(s.part[name].w.at[pl.ds(0, 480)], (name, B))
        left(s.part[name].r1, (name, E))
        left(s.part[name].r2.at[pl.ds(0, 31 * 16)], (name, FR))
    for n in range(3):
        left(s.part[n].w.at[pl.ds(0, 240)], (n, B))
        left(s.part[n].w.at[pl.ds(0, 320)], (n, C))
        left(s.part[n].r0, (n, DD))
        left(s.part[n].r1, (n, E))
    left_low(s.part[0].r2, (0, FR), 16)
    left(s.part[1].r2.at[pl.ds(0, 240)], (1, FR))
    left(s.part[2].r2.at[pl.ds(0, 240)], (2, FR))
    left(s.part[OUT].w.at[pl.ds(0, 384)], (OUT, B))
    left(s.part[OUT].w.at[pl.ds(0, 512)], (OUT, C))
    left(s.part[OUT].r0, (OUT, DD))
    left(s.part[OUT].r1, (OUT, E))
    left_low(s.part[OUT].r2, (OUT, FR), 16)
    left(s.part[DOWN].w.at[pl.ds(0, 768)], (DOWN, B))
    left(s.part[DOWN].r1, (DOWN, E))
    left_low(s.part[DOWN].r2, (DOWN, FR), 16)
    left(s.cin, DY)
    left(s.esend, EE)
    left(s.osend, OO)
    left(s.osend, X2)
    for back in (1, 2):

        @pl.when(me.ctx + back < 8)
        def _():
            left(kv.at[pl.ds(0, TOK)], (KV, back))

        @pl.when(me.ctx >= back)
        def _():
            left(s.kvsend.at[pl.ds(0, TOK)], (DKV, back))

    assert len(sems) <= SEMS


def whole_step(tokens, cotangent, starts, wq, wo, wgu, wd, gains):
    orders, pick5, pick8, rope = constants()
    scratch = scratch_list()
    vmem = pl.BlockSpec(memory_space=pltpu.VMEM)
    anywhere = pl.BlockSpec(memory_space=pl.ANY)
    smem = pl.BlockSpec(memory_space=pltpu.SMEM)
    shapes = [(TOK, D), (TOK, D)] + [(16, 256)] * 3 + [(16, 384), (32, 384), (32, 384), (16, 640)]
    return pl.pallas_call(
        functools.partial(step_kernel, scratch),
        name="whole_step",
        out_shape=[jax.ShapeDtypeStruct(shape, F32) for shape in shapes],
        in_specs=[anywhere, anywhere, smem] + [vmem] * 5 + [anywhere] * 4,
        out_specs=[vmem] * len(shapes),
        scratch_shapes=leaves(scratch)
        + [
            pltpu.SemaphoreType.DMA((8,)),
            pltpu.SemaphoreType.DMA((SEMS,)),
            pltpu.SemaphoreType.DMA((SEMS,)),
        ],
        compiler_params=pltpu.CompilerParams(
            collective_id=0, has_side_effects=True, vmem_limit_bytes=62 * 2**20
        ),
        cost_estimate=pl.CostEstimate(
            flops=12_000_000_000, bytes_accessed=8_000_000, transcendentals=2_000_000
        ),
    )(tokens, cotangent, starts, wq, wo, wgu, wd, gains, orders, pick5, pick8, rope)


def adamw(master, first, second, gradient, rate, decay):
    first_next = beta_one * first + (1.0 - beta_one) * gradient
    second_next = beta_two * second + (1.0 - beta_two) * gradient * gradient
    first_fixed = first_next * (1.0 / (1.0 - beta_one**STEP))
    second_fixed = second_next * (1.0 / (1.0 - beta_two**STEP))
    update = first_fixed / (jnp.sqrt(second_fixed) + eps_adam) + decay * master
    return master - rate * update, first_next, second_next


def update_kernel(*refs):
    inner = refs[41:65]
    sem = refs[65]
    copies = [
        pltpu.make_async_copy(src, dst, sem.at[n])
        for n, (src, dst) in enumerate(zip(refs[:24], inner))
    ]
    for one in copies:
        one.start()
    (sq0, sq1, sq2, so, sg, su, sd) = inner[2:9]
    (wq, qf, qs, wo, of, os_, wgu, gf, gs, wd, df, ds_, gains, nf, ns) = inner[9:]
    (oq, oqf, oqs, oo, oof, oos, og, ogf, ogs, od, odf, ods, on, onf, ons) = refs[26:41]
    for one in copies:
        one.wait()
    through = [
        pltpu.make_async_copy(inner[n], refs[24 + n].at[0], sem.at[24 + n]) for n in range(2)
    ]
    for one in through:
        one.start()

    rate = 1.5 * D**-0.5
    gain0 = column(gains[0:1, :])
    gain1 = column(gains[1:2, :])
    total0 = jnp.zeros((5, 1), F32)
    for n, share in enumerate((sq0, sq1, sq2)):
        for g in range(2):
            at = slice(n * 512 + g * 256, n * 512 + g * 256 + 256)
            raw = share[5 * g : 5 * g + 5, :]
            w = wq[:, at]
            total0 = total0 + jnp.sum(w.astype(BF).astype(F32) * raw, axis=1, keepdims=True)
            oq[:, at], oqf[:, at], oqs[:, at] = adamw(
                w, qf[:, at], qs[:, at], raw * gain0, rate, weight_decay
            )
    total1 = jnp.zeros((5, 1), F32)
    for n, share in enumerate((sg, su)):
        for c in range(2):
            for t in range(8):
                g, i = t // 3, t % 3
                base = n * FF + (t // 2) * 512 + c * 256 + (t % 2) * 128
                at = slice(base, base + 128)
                raw = share[c * 16 + 5 * g : c * 16 + 5 * g + 5, i * 128 : i * 128 + 128]
                w = wgu[:, at]
                total1 = total1 + jnp.sum(w.astype(BF).astype(F32) * raw, axis=1, keepdims=True)
                og[:, at], ogf[:, at], ogs[:, at] = adamw(
                    w, gf[:, at], gs[:, at], raw * gain1, rate, weight_decay
                )
    rate = 1.5 * OUT_FAN**-0.5
    for r, at in ((0, slice(0, 384)), (8, slice(384, 640))):
        raw = so[r : r + 8, 0 : at.stop - at.start]
        oo[:, at], oof[:, at], oos[:, at] = adamw(
            wo[:, at], of[:, at], os_[:, at], raw, rate, weight_decay
        )
    od[...], odf[...], ods[...] = adamw(
        wd[...], df[...], ds_[...], sd[...], 1.5 * FF**-0.5, weight_decay
    )
    i = lax.broadcasted_iota(jnp.int32, (5, 5), 0)
    j = lax.broadcasted_iota(jnp.int32, (5, 5), 1)
    for row, total in ((0, total0), (1, total1)):
        flat = jnp.sum(jnp.where(i == j, jnp.broadcast_to(total, (5, 5)), 0.0), axis=0, keepdims=True)
        at = slice(row, row + 1)
        on[at, :], onf[at, :], ons[at, :] = adamw(gains[at, :], nf[at, :], ns[at, :], flat, 0.5, 0.0)
    for one in through:
        one.wait()


def update(*arrays):
    vmem = pl.BlockSpec(memory_space=pltpu.VMEM)
    anywhere = pl.BlockSpec(memory_space=pl.ANY)
    outs = [jax.ShapeDtypeStruct((1, TOK, D), F32)] * 2 + [
        jax.ShapeDtypeStruct(a.shape, F32) for a in arrays[9:]
    ]
    return pl.pallas_call(
        update_kernel,
        name="update",
        out_shape=outs,
        in_specs=[anywhere] * len(arrays),
        out_specs=[anywhere] * 2 + [vmem] * (len(outs) - 2),
        scratch_shapes=[pltpu.VMEM(a.shape, F32) for a in arrays]
        + [pltpu.SemaphoreType.DMA((len(arrays) + 2,))],
        compiler_params=pltpu.CompilerParams(vmem_limit_bytes=60 * 2**20),
    )(*arrays)


def body(
    tokens,
    cotangent,
    starts,
    qkv_weight,
    qkv_first,
    qkv_second,
    out_weight,
    out_first,
    out_second,
    gate_up_weight,
    gate_up_first,
    gate_up_second,
    down_weight,
    down_first,
    down_second,
    norm_gains,
    gains_first,
    gains_second,
):
    results = whole_step(
        tokens, cotangent, starts, qkv_weight, out_weight, gate_up_weight, down_weight, norm_gains
    )
    return tuple(
        update(
            *results,
            qkv_weight,
            qkv_first,
            qkv_second,
            out_weight,
            out_first,
            out_second,
            gate_up_weight,
            gate_up_first,
            gate_up_second,
            down_weight,
            down_first,
            down_second,
            norm_gains,
            gains_first,
            gains_second,
        )
    )


def solution(mesh):
    act = P("fsdp", "ctx", None)
    row = P(("ctx", "fsdp"), None)
    gain = P(None, ("ctx", "fsdp"))
    return jax.shard_map(
        body,
        mesh=mesh,
        in_specs=(act, act, P("fsdp")) + (row,) * 12 + (gain,) * 3,
        out_specs=(act, act) + (row,) * 12 + (gain,) * 3,
        check_vma=False,
    )
```

```python
import functools

import jax
import jax.numpy as jnp
import numpy as np
from jax import lax
from jax.experimental import pallas as pl
from jax.experimental.pallas import tpu as pltpu
from jax.sharding import PartitionSpec as P

D = 640
HEADS = 4
HEAD = 256
FF = 2048
WINDOW = 512
STEP = 10
QW = 1024
OUT_FAN = 8
TOK = 256
LENGTH = 2048

eps_norm = 1e-06
beta_one = 0.9
beta_two = 0.95
eps_adam = 1e-08
weight_decay = 0.1
masked_score = -1e30

MESH = pl.DeviceIdType.MESH
BF = jnp.bfloat16
F32 = jnp.float32


class Place:
    def __init__(self):
        self.ctx = lax.axis_index("ctx")
        self.fsdp = lax.axis_index("fsdp")
        self.x = lax.div(self.ctx, 2)
        self.zl = lax.rem(self.ctx, 2)
        self.zh = lax.div(self.fsdp, 8)
        self.y = lax.div(lax.rem(self.fsdp, 8), 2)
        self.k = lax.rem(self.fsdp, 2)
        self.z = 2 * self.zh + self.zl


def device(x, y, z, k):
    return (2 * x + lax.rem(z, 2), 8 * lax.div(z, 2) + 2 * y + k)


def around(a, b):
    return lax.rem(a + b, 4)


def plane_chip(me, last, j):
    a, b = lax.rem(j, 4), lax.div(j, 4)
    if last == XA:
        return me.x, around(me.y, a), around(me.z, b)
    if last == YA:
        return around(me.x, a), me.y, around(me.z, b)
    return around(me.x, a), around(me.y, b), me.z


def line_chip(me, last, j):
    if last == XA:
        return around(me.x, j), me.y, me.z
    if last == YA:
        return me.x, around(me.y, j), me.z
    return me.x, me.y, around(me.z, j)


def along(me, last):
    return (me.x, me.y, me.z)[last]


def in_plane(last, x, y, z):
    if last == XA:
        return lax.rem(z, 2) * 8 + lax.div(z, 2) * 4 + y
    if last == YA:
        return 4 * x + z
    return 4 * x + y


def rows(start, size):
    return pl.ds(pl.multiple_of(start, 16), size)


def feature_order(last):
    order = np.zeros(D, np.int64)
    for x in range(4):
        for y in range(4):
            for z in range(4):
                for k in range(2):
                    dev = x * 32 + (z % 2) * 16 + (z // 2) * 8 + y * 2 + k
                    b, p = (y, 4 * x + z) if last == YA else (z, 4 * y + x)
                    for r in range(5):
                        order[b * 160 + k * 80 + p * 5 + r] = 5 * dev + r
    return order


def constants():
    orders = np.zeros((2, D, D), np.float32)
    for n, last in enumerate((YA, ZA)):
        orders[n, feature_order(last), np.arange(D)] = 1.0
    pick5 = np.zeros((3, 160, 512), np.float32)
    for g in range(3):
        for s in range(32):
            for r in range(5):
                pick5[g, s * 5 + r, s * 16 + g * 5 + r] = 1.0
    pick8 = np.zeros((2, 128, 256), np.float32)
    for g in range(2):
        for s in range(16):
            for r in range(8):
                pick8[g, s * 8 + r, s * 16 + g * 8 + r] = 1.0
    half = HEAD // 2
    frequency = np.float32(10000.0) ** (
        -(np.float32(2.0) * np.arange(half, dtype=np.float32)) / np.float32(HEAD)
    )
    angles = np.arange(LENGTH, dtype=np.float32)[:, None] * frequency.astype(np.float32)[None, :]
    rope = np.stack([np.cos(angles.astype(np.float64)), np.sin(angles.astype(np.float64))])
    return (
        jnp.asarray(orders, BF),
        jnp.asarray(pick5, BF),
        jnp.asarray(pick8, BF),
        jnp.asarray(rope.astype(np.float32)),
    )


def dot(a, b):
    return lax.dot_general(a, b, (((1,), (0,)), ((), ())), preferred_element_type=F32)


def dot_nt(a, b):
    return lax.dot_general(a, b, (((1,), (1,)), ((), ())), preferred_element_type=F32)


def dot_tn(a, b):
    return lax.dot_general(a, b, (((0,), (0,)), ((), ())), preferred_element_type=F32)


def rotate(u, cos, sin):
    a, b = u[:, :128], u[:, 128:]
    return jnp.concatenate([a * cos - b * sin, b * cos + a * sin], axis=1)


def column(row):
    n = row.shape[1]
    i = lax.broadcasted_iota(jnp.int32, (n, n), 0)
    j = lax.broadcasted_iota(jnp.int32, (n, n), 1)
    wide = jnp.broadcast_to(row.astype(BF).astype(F32), (n, n))
    return jnp.sum(jnp.where(i == j, wide, 0.0), axis=1, keepdims=True)


class Bag(dict):
    __getattr__ = dict.__getitem__


def scratch_list():
    def v(*shape, kind=BF):
        return pltpu.VMEM(shape, kind)

    qkv = [
        Bag(
            pk=v(16, 256),
            st=v(256, 256),
            w=v(640, 512),
            g=v(640, 512),
            r0=v(320, 512),
            gs=v(320, 512),
            r1=v(240, 512),
            gp=v(256, 256),
            ra=v(192, 256),
            ga=v(64, 256),
            rb=v(64, 256),
        )
        for n in range(3)
    ]
    out = Bag(
        pk=v(16, 384),
        st=v(256, 384),
        w=v(1024, 640),
        g=v(1024, 640),
        r0=v(512, 640),
        gs=v(512, 640),
        r1=v(384, 640),
        gp=v(256, 384),
        ra=v(192, 384),
        ga=v(64, 384),
        rb=v(64, 384),
    )
    gate_up = [
        Bag(
            pk=v(32, 384),
            st=v(512, 384),
            w=v(640, 1024),
            g=v(640, 1024),
            rf=v(160, 1024),
            sf=v(160, 1024),
            r1=v(320, 1024),
            gp=v(512, 384),
            ra=v(384, 384),
            ga=v(128, 384),
            rb=v(128, 384),
        )
        for n in range(2)
    ]
    down = Bag(
        pk=v(16, 640),
        w=v(1024, 640),
        g=v(1024, 640),
        rf=v(256, 640),
        sf=v(256, 640),
        r1=v(512, 640),
        gp=v(256, 640),
        ra=v(192, 640),
        ga=v(64, 640),
        rb=v(64, 640),
    )
    return Bag(
        part=qkv + [out] + gate_up + [down],
        tokens=v(3 * TOK, D),
        cin=v(TOK, D),
        orders=v(2, D, D),
        pick5=v(3, 160, 512),
        pick8=v(2, 128, 256),
        rope=v(3, 2, TOK, 128, kind=F32),
        pad=v(16, 384, kind=F32),
        xn=v(2, TOK, D),
        xnz=v(3 * TOK, D),
        qs=v(HEADS * TOK, HEAD),
        kv=v(3 * TOK, 2 * HEAD),
        bias=v(TOK, 3 * TOK, kind=F32),
        probs=v(HEADS * TOK, 3 * TOK),
        ds=v(HEADS * TOK, 3 * TOK),
        mixed=v(TOK, QW),
        dmix=v(HEADS * TOK, HEAD),
        x1=v(TOK, D, kind=F32),
        x2=v(2 * TOK, D),
        x2z=v(2 * TOK, D),
        dy2=v(2 * TOK, D),
        outp=v(2 * TOK, D, kind=F32),
        ex=v(2 * TOK, D, kind=F32),
        ez=v(2 * TOK, D, kind=F32),
        osend=v(TOK, D),
        orecv=v(TOK, D),
        esend=v(TOK, D),
        erecv=v(TOK, D),
        dx1=v(TOK, D, kind=F32),
        dq=v(TOK, QW),
        dkv=v(3 * TOK, 2 * HEAD),
        dkvr=v(3 * TOK, 2 * HEAD),
        dkvs=v(TOK, 2 * HEAD),
    )


def leaves(tree):
    if isinstance(tree, dict):
        return [leaf for branch in tree.values() for leaf in leaves(branch)]
    if isinstance(tree, list):
        return [leaf for branch in tree for leaf in leaves(branch)]
    return [tree]


def refill(tree, values):
    if isinstance(tree, dict):
        return Bag({key: refill(branch, values) for key, branch in tree.items()})
    if isinstance(tree, list):
        return [refill(branch, values) for branch in tree]
    return next(values)


OUT, GATE, UP, DOWN = 3, 4, 5, 6
XA, YA, ZA = range(3)
LAST = (XA, YA, ZA, ZA, XA, ZA, YA)
A1, A2, B1, B2, C, D1, E1, E2, F1, F2 = range(10)
DY, X2, EE, OO, TK, DKV = range(7, 13)
SEMS = 128


def wait_for(ref, sem):
    pltpu.make_async_copy(ref, ref, sem).wait()


def step_kernel(shape, *refs):
    (tok, cot, starts, wq, wo, wgu, wd, gains, orders_h, pick5_h, pick8_h, rope_h) = refs[:12]
    (lo, ig, sq0, sq1, sq2, so, sg, su, sd) = refs[12:21]
    s = refill(shape, iter(refs[21:-3]))
    local, sent, came = refs[-3:]
    me = Place()
    sems = {}
    taken = [0]

    def sem_of(name, size=1):
        if name not in sems:
            sems[name] = taken[0]
            taken[0] += size
        return sems[name]

    def remote(src, dst, name, target, tile=None):
        n = sem_of(name, 1 if tile is None else 4)
        pltpu.make_async_remote_copy(
            src_ref=src,
            dst_ref=dst,
            send_sem=sent.at[n],
            recv_sem=came.at[n if tile is None else n + tile],
            device_id=target,
            device_id_type=MESH,
        ).start()

    def own_copy(src, dst, name):
        pltpu.make_async_copy(src, dst, came.at[sem_of(name)]).start()

    def arrived(ref, name, tile=0):
        wait_for(ref, came.at[sem_of(name) + tile])

    def left(ref, name):
        wait_for(ref, sent.at[sem_of(name)])

    sibling = device(me.x, me.y, me.z, 1 - me.k)

    fetch = [
        (tok.at[0], s.tokens.at[pl.ds(0, TOK)]),
        (orders_h, s.orders),
        (pick5_h, s.pick5),
        (pick8_h, s.pick8),
        (cot.at[0], s.cin),
        (cot.at[0], s.dy2.at[pl.ds(0, TOK)]),
    ]
    for back in range(3):
        block = jnp.maximum(me.ctx - back, 0) * TOK
        fetch.append((rope_h.at[:, pl.ds(pl.multiple_of(block, TOK), TOK), :], s.rope.at[back]))
    fetches = [pltpu.make_async_copy(a, b, local.at[n]) for n, (a, b) in enumerate(fetch)]
    for one in fetches:
        one.start()

    barrier = pltpu.get_barrier_semaphore()
    for j in range(1, 4):
        for axis in range(3):
            for core in range(2):
                pl.semaphore_signal(
                    barrier,
                    inc=1,
                    device_id=device(*line_chip(me, axis, j), core),
                    device_id_type=MESH,
                )
    pl.semaphore_signal(barrier, inc=1, device_id=sibling, device_id_type=MESH)

    pad = s.pad
    pad[...] = jnp.zeros((16, 384), F32)
    wqb = wq[...].astype(BF).astype(F32) * column(gains[0:1, :])
    for n in range(3):
        for g in range(2):
            pad[5 * g : 5 * g + 5, 0:256] = wqb[:, n * 512 + g * 256 : n * 512 + g * 256 + 256]
        s.part[n].pk[...] = pad[:, 0:256].astype(BF)
    gain = column(gains[1:2, :])
    for n, name in enumerate((GATE, UP)):
        for c in range(2):
            for t in range(8):
                g, i = t // 3, t % 3
                base = n * FF + (t // 2) * 512 + c * 256 + (t % 2) * 128
                pad[5 * g : 5 * g + 5, i * 128 : i * 128 + 128] = (
                    wgu[:, base : base + 128].astype(BF).astype(F32) * gain
                )
            pad[10:15, 256:384] = jnp.zeros((5, 128), F32)
            s.part[name].pk[c * 16 : c * 16 + 16, :] = pad[...].astype(BF)
    pad[0:8, :] = wo[:, 0:384]
    pad[8:16, 0:256] = wo[:, 384:640]
    pad[8:16, 256:384] = jnp.zeros((8, 128), F32)
    s.part[OUT].pk[...] = pad[...].astype(BF)
    s.part[DOWN].pk[...] = wd[...].astype(BF)
    fetches[0].wait()
    pl.semaphore_wait(barrier, 19)

    def to_line(axis, src, dst, name, core):
        for j in (1, 3, 2):
            remote(src, dst, name, device(*line_chip(me, axis, j), core))

    def to_line_core(axis, src, dst, name, core):
        to_line(axis, src, dst, name, core)

        @pl.when(core == me.k)
        def _():
            own_copy(src, dst, name)

        @pl.when(core != me.k)
        def _():
            remote(src, dst, name, sibling)

    def to_line_both(axis, src, dst, name):
        for j in (1, 3, 2):
            for core in range(2):
                remote(
                    src.at[pl.ds(core * 16, 16)], dst, name, device(*line_chip(me, axis, j), core)
                )
        own_copy(src.at[rows(me.k * 16, 16)], dst, name)
        remote(src.at[rows((1 - me.k) * 16, 16)], dst, name, sibling)

    xh, xl = lax.div(me.x, 2), lax.rem(me.x, 2)
    zi = me.zl * 2 + me.zh
    part = s.part
    place = part[2].st.at[rows((4 * me.y + me.x) * 16, 16)]
    own_copy(part[2].pk, place, (2, A1))
    to_line(XA, part[2].pk, place, (2, A1), me.k)
    place = part[1].st.at[rows((4 * me.x + me.z) * 16, 16)]
    own_copy(part[1].pk, place, (1, A1))
    to_line(ZA, part[1].pk, place, (1, A1), me.k)
    low_slot = (me.zh * 4 + me.y) * 2 + me.k
    to_line_core(ZA, part[0].pk, part[0].st.at[rows(low_slot * 16, 16)], (0, A1), me.zl)

    def block(ref, back):
        return ref.at[pl.ds(back * TOK, TOK)]

    @pl.when(me.ctx < 6)
    def _():
        remote(block(s.tokens, 0), block(s.tokens, 2), (TK, 2), (me.ctx + 2, me.fsdp))

    @pl.when(me.zl == 0)
    def _():
        remote(block(s.tokens, 0), block(s.tokens, 1), (TK, 1), (me.ctx + 1, me.fsdp))

    def first_norm(rows_in):
        field = rows_in.astype(F32)
        r = lax.rsqrt(jnp.mean(field * field, axis=1, keepdims=True) + eps_norm)
        return (field * r).astype(BF)

    xn = first_norm(s.tokens[0:TOK, :])
    s.xn[0] = xn
    for n in range(1, len(fetches)):
        fetches[n].wait()
    s.xn[1] = dot(xn, s.orders[0]).astype(BF)
    s.xnz[0:TOK, :] = dot(xn, s.orders[1]).astype(BF)

    def pieces_on(axis, ref, starts_, size, name):
        for j in (1, 3, 2):
            for start in starts_:
                at = ref.at[rows(start, size)]
                remote(at, at, name, device(*line_chip(me, axis, j), me.k))

    arrived(part[2].st.at[pl.ds(0, 64)], (2, A1))
    pieces_on(YA, part[2].st, [me.y * 64], 64, (2, A2))
    arrived(part[1].st.at[pl.ds(0, 64)], (1, A1))
    pieces_on(XA, part[1].st, [me.x * 64], 64, (1, A2))
    arrived(part[0].st.at[pl.ds(0, 64)], (0, A1))
    pieces_on(YA, part[0].st, [(zh * 4 + me.y) * 32 for zh in range(2)], 32, (0, A2))
    remote(s.cin, block(s.dy2, 1), DY, sibling)
    out_slot = (xl * 4 + me.y) * 2 + me.k
    to_line_core(XA, part[OUT].pk, part[OUT].st.at[rows(out_slot * 16, 16)], (OUT, A1), xh)
    gate_slot = (zi * 4 + me.y) * 2 + me.k
    to_line_both(ZA, part[GATE].pk, part[GATE].st.at[rows(gate_slot * 16, 16)], (GATE, A1))
    up_slot = me.k * 16 + me.y * 4 + me.x
    to_line_both(XA, part[UP].pk, part[UP].st.at[rows(up_slot * 16, 16)], (UP, A1))
    down_row = me.x * 256 + me.zh * 128 + me.y * 32 + me.k * 16
    to_line_core(ZA, part[DOWN].pk, part[DOWN].w.at[rows(down_row, 16)], (DOWN, A1), me.zl)

    for n in (2, 1, 0):
        arrived(part[n].st.at[pl.ds(0, 192)], (n, A2))
        start = along(me, LAST[n]) * 160 + me.k * 80
        st = part[n].st[...]
        for g in range(2):
            part[n].w[rows(start, 80), g * 256 : g * 256 + 256] = dot(
                s.pick5[g, 0:80, 0:256], st
            ).astype(BF)
        pieces_on(LAST[n], part[n].w, [start], 80, (n, B1))

    arrived(part[OUT].st.at[pl.ds(0, 64)], (OUT, A1))
    pieces_on(YA, part[OUT].st, [(n * 4 + me.y) * 32 for n in range(2)], 32, (OUT, A2))
    arrived(part[GATE].st.at[pl.ds(0, 128)], (GATE, A1))
    pieces_on(YA, part[GATE].st, [(n * 4 + me.y) * 32 for n in range(4)], 32, (GATE, A2))
    arrived(part[UP].st.at[pl.ds(0, 128)], (UP, A1))
    pieces_on(YA, part[UP].st, [n * 256 + me.y * 64 for n in range(2)], 64, (UP, A2))
    arrived(part[DOWN].w.at[pl.ds(0, 64)], (DOWN, A1))
    pieces_on(
        XA, part[DOWN].w, [me.x * 256 + n * 128 + me.y * 32 for n in range(2)], 32, (DOWN, A2)
    )

    def columns(t):
        return pl.ds(pl.multiple_of(t * 256, 256), 256)

    def tile_of(name, b, t):
        if name == DOWN:
            return [rows(t * 256 + zh * 128 + b * 32, 32) for zh in range(2)]
        return [(rows(b * 160, 160), columns(t))]

    def tile_step(t):
        return 1 + 2 * lax.rem(t, 2)

    def start_tiles(name):
        b = along(me, LAST[name])
        ref = part[name].w
        for t in range(4):
            ahead = 1 + 2 * (t % 2)
            for at in tile_of(name, b, t):
                for stage, j in ((B1, ahead), (B2, 4 - ahead)):
                    target = device(*line_chip(me, LAST[name], j), me.k)
                    remote(ref.at[at], ref.at[at], (name, stage), target, t)

    def pass_tile(name, t):
        j = tile_step(t)
        b = around(along(me, LAST[name]), 4 - j)
        ref = part[name].w
        target = device(*line_chip(me, LAST[name], j), me.k)
        size = tile_bytes(name, 1)
        arrived(size, (name, B1), t)
        for at in tile_of(name, b, t):
            remote(ref.at[at], ref.at[at], (name, B2), target, t)

    def tile_bytes(name, count):
        if name == DOWN:
            return part[name].w.at[pl.ds(0, 64 * count)]
        return part[name].w.at[pl.ds(0, 160 * count), pl.ds(0, 256)]

    def out_rows(z):
        return [rows((2 * me.k + n) * 256 + lax.rem(z, 2) * 128 + lax.div(z, 2) * 64, 64) for n in range(2)]

    def start_out():
        for n in range(2):
            at = part[OUT].w.at[out_rows(me.z)[n]]
            for stage, j in ((B1, 1 + 2 * n), (B2, 3 - 2 * n)):
                remote(at, at, (OUT, stage), device(*line_chip(me, ZA, j), me.k), n)

    def pass_out():
        for n in range(2):
            at = part[OUT].w.at[out_rows(around(me.z, 3 - 2 * n))[n]]
            arrived(part[OUT].w.at[pl.ds(0, 64)], (OUT, B1), n)
            remote(at, at, (OUT, B2), device(*line_chip(me, ZA, 1 + 2 * n), me.k), n)

    def unpack5(name):
        start = along(me, LAST[name]) * 160
        st = part[name].st[...]
        for g in range(3):
            width = 384 if g < 2 else 256
            part[name].w[rows(start, 160), g * 384 : g * 384 + width] = dot(
                s.pick5[g], st[:, 0:width]
            ).astype(BF)

    for back in (1, 2):

        @pl.when(me.ctx < back)
        def _():
            s.tokens[back * TOK : back * TOK + TOK, :] = jnp.zeros((TOK, D), BF)

    @pl.when(me.ctx >= 2)
    def _():
        arrived(block(s.tokens, 2), (TK, 2))

    @pl.when((me.zl == 1) & (me.ctx >= 2))
    def _():
        remote(block(s.tokens, 2), block(s.tokens, 1), (TK, 1), (me.ctx - 1, me.fsdp))

    for n in (2, 1, 0):
        arrived(part[n].w.at[pl.ds(0, 240)], (n, B1))
        for b in range(4):
            at = part[n].w.at[rows(b * 160 + me.k * 80, 80)]
            remote(at, at, (n, C), sibling)

    arrived(part[OUT].st.at[pl.ds(0, 192)], (OUT, A2))
    st = part[OUT].st[...]
    left_cols = dot(s.pick8[0], st).astype(BF)
    right_cols = dot(s.pick8[1], st[:, 0:256]).astype(BF)
    for n in range(2):
        part[OUT].w[out_rows(me.z)[n], 0:384] = left_cols[n * 64 : n * 64 + 64, :]
        part[OUT].w[out_rows(me.z)[n], 384:640] = right_cols[n * 64 : n * 64 + 64, :]
    start_out()
    arrived(part[GATE].st.at[pl.ds(0, 384)], (GATE, A2))
    unpack5(GATE)
    start_tiles(GATE)
    arrived(part[UP].st.at[pl.ds(0, 384)], (UP, A2))
    unpack5(UP)
    start_tiles(UP)
    arrived(part[DOWN].w.at[pl.ds(0, 192)], (DOWN, A2))
    start_tiles(DOWN)

    s.xnz[2 * TOK :, :] = dot(first_norm(s.tokens[2 * TOK :, :]), s.orders[1]).astype(BF)

    boundary = starts[0]
    qi = lax.broadcasted_iota(jnp.int32, (TOK, TOK), 0)
    kj = lax.broadcasted_iota(jnp.int32, (TOK, TOK), 1)
    query_place = me.ctx * TOK + qi
    query_doc = (query_place >= boundary).astype(jnp.int32)
    for back in range(3):
        key_place = (me.ctx - back) * TOK + kj
        gap = query_place - key_place
        key_doc = (key_place >= boundary).astype(jnp.int32)
        allowed = (gap >= 0) & (gap < WINDOW) & (key_place >= 0) & (query_doc == key_doc)
        s.bias[:, back * TOK : back * TOK + TOK] = jnp.where(allowed, 0.0, masked_score)

    kv = s.kv
    cos = s.rope[0, 0]
    sin = s.rope[0, 1]
    for n in (1, 0):
        arrived(part[n].w.at[pl.ds(0, 320)], (n, C))
        field = dot(s.xn[n], part[n].w[...])
        for i in range(2):
            h = 2 * n + i
            s.qs[h * TOK : h * TOK + TOK, :] = (
                rotate(field[:, i * HEAD : i * HEAD + HEAD], cos, sin) * HEAD**-0.5
            ).astype(BF)

    def keys_values(back):
        at = slice(back * TOK, back * TOK + TOK)
        field = dot(s.xnz[at, :], part[2].w[...])
        kv[at, 0:HEAD] = rotate(field[:, 0:HEAD], s.rope[back, 0], s.rope[back, 1]).astype(BF)
        kv[at, HEAD:] = field[:, HEAD:].astype(BF)

    arrived(part[2].w.at[pl.ds(0, 320)], (2, C))
    keys_values(0)
    keys_values(2)

    @pl.when(me.ctx >= 1)
    def _():
        arrived(block(s.tokens, 1), (TK, 1))

    s.xnz[TOK : 2 * TOK, :] = dot(first_norm(s.tokens[TOK : 2 * TOK, :]), s.orders[1]).astype(BF)
    keys_values(1)

    def head_forward(h, carry):
        hs = pl.ds(pl.multiple_of(h * TOK, TOK), TOK)
        scores = dot_nt(s.qs[hs, :], kv[:, 0:HEAD]) + s.bias[...]
        top = jnp.max(scores, axis=1, keepdims=True)
        e = jnp.exp(scores - top)
        p = (e * (1.0 / jnp.sum(e, axis=1, keepdims=True))).astype(BF)
        s.probs[hs, :] = p
        s.mixed[:, hs] = dot(p, kv[:, HEAD:]).astype(BF)
        for name in (GATE, UP, DOWN):
            pass_tile(name, h)
        return carry

    pass_out()
    lax.fori_loop(0, HEADS, head_forward, 0)
    for n in range(2):
        arrived(part[OUT].w.at[pl.ds(0, 128)], (OUT, B2), n)
    half = part[OUT].w.at[rows(me.k * 512, 512)]
    remote(half, half, (OUT, C), sibling)

    x = s.tokens[0:TOK, :].astype(F32)
    arrived(part[OUT].w.at[pl.ds(0, 512)], (OUT, C))
    x1 = x + dot(s.mixed[...], part[OUT].w[...])
    s.x1[...] = x1
    r1 = lax.rsqrt(jnp.mean(x1 * x1, axis=1, keepdims=True) + eps_norm)
    s.x2[0:TOK, :] = (x1 * r1).astype(BF)
    remote(block(s.x2, 0), block(s.x2, 1), X2, sibling)
    arrived(block(s.dy2, 1), DY)
    s.outp[...] = jnp.zeros((2 * TOK, D), F32)
    s.ex[...] = jnp.zeros((2 * TOK, D), F32)
    s.ez[...] = jnp.zeros((2 * TOK, D), F32)
    s.x2z[0:TOK, :] = dot(s.x2[0:TOK, :], s.orders[1]).astype(BF)
    arrived(block(s.x2, 1), X2)
    s.x2z[TOK:, :] = dot(s.x2[TOK:, :], s.orders[1]).astype(BF)

    root = 0.7978845608028654

    def sum_at(name, t):
        if name == DOWN:
            return [rows(t * 64 + zh * 32, 32) for zh in range(2)]
        return [(pl.ds(0, 160), columns(t))]

    def start_sums(name, t):
        j = tile_step(t)
        b = along(me, LAST[name])
        size = 160 if name != DOWN else 256
        for stage, step, source, dst in (
            (E1, j, around(b, 2), part[name].rf),
            (E2, 4 - j, around(b, 4 - j), part[name].r1.at[pl.ds(0, size)]),
        ):
            target = device(*line_chip(me, LAST[name], step), me.k)
            for at, to in zip(tile_of(name, source, t), sum_at(name, t)):
                remote(part[name].g.at[at], dst.at[to], (name, stage), target, t)

    def pass_sums(name, t):
        j = tile_step(t)
        source = around(along(me, LAST[name]), j)
        size = 160 if name != DOWN else 256
        target = device(*line_chip(me, LAST[name], j), me.k)
        arrived(tile_bytes(name, 1), (name, E1), t)
        for at, to in zip(tile_of(name, source, t), sum_at(name, t)):
            part[name].sf[to] = (
                part[name].g[at].astype(F32) + part[name].rf[to].astype(F32)
            ).astype(BF)
            remote(
                part[name].sf.at[to],
                part[name].r1.at[pl.ds(size, size)].at[to],
                (name, E2),
                target,
                t,
            )

    def hidden_step(t, carry):
        for name in (GATE, UP, DOWN):
            arrived(tile_bytes(name, 2), (name, B2), t)
        ts = columns(t)
        w_g, w_u, w_d = part[GATE].w, part[UP].w, part[DOWN].w
        gate = dot(s.x2[...], w_g[:, ts])
        up = dot(s.x2z[...], w_u[:, ts])
        d_hidden = dot_nt(s.dy2[...], w_d[ts, :])
        square = gate * gate
        th = jnp.tanh(root * gate * (1.0 + 0.044715 * square))
        half = 0.5 * (1.0 + th)
        act = gate * half
        slope = half + 0.5 * gate * (1.0 - th * th) * (root * (1.0 + 0.134145 * square))
        hidden = (act * up).astype(BF)
        d_gate = (d_hidden * up * slope).astype(BF)
        d_up = (d_hidden * act).astype(BF)
        part[DOWN].g[ts, :] = dot_tn(hidden, s.dy2[...]).astype(BF)
        part[GATE].g[:, ts] = dot_tn(s.x2[...], d_gate).astype(BF)
        part[UP].g[:, ts] = dot_tn(s.x2z[...], d_up).astype(BF)
        for name in (GATE, UP, DOWN):
            start_sums(name, t)
        s.outp[...] += dot(hidden, w_d[ts, :])
        s.ex[...] += dot_nt(d_gate, w_g[:, ts])
        s.ez[...] += dot_nt(d_up, w_u[:, ts])
        return carry

    lax.fori_loop(0, 4, hidden_step, 0)

    other = s.ex[TOK:, :] + dot_nt(s.ez[TOK:, :].astype(BF), s.orders[1])
    s.esend[...] = other.astype(BF)
    remote(s.esend, s.erecv, EE, sibling)
    s.osend[...] = s.outp[TOK:, :].astype(BF)
    remote(s.osend, s.orecv, OO, sibling)
    e1 = s.ex[0:TOK, :] + dot_nt(s.ez[0:TOK, :].astype(BF), s.orders[1])
    arrived(s.erecv, EE)
    e1 = e1 + s.erecv[...].astype(F32)
    x1 = s.x1[...]
    r1 = lax.rsqrt(jnp.mean(x1 * x1, axis=1, keepdims=True) + eps_norm)
    dx1 = (
        s.cin[...].astype(F32)
        + r1 * e1
        - x1 * (r1 * r1 * r1 * jnp.mean(x1 * e1, axis=1, keepdims=True))
    )
    s.dx1[...] = dx1
    da = dx1.astype(BF)

    def head_backward(h, carry):
        hs = pl.ds(pl.multiple_of(h * TOK, TOK), TOK)
        dmix = dot_nt(da, part[OUT].w[hs, :]).astype(BF)
        s.dmix[hs, :] = dmix
        d_probs = dot_nt(dmix, kv[:, HEAD:])
        p = s.probs[hs, :].astype(F32)
        center = jnp.sum(p * d_probs, axis=1, keepdims=True)
        s.ds[hs, :] = (p * (d_probs - center)).astype(BF)
        for name in (GATE, UP, DOWN):
            pass_sums(name, h)
        return carry

    lax.fori_loop(0, HEADS, head_backward, 0)

    for back in (2, 1, 0):
        at = slice(back * TOK, back * TOK + TOK)
        dk = dot_tn(s.ds[:, at], s.qs[...])
        s.dkv[at, 0:HEAD] = rotate(dk, s.rope[back, 0], -s.rope[back, 1]).astype(BF)
        s.dkv[at, HEAD:] = dot_tn(s.probs[:, at], s.dmix[...]).astype(BF)

    def swap_halves(n):
        for b in range(4):
            remote(
                part[n].g.at[rows(b * 160 + (1 - me.k) * 80, 80)],
                part[n].r0.at[pl.ds(b * 80, 80)],
                (n, D1),
                sibling,
            )

    part[2].g[...] = dot_tn(s.xnz[...], s.dkv[...]).astype(BF)
    swap_halves(2)

    @pl.when((me.zl == 0) & (me.ctx >= 2))
    def _():
        remote(block(s.dkv, 1), block(s.dkvr, 0), (DKV, 0), (me.ctx + 1, me.fsdp))
        remote(block(s.dkv, 2), block(s.dkvr, 2), (DKV, 2), (me.ctx - 2, me.fsdp))

    @pl.when(me.zl == 1)
    def _():
        remote(block(s.dkv, 1), block(s.dkvr, 1), (DKV, 1), (me.ctx - 1, me.fsdp))

    def head_query(h, carry):
        hs = pl.ds(pl.multiple_of(h * TOK, TOK), TOK)
        dq = dot(s.ds[hs, :], kv[:, 0:HEAD]) * HEAD**-0.5
        s.dq[:, hs] = rotate(dq, cos, -sin).astype(BF)
        part[OUT].g[hs, :] = dot_tn(s.mixed[:, hs], da).astype(BF)
        return carry

    lax.fori_loop(0, HEADS, head_query, 0)
    for n in (1, 0):
        part[n].g[...] = dot_tn(s.xn[n], s.dq[:, n * 512 : n * 512 + 512]).astype(BF)
        swap_halves(n)
    remote(part[OUT].g.at[rows((1 - me.k) * 512, 512)], part[OUT].r0, (OUT, D1), sibling)

    def scatter(n, axis, starts_of, size):
        for j in (1, 3, 2):
            chip = line_chip(me, axis, j)
            starts_ = starts_of(*chip)
            for i, start in enumerate(starts_):
                remote(
                    part[n].gp.at[rows(start, size)],
                    part[n].ra.at[pl.ds(((j - 1) * len(starts_) + i) * size, size)],
                    (n, F1),
                    device(*chip, me.k),
                )

    def gathered(n, starts_of, size):
        starts_ = starts_of(me.x, me.y, me.z)
        total = size * len(starts_)
        arrived(part[n].ra, (n, F1))
        for i, start in enumerate(starts_):
            rows_here = part[n].gp[rows(start, size), :].astype(F32)
            for j in range(3):
                at = j * total + i * size
                rows_here = rows_here + part[n].ra[at : at + size, :].astype(F32)
            part[n].ga[i * size : i * size + size, :] = rows_here.astype(BF)

    def q0_rows(x, y, z):
        return [(n * 4 + y) * 32 for n in range(2)]

    def q1_rows(x, y, z):
        return [x * 64]

    def q2_rows(x, y, z):
        return [y * 64]

    def gate_rows(x, y, z):
        return [(n * 4 + y) * 32 for n in range(4)]

    def up_rows(x, y, z):
        return [n * 256 + y * 64 for n in range(2)]

    plane_of = {
        0: (YA, q0_rows, 32),
        1: (XA, q1_rows, 64),
        2: (YA, q2_rows, 64),
        OUT: (YA, q0_rows, 32),
        GATE: (YA, gate_rows, 32),
        UP: (YA, up_rows, 64),
        DOWN: (XA, q1_rows, 64),
    }

    for name in (GATE, UP, DOWN):
        for t in range(4):
            arrived(tile_bytes(name, 2), (name, E2), t)
        r1 = part[name].r1
        if name == DOWN:
            for n in range(8):
                at = slice(n * 32, n * 32 + 32)
                part[DOWN].gp[at, :] = (
                    part[DOWN].g[rows(n * 128 + me.y * 32, 32), :].astype(F32)
                    + r1[at, :].astype(F32)
                    + r1[256 + n * 32 : 256 + n * 32 + 32, :].astype(F32)
                ).astype(BF)
        else:
            total = (
                part[name].g[rows(along(me, LAST[name]) * 160, 160), :].astype(F32)
                + r1[0:160, :].astype(F32)
                + r1[160:320, :].astype(F32)
            ).astype(BF)
            part[name].gp[:, 0:256] = (
                dot_tn(s.pick5[0], total[:, 0:256])
                + dot_tn(s.pick5[1], total[:, 384:640])
                + dot_tn(s.pick5[2], total[:, 768:1024])
            ).astype(BF)
            part[name].gp[:, 256:384] = (
                dot_tn(s.pick5[0], total[:, 256:384]) + dot_tn(s.pick5[1], total[:, 640:768])
            ).astype(BF)
        scatter(name, *plane_of[name])

    def to_blocks(n, starts_of, size):
        for j in (1, 3, 2):
            b = around(along(me, LAST[n]), j)
            for i, start in enumerate(starts_of(b)):
                remote(
                    part[n].gs.at[rows(start, size)],
                    part[n].r1.at[pl.ds(((j - 1) * len(starts_of(b)) + i) * size, size)],
                    (n, E1),
                    device(*line_chip(me, LAST[n], j), me.k),
                )

    def qkv_rows(b):
        return [b * 80]

    def out_half_rows(b):
        return [n * 256 + lax.rem(b, 2) * 128 + lax.div(b, 2) * 64 for n in range(2)]

    for n in (2, 1, 0):
        arrived(part[n].r0, (n, D1))
        for b in range(4):
            at = slice(b * 80, b * 80 + 80)
            part[n].gs[at, :] = (
                part[n].g[rows(b * 160 + me.k * 80, 80), :].astype(F32)
                + part[n].r0[at, :].astype(F32)
            ).astype(BF)
        to_blocks(n, qkv_rows, 80)
    arrived(part[OUT].r0, (OUT, D1))
    part[OUT].gs[...] = (
        part[OUT].g[rows(me.k * 512, 512), :].astype(F32) + part[OUT].r0[...].astype(F32)
    ).astype(BF)
    to_blocks(OUT, out_half_rows, 64)

    def owners_same(n, axis):
        home = part[n].rb.at[rows(along(me, axis) * 16, 16)]
        own_copy(part[n].ga.at[rows(along(me, axis) * 16, 16)], home, (n, F2))
        for j in (1, 3, 2):
            chip = line_chip(me, axis, j)
            remote(
                part[n].ga.at[rows(chip[axis] * 16, 16)],
                home,
                (n, F2),
                device(*chip, me.k),
            )

    def owners_low(n, axis):
        home = part[n].rb.at[rows(along(me, axis) * 16, 16)]
        for i in range(2):
            for core in range(2):
                if axis == ZA:
                    chip = (me.x, me.y, 2 * i + me.k)
                    here = chip[2] == me.z
                else:
                    chip = (2 * me.k + i, me.y, me.z)
                    here = chip[0] == me.x
                src = part[n].ga.at[pl.ds((i * 2 + core) * 16, 16)]
                mine = here & (me.k == core)

                @pl.when(mine)
                def _():
                    own_copy(src, home, (n, F2))

                @pl.when(jnp.logical_not(mine))
                def _():
                    remote(src, home, (n, F2), device(*chip, core))

    def owners_both(n, axis, slot_of):
        home = part[n].rb.at[rows((me.k * 4 + along(me, axis)) * 16, 16)]
        for j in (0, 1, 3, 2):
            chip = line_chip(me, axis, j)
            for flip in range(2):
                core = lax.rem(me.k + flip, 2)
                src = part[n].ga.at[rows(slot_of(chip[axis], core) * 16, 16)]
                if j == 0 and flip == 0:
                    own_copy(src, home, (n, F2))
                else:
                    remote(src, home, (n, F2), device(*chip, core))

    def spread_owners(n):
        gathered(n, *plane_of[n][1:])
        if n == 1:
            owners_same(1, ZA)
        elif n == 2:
            owners_same(2, XA)
        elif n == GATE:
            owners_both(n, ZA, lambda z, core: (lax.rem(z, 2) * 2 + lax.div(z, 2)) * 2 + core)
        elif n == UP:
            owners_both(n, XA, lambda place, core: core * 4 + place)
        else:
            owners_low(n, XA if n == OUT else ZA)

    for name in (GATE, UP, DOWN):
        spread_owners(name)

    for n in (2, 1, 0):
        arrived(part[n].r1, (n, E1))
        total = part[n].gs[rows(along(me, LAST[n]) * 80, 80), :].astype(F32)
        for j in range(3):
            total = total + part[n].r1[j * 80 : j * 80 + 80, :].astype(F32)
        total = total.astype(BF)
        part[n].gp[...] = (
            dot_tn(s.pick5[0, 0:80, 0:256], total[:, 0:256])
            + dot_tn(s.pick5[1, 0:80, 0:256], total[:, 256:512])
        ).astype(BF)
        scatter(n, *plane_of[n])

    arrived(part[OUT].r1, (OUT, E1))
    halves = []
    for i, start in enumerate(out_half_rows(me.z)):
        total = part[OUT].gs[rows(start, 64), :].astype(F32)
        for j in range(3):
            at = (j * 2 + i) * 64
            total = total + part[OUT].r1[at : at + 64, :].astype(F32)
        halves.append(total.astype(BF))
    total = jnp.concatenate(halves, axis=0)
    part[OUT].gp[:, 0:256] = (
        dot_tn(s.pick8[0], total[:, 0:256]) + dot_tn(s.pick8[1], total[:, 384:640])
    ).astype(BF)
    part[OUT].gp[:, 256:384] = dot_tn(s.pick8[0], total[:, 256:384]).astype(BF)
    scatter(OUT, *plane_of[OUT])

    @pl.when((me.zl == 1) & (me.ctx >= 2))
    def _():
        arrived(block(s.dkvr, 0), (DKV, 0))
        s.dkvs[...] = (s.dkv[2 * TOK :, :].astype(F32) + s.dkvr[0:TOK, :].astype(F32)).astype(BF)
        remote(s.dkvs, block(s.dkvr, 2), (DKV, 2), (me.ctx - 2, me.fsdp))

    e0 = dot_nt(s.dq[:, 0:512], part[0].w[...])
    field = dot_nt(s.dq[:, 512:1024], part[1].w[...])
    e0 = e0 + dot_nt(field.astype(BF), s.orders[0])
    s.ex[0:TOK, :] = e0
    arrived(s.orecv, OO)
    lo[...] = s.x1[...] + s.outp[0:TOK, :] + s.orecv[...].astype(F32)

    for n in (2, 1, 0, OUT):
        spread_owners(n)

    @pl.when(me.ctx < 6)
    def _():
        arrived(block(s.dkvr, 2), (DKV, 2))

    @pl.when(me.ctx >= 6)
    def _():
        s.dkvr[2 * TOK :, :] = jnp.zeros((TOK, 2 * HEAD), BF)

    @pl.when(me.zl == 0)
    def _():
        arrived(block(s.dkvr, 1), (DKV, 1))

    @pl.when(me.zl == 1)
    def _():
        s.dkvr[TOK : 2 * TOK, :] = jnp.zeros((TOK, 2 * HEAD), BF)

    dkv = (
        s.dkv[0:TOK, :].astype(F32)
        + s.dkvr[TOK : 2 * TOK, :].astype(F32)
        + s.dkvr[2 * TOK :, :].astype(F32)
    ).astype(BF)
    field = dot_nt(dkv, part[2].w[...])
    e0 = s.ex[0:TOK, :] + dot_nt(field.astype(BF), s.orders[1])
    x = s.tokens[0:TOK, :].astype(F32)
    r0 = lax.rsqrt(jnp.mean(x * x, axis=1, keepdims=True) + eps_norm)
    ig[...] = s.dx1[...] + r0 * e0 - x * (r0 * r0 * r0 * jnp.mean(x * e0, axis=1, keepdims=True))

    def line_total(n, out, first):
        base = first * 4
        total = part[n].rb[base : base + 16, :].astype(F32)
        for p in range(1, 4):
            total = total + part[n].rb[base + p * 16 : base + p * 16 + 16, :].astype(F32)
        out[first : first + 16, :] = total

    for n, out in ((GATE, sg), (UP, su), (DOWN, sd), (2, sq2), (1, sq1), (0, sq0), (OUT, so)):
        arrived(part[n].rb, (n, F2))
        line_total(n, out, 0)
        if n in (GATE, UP):
            line_total(n, out, 16)

    def left_or(condition, ref, name, low, high):
        @pl.when(condition)
        def _():
            left(ref.at[pl.ds(0, low)], name)

        @pl.when(jnp.logical_not(condition))
        def _():
            left(ref.at[pl.ds(0, high)], name)

    for n in range(7):
        p = part[n]
        home = {0: me.zl, OUT: xh, DOWN: me.zl}
        if n in home:
            left_or(home[n] == me.k, p.gp, (n, A1), 48, 64)
            left_or(home[n] == me.k, p.gp, (n, F2), 48, 64)
        elif n in (GATE, UP):
            left(p.st.at[pl.ds(0, 7 * 16)], (n, A1))
            left(p.rb.at[pl.ds(0, 7 * 16)], (n, F2))
        else:
            left(p.st.at[pl.ds(0, 48)], (n, A1))
            left(p.rb.at[pl.ds(0, 48)], (n, F2))
        left(p.ra, (n, F1))
    for n in range(3):
        left(part[n].st.at[pl.ds(0, 192)], (n, A2))
        left(part[n].w.at[pl.ds(0, 240)], (n, B1))
        left(part[n].w.at[pl.ds(0, 320)], (n, C))
        left(part[n].r0, (n, D1))
        left(part[n].r1, (n, E1))
    left(part[OUT].st.at[pl.ds(0, 192)], (OUT, A2))
    left(part[OUT].w.at[pl.ds(0, 128)], (OUT, B1))
    left(part[OUT].w.at[pl.ds(0, 256)], (OUT, B2))
    left(part[OUT].w.at[pl.ds(0, 512)], (OUT, C))
    left(part[OUT].r0, (OUT, D1))
    left(part[OUT].r1, (OUT, E1))
    for name in (GATE, UP, DOWN):
        if name == DOWN:
            left(part[name].w.at[pl.ds(0, 192)], (name, A2))
        else:
            left(part[name].st.at[pl.ds(0, 384)], (name, A2))
        block_rows = 256 if name == DOWN else 160
        left(part[name].w.at[pl.ds(0, block_rows)], (name, B1))
        left(part[name].w.at[pl.ds(0, 2 * block_rows)], (name, B2))
        left(part[name].w.at[pl.ds(0, block_rows)], (name, E1))
        left(part[name].w.at[pl.ds(0, 2 * block_rows)], (name, E2))
    left(s.cin, DY)
    left(s.esend, EE)
    left(s.osend, OO)
    left(s.osend, X2)

    @pl.when(me.ctx < 6)
    def _():
        left(block(s.tokens, 0), (TK, 2))

    @pl.when((me.zl == 0) | (me.ctx >= 2))
    def _():
        left(block(s.tokens, 0), (TK, 1))

    @pl.when((me.zl == 0) & (me.ctx >= 2))
    def _():
        left(s.dkvs, (DKV, 0))

    @pl.when(me.ctx >= 2)
    def _():
        left(s.dkvs, (DKV, 2))

    @pl.when(me.zl == 1)
    def _():
        left(s.dkvs, (DKV, 1))

    assert taken[0] <= SEMS


def whole_step(tokens, cotangent, starts, wq, wo, wgu, wd, gains):
    orders, pick5, pick8, rope = constants()
    scratch = scratch_list()
    vmem = pl.BlockSpec(memory_space=pltpu.VMEM)
    anywhere = pl.BlockSpec(memory_space=pl.ANY)
    smem = pl.BlockSpec(memory_space=pltpu.SMEM)
    shapes = [(TOK, D), (TOK, D)] + [(16, 256)] * 3 + [(16, 384), (32, 384), (32, 384), (16, 640)]
    return pl.pallas_call(
        functools.partial(step_kernel, scratch),
        name="whole_step",
        out_shape=[jax.ShapeDtypeStruct(shape, F32) for shape in shapes],
        in_specs=[anywhere, anywhere, smem] + [vmem] * 5 + [anywhere] * 4,
        out_specs=[vmem] * len(shapes),
        scratch_shapes=leaves(scratch)
        + [
            pltpu.SemaphoreType.DMA((12,)),
            pltpu.SemaphoreType.DMA((SEMS,)),
            pltpu.SemaphoreType.DMA((SEMS,)),
        ],
        compiler_params=pltpu.CompilerParams(
            collective_id=0, has_side_effects=True, vmem_limit_bytes=62 * 2**20
        ),
        cost_estimate=pl.CostEstimate(
            flops=12_000_000_000, bytes_accessed=8_000_000, transcendentals=2_000_000
        ),
    )(tokens, cotangent, starts, wq, wo, wgu, wd, gains, orders, pick5, pick8, rope)


def adamw(master, first, second, gradient, rate, decay):
    first_next = beta_one * first + (1.0 - beta_one) * gradient
    second_next = beta_two * second + (1.0 - beta_two) * gradient * gradient
    first_fixed = first_next * (1.0 / (1.0 - beta_one**STEP))
    second_fixed = second_next * (1.0 / (1.0 - beta_two**STEP))
    update = first_fixed / (jnp.sqrt(second_fixed) + eps_adam) + decay * master
    return master - rate * update, first_next, second_next


def update_kernel(*refs):
    inner = refs[41:65]
    sem = refs[65]
    copies = [
        pltpu.make_async_copy(src, dst, sem.at[n])
        for n, (src, dst) in enumerate(zip(refs[:24], inner))
    ]
    for one in copies:
        one.start()
    (sq0, sq1, sq2, so, sg, su, sd) = inner[2:9]
    (wq, qf, qs, wo, of, os_, wgu, gf, gs, wd, df, ds_, gains, nf, ns) = inner[9:]
    (oq, oqf, oqs, oo, oof, oos, og, ogf, ogs, od, odf, ods, on, onf, ons) = refs[26:41]
    for one in copies:
        one.wait()
    through = [
        pltpu.make_async_copy(inner[n], refs[24 + n].at[0], sem.at[24 + n]) for n in range(2)
    ]
    for one in through:
        one.start()

    rate = 1.5 * D**-0.5
    gain0 = column(gains[0:1, :])
    gain1 = column(gains[1:2, :])
    total0 = jnp.zeros((5, 1), F32)
    for n, share in enumerate((sq0, sq1, sq2)):
        for g in range(2):
            at = slice(n * 512 + g * 256, n * 512 + g * 256 + 256)
            raw = share[5 * g : 5 * g + 5, :]
            w = wq[:, at]
            total0 = total0 + jnp.sum(w.astype(BF).astype(F32) * raw, axis=1, keepdims=True)
            oq[:, at], oqf[:, at], oqs[:, at] = adamw(
                w, qf[:, at], qs[:, at], raw * gain0, rate, weight_decay
            )
    total1 = jnp.zeros((5, 1), F32)
    for n, share in enumerate((sg, su)):
        for c in range(2):
            for t in range(8):
                g, i = t // 3, t % 3
                base = n * FF + (t // 2) * 512 + c * 256 + (t % 2) * 128
                at = slice(base, base + 128)
                raw = share[c * 16 + 5 * g : c * 16 + 5 * g + 5, i * 128 : i * 128 + 128]
                w = wgu[:, at]
                total1 = total1 + jnp.sum(w.astype(BF).astype(F32) * raw, axis=1, keepdims=True)
                og[:, at], ogf[:, at], ogs[:, at] = adamw(
                    w, gf[:, at], gs[:, at], raw * gain1, rate, weight_decay
                )
    rate = 1.5 * OUT_FAN**-0.5
    for r, at in ((0, slice(0, 384)), (8, slice(384, 640))):
        raw = so[r : r + 8, 0 : at.stop - at.start]
        oo[:, at], oof[:, at], oos[:, at] = adamw(
            wo[:, at], of[:, at], os_[:, at], raw, rate, weight_decay
        )
    od[...], odf[...], ods[...] = adamw(
        wd[...], df[...], ds_[...], sd[...], 1.5 * FF**-0.5, weight_decay
    )
    i = lax.broadcasted_iota(jnp.int32, (5, 5), 0)
    j = lax.broadcasted_iota(jnp.int32, (5, 5), 1)
    for row, total in ((0, total0), (1, total1)):
        flat = jnp.sum(jnp.where(i == j, jnp.broadcast_to(total, (5, 5)), 0.0), axis=0, keepdims=True)
        at = slice(row, row + 1)
        on[at, :], onf[at, :], ons[at, :] = adamw(gains[at, :], nf[at, :], ns[at, :], flat, 0.5, 0.0)
    for one in through:
        one.wait()


def update(*arrays):
    vmem = pl.BlockSpec(memory_space=pltpu.VMEM)
    anywhere = pl.BlockSpec(memory_space=pl.ANY)
    outs = [jax.ShapeDtypeStruct((1, TOK, D), F32)] * 2 + [
        jax.ShapeDtypeStruct(a.shape, F32) for a in arrays[9:]
    ]
    return pl.pallas_call(
        update_kernel,
        name="update",
        out_shape=outs,
        in_specs=[anywhere] * len(arrays),
        out_specs=[anywhere] * 2 + [vmem] * (len(outs) - 2),
        scratch_shapes=[pltpu.VMEM(a.shape, F32) for a in arrays]
        + [pltpu.SemaphoreType.DMA((len(arrays) + 2,))],
        compiler_params=pltpu.CompilerParams(vmem_limit_bytes=60 * 2**20),
    )(*arrays)


def body(
    tokens,
    cotangent,
    starts,
    qkv_weight,
    qkv_first,
    qkv_second,
    out_weight,
    out_first,
    out_second,
    gate_up_weight,
    gate_up_first,
    gate_up_second,
    down_weight,
    down_first,
    down_second,
    norm_gains,
    gains_first,
    gains_second,
):
    results = whole_step(
        tokens, cotangent, starts, qkv_weight, out_weight, gate_up_weight, down_weight, norm_gains
    )
    return tuple(
        update(
            *results,
            qkv_weight,
            qkv_first,
            qkv_second,
            out_weight,
            out_first,
            out_second,
            gate_up_weight,
            gate_up_first,
            gate_up_second,
            down_weight,
            down_first,
            down_second,
            norm_gains,
            gains_first,
            gains_second,
        )
    )


def solution(mesh):
    act = P("fsdp", "ctx", None)
    row = P(("ctx", "fsdp"), None)
    gain = P(None, ("ctx", "fsdp"))
    return jax.shard_map(
        body,
        mesh=mesh,
        in_specs=(act, act, P("fsdp")) + (row,) * 12 + (gain,) * 3,
        out_specs=(act, act) + (row,) * 12 + (gain,) * 3,
        check_vma=False,
    )
```

```python
import functools

import jax
import jax.numpy as jnp
import numpy as np
from jax import lax
from jax.experimental import pallas as pl
from jax.experimental.pallas import tpu as pltpu
from jax.sharding import PartitionSpec as P

D = 640
HEADS = 4
HEAD = 256
FF = 2048
WINDOW = 512
STEP = 10
QW = 1024
OUT_FAN = 8
TOK = 256
LENGTH = 2048

eps_norm = 1e-06
beta_one = 0.9
beta_two = 0.95
eps_adam = 1e-08
weight_decay = 0.1
masked_score = -1e30

MESH = pl.DeviceIdType.MESH
BF = jnp.bfloat16
F32 = jnp.float32


class Place:
    def __init__(self):
        self.ctx = lax.axis_index("ctx")
        self.fsdp = lax.axis_index("fsdp")
        self.x = lax.div(self.ctx, 2)
        self.zl = lax.rem(self.ctx, 2)
        self.zh = lax.div(self.fsdp, 8)
        self.y = lax.div(lax.rem(self.fsdp, 8), 2)
        self.k = lax.rem(self.fsdp, 2)
        self.z = 2 * self.zh + self.zl


def device(x, y, z, k):
    return (2 * x + lax.rem(z, 2), 8 * lax.div(z, 2) + 2 * y + k)


def around(a, b):
    return lax.rem(a + b, 4)


def plane_chip(me, last, j):
    a, b = lax.rem(j, 4), lax.div(j, 4)
    if last == XA:
        return me.x, around(me.y, a), around(me.z, b)
    if last == YA:
        return around(me.x, a), me.y, around(me.z, b)
    return around(me.x, a), around(me.y, b), me.z


def line_chip(me, last, j):
    if last == XA:
        return around(me.x, j), me.y, me.z
    if last == YA:
        return me.x, around(me.y, j), me.z
    return me.x, me.y, around(me.z, j)


def along(me, last):
    return (me.x, me.y, me.z)[last]


def in_plane(last, x, y, z):
    if last == XA:
        return lax.rem(z, 2) * 8 + lax.div(z, 2) * 4 + y
    if last == YA:
        return 4 * x + z
    return 4 * x + y


def rows(start, size):
    return pl.ds(pl.multiple_of(start, 16), size)


def feature_order(last):
    order = np.zeros(D, np.int64)
    for x in range(4):
        for y in range(4):
            for z in range(4):
                for k in range(2):
                    dev = x * 32 + (z % 2) * 16 + (z // 2) * 8 + y * 2 + k
                    b, p = (y, 4 * x + z) if last == YA else (z, 4 * y + x)
                    for r in range(5):
                        order[b * 160 + k * 80 + p * 5 + r] = 5 * dev + r
    return order


def constants():
    orders = np.zeros((2, D, D), np.float32)
    for n, last in enumerate((YA, ZA)):
        orders[n, feature_order(last), np.arange(D)] = 1.0
    pick5 = np.zeros((3, 160, 512), np.float32)
    for g in range(3):
        for s in range(32):
            for r in range(5):
                pick5[g, s * 5 + r, s * 16 + g * 5 + r] = 1.0
    pick8 = np.zeros((2, 128, 256), np.float32)
    for g in range(2):
        for s in range(16):
            for r in range(8):
                pick8[g, s * 8 + r, s * 16 + g * 8 + r] = 1.0
    half = HEAD // 2
    frequency = np.float32(10000.0) ** (
        -(np.float32(2.0) * np.arange(half, dtype=np.float32)) / np.float32(HEAD)
    )
    angles = np.arange(LENGTH, dtype=np.float32)[:, None] * frequency.astype(np.float32)[None, :]
    rope = np.stack([np.cos(angles.astype(np.float64)), np.sin(angles.astype(np.float64))])
    return (
        jnp.asarray(orders, BF),
        jnp.asarray(pick5, BF),
        jnp.asarray(pick8, BF),
        jnp.asarray(rope.astype(np.float32)),
    )


def dot(a, b):
    return lax.dot_general(a, b, (((1,), (0,)), ((), ())), preferred_element_type=F32)


def dot_nt(a, b):
    return lax.dot_general(a, b, (((1,), (1,)), ((), ())), preferred_element_type=F32)


def dot_tn(a, b):
    return lax.dot_general(a, b, (((0,), (0,)), ((), ())), preferred_element_type=F32)


def rotate(u, cos, sin):
    a, b = u[:, :128], u[:, 128:]
    return jnp.concatenate([a * cos - b * sin, b * cos + a * sin], axis=1)


def column(row):
    n = row.shape[1]
    i = lax.broadcasted_iota(jnp.int32, (n, n), 0)
    j = lax.broadcasted_iota(jnp.int32, (n, n), 1)
    wide = jnp.broadcast_to(row.astype(BF).astype(F32), (n, n))
    return jnp.sum(jnp.where(i == j, wide, 0.0), axis=1, keepdims=True)


class Bag(dict):
    __getattr__ = dict.__getitem__


def scratch_list():
    def v(*shape, kind=BF):
        return pltpu.VMEM(shape, kind)

    qkv = [
        Bag(
            pk=v(16, 256),
            st=v(256, 256),
            w=v(640, 512),
            g=v(640, 512),
            r0=v(320, 512),
            gs=v(320, 512),
            r1=v(240, 512),
            gp=v(256, 256),
            ra=v(192, 256),
            ga=v(64, 256),
            rb=v(64, 256),
        )
        for n in range(3)
    ]
    out = Bag(
        pk=v(16, 384),
        st=v(256, 384),
        w=v(1024, 640),
        g=v(1024, 640),
        r0=v(512, 640),
        gs=v(512, 640),
        r1=v(384, 640),
        gp=v(256, 384),
        ra=v(192, 384),
        ga=v(64, 384),
        rb=v(64, 384),
    )
    gate_up = [
        Bag(
            pk=v(32, 384),
            st=v(512, 384),
            w=v(640, 1024),
            g=v(640, 1024),
            rf=v(160, 1024),
            sf=v(160, 1024),
            r1=v(320, 1024),
            gp=v(512, 384),
            ra=v(384, 384),
            ga=v(128, 384),
            rb=v(128, 384),
        )
        for n in range(2)
    ]
    down = Bag(
        pk=v(16, 640),
        w=v(1024, 640),
        g=v(1024, 640),
        rf=v(256, 640),
        sf=v(256, 640),
        r1=v(512, 640),
        gp=v(256, 640),
        ra=v(192, 640),
        ga=v(64, 640),
        rb=v(64, 640),
    )
    return Bag(
        part=qkv + [out] + gate_up + [down],
        tokens=v(3 * TOK, D),
        cin=v(TOK, D),
        orders=v(2, D, D),
        pick5=v(3, 160, 512),
        pick8=v(2, 128, 256),
        rope=v(3, 2, TOK, 128, kind=F32),
        pad=v(16, 384, kind=F32),
        xn=v(2, TOK, D),
        xnz=v(3 * TOK, D),
        qs=v(HEADS * TOK, HEAD),
        kv=v(3 * TOK, 2 * HEAD),
        bias=v(TOK, 3 * TOK, kind=F32),
        probs=v(HEADS * TOK, 3 * TOK),
        ds=v(HEADS * TOK, 3 * TOK),
        mixed=v(TOK, QW),
        dmix=v(HEADS * TOK, HEAD),
        x1=v(TOK, D, kind=F32),
        x2=v(2 * TOK, D),
        x2z=v(2 * TOK, D),
        dy2=v(2 * TOK, D),
        hidden=v(2 * TOK, FF // 2),
        d_gate=v(2 * TOK, FF // 2),
        d_up=v(2 * TOK, FF // 2),
        outp=v(TOK, D, kind=F32),
        e0=v(TOK, D, kind=F32),
        osend=v(TOK, D),
        orecv=v(TOK, D),
        esend=v(TOK, D),
        erecv=v(TOK, D),
        dx1=v(TOK, D, kind=F32),
        dq=v(TOK, QW),
        dkv=v(3 * TOK, 2 * HEAD),
        dkvr=v(3 * TOK, 2 * HEAD),
        dkvs=v(TOK, 2 * HEAD),
    )


def leaves(tree):
    if isinstance(tree, dict):
        return [leaf for branch in tree.values() for leaf in leaves(branch)]
    if isinstance(tree, list):
        return [leaf for branch in tree for leaf in leaves(branch)]
    return [tree]


def refill(tree, values):
    if isinstance(tree, dict):
        return Bag({key: refill(branch, values) for key, branch in tree.items()})
    if isinstance(tree, list):
        return [refill(branch, values) for branch in tree]
    return next(values)


OUT, GATE, UP, DOWN = 3, 4, 5, 6
XA, YA, ZA = range(3)
LAST = (XA, YA, ZA, ZA, XA, ZA, YA)
A1, A2, B1, B2, C, D1, E1, E2, F1, F2 = range(10)
DY, X2, EE, OO, TK, DKV = range(7, 13)
SEMS = 128


def wait_for(ref, sem):
    pltpu.make_async_copy(ref, ref, sem).wait()


def step_kernel(shape, *refs):
    (tok, cot, starts, wq, wo, wgu, wd, gains, orders_h, pick5_h, pick8_h, rope_h) = refs[:12]
    (lo, ig, sq0, sq1, sq2, so, sg, su, sd) = refs[12:21]
    s = refill(shape, iter(refs[21:-3]))
    local, sent, came = refs[-3:]
    me = Place()
    sems = {}
    taken = [0]

    def sem_of(name, size=1):
        if name not in sems:
            sems[name] = taken[0]
            taken[0] += size
        return sems[name]

    def remote(src, dst, name, target, tile=None):
        n = sem_of(name, 1 if tile is None else 4)
        pltpu.make_async_remote_copy(
            src_ref=src,
            dst_ref=dst,
            send_sem=sent.at[n],
            recv_sem=came.at[n if tile is None else n + tile],
            device_id=target,
            device_id_type=MESH,
        ).start()

    def own_copy(src, dst, name):
        pltpu.make_async_copy(src, dst, came.at[sem_of(name)]).start()

    def arrived(ref, name, tile=0):
        wait_for(ref, came.at[sem_of(name) + tile])

    def left(ref, name):
        wait_for(ref, sent.at[sem_of(name)])

    sibling = device(me.x, me.y, me.z, 1 - me.k)

    fetch = [
        (tok.at[0], s.tokens.at[pl.ds(0, TOK)]),
        (orders_h, s.orders),
        (pick5_h, s.pick5),
        (pick8_h, s.pick8),
        (cot.at[0], s.cin),
        (cot.at[0], s.dy2.at[pl.ds(0, TOK)]),
    ]
    for back in range(3):
        block = jnp.maximum(me.ctx - back, 0) * TOK
        fetch.append((rope_h.at[:, pl.ds(pl.multiple_of(block, TOK), TOK), :], s.rope.at[back]))
    fetches = [pltpu.make_async_copy(a, b, local.at[n]) for n, (a, b) in enumerate(fetch)]
    for one in fetches:
        one.start()

    barrier = pltpu.get_barrier_semaphore()
    for j in range(1, 4):
        for axis in range(3):
            for core in range(2):
                pl.semaphore_signal(
                    barrier,
                    inc=1,
                    device_id=device(*line_chip(me, axis, j), core),
                    device_id_type=MESH,
                )
    pl.semaphore_signal(barrier, inc=1, device_id=sibling, device_id_type=MESH)

    pad = s.pad
    pad[...] = jnp.zeros((16, 384), F32)
    wqb = wq[...].astype(BF).astype(F32) * column(gains[0:1, :])
    for n in range(3):
        for g in range(2):
            pad[5 * g : 5 * g + 5, 0:256] = wqb[:, n * 512 + g * 256 : n * 512 + g * 256 + 256]
        s.part[n].pk[...] = pad[:, 0:256].astype(BF)
    gain = column(gains[1:2, :])
    for n, name in enumerate((GATE, UP)):
        for c in range(2):
            for t in range(8):
                g, i = t // 3, t % 3
                base = n * FF + (t // 2) * 512 + c * 256 + (t % 2) * 128
                pad[5 * g : 5 * g + 5, i * 128 : i * 128 + 128] = (
                    wgu[:, base : base + 128].astype(BF).astype(F32) * gain
                )
            pad[10:15, 256:384] = jnp.zeros((5, 128), F32)
            s.part[name].pk[c * 16 : c * 16 + 16, :] = pad[...].astype(BF)
    pad[0:8, :] = wo[:, 0:384]
    pad[8:16, 0:256] = wo[:, 384:640]
    pad[8:16, 256:384] = jnp.zeros((8, 128), F32)
    s.part[OUT].pk[...] = pad[...].astype(BF)
    s.part[DOWN].pk[...] = wd[...].astype(BF)
    fetches[0].wait()
    pl.semaphore_wait(barrier, 19)

    def to_line(axis, src, dst, name, core):
        for j in (1, 3, 2):
            remote(src, dst, name, device(*line_chip(me, axis, j), core))

    def to_line_core(axis, src, dst, name, core):
        to_line(axis, src, dst, name, core)

        @pl.when(core == me.k)
        def _():
            own_copy(src, dst, name)

        @pl.when(core != me.k)
        def _():
            remote(src, dst, name, sibling)

    def to_line_both(axis, src, dst, name):
        for j in (1, 3, 2):
            for core in range(2):
                remote(
                    src.at[pl.ds(core * 16, 16)], dst, name, device(*line_chip(me, axis, j), core)
                )
        own_copy(src.at[rows(me.k * 16, 16)], dst, name)
        remote(src.at[rows((1 - me.k) * 16, 16)], dst, name, sibling)

    xh, xl = lax.div(me.x, 2), lax.rem(me.x, 2)
    zi = me.zl * 2 + me.zh
    part = s.part
    place = part[2].st.at[rows((4 * me.y + me.x) * 16, 16)]
    own_copy(part[2].pk, place, (2, A1))
    to_line(XA, part[2].pk, place, (2, A1), me.k)
    place = part[1].st.at[rows((4 * me.x + me.z) * 16, 16)]
    own_copy(part[1].pk, place, (1, A1))
    to_line(ZA, part[1].pk, place, (1, A1), me.k)
    low_slot = (me.zh * 4 + me.y) * 2 + me.k
    to_line_core(ZA, part[0].pk, part[0].st.at[rows(low_slot * 16, 16)], (0, A1), me.zl)

    def block(ref, back):
        return ref.at[pl.ds(back * TOK, TOK)]

    @pl.when(me.ctx < 6)
    def _():
        remote(block(s.tokens, 0), block(s.tokens, 2), (TK, 2), (me.ctx + 2, me.fsdp))

    @pl.when(me.zl == 0)
    def _():
        remote(block(s.tokens, 0), block(s.tokens, 1), (TK, 1), (me.ctx + 1, me.fsdp))

    def first_norm(rows_in):
        field = rows_in.astype(F32)
        r = lax.rsqrt(jnp.mean(field * field, axis=1, keepdims=True) + eps_norm)
        return (field * r).astype(BF)

    xn = first_norm(s.tokens[0:TOK, :])
    s.xn[0] = xn
    for n in range(1, len(fetches)):
        fetches[n].wait()
    s.xn[1] = dot(xn, s.orders[0]).astype(BF)
    s.xnz[0:TOK, :] = dot(xn, s.orders[1]).astype(BF)

    def pieces_on(axis, ref, starts_, size, name):
        for j in (1, 3, 2):
            for start in starts_:
                at = ref.at[rows(start, size)]
                remote(at, at, name, device(*line_chip(me, axis, j), me.k))

    arrived(part[2].st.at[pl.ds(0, 64)], (2, A1))
    pieces_on(YA, part[2].st, [me.y * 64], 64, (2, A2))
    arrived(part[1].st.at[pl.ds(0, 64)], (1, A1))
    pieces_on(XA, part[1].st, [me.x * 64], 64, (1, A2))
    arrived(part[0].st.at[pl.ds(0, 64)], (0, A1))
    pieces_on(YA, part[0].st, [(zh * 4 + me.y) * 32 for zh in range(2)], 32, (0, A2))
    remote(s.cin, block(s.dy2, 1), DY, sibling)
    out_slot = (xl * 4 + me.y) * 2 + me.k
    to_line_core(XA, part[OUT].pk, part[OUT].st.at[rows(out_slot * 16, 16)], (OUT, A1), xh)
    gate_slot = (zi * 4 + me.y) * 2 + me.k
    to_line_both(YA, part[GATE].pk, part[GATE].st.at[rows(gate_slot * 16, 16)], (GATE, A1))
    up_slot = me.k * 16 + me.y * 4 + me.x
    to_line_both(XA, part[UP].pk, part[UP].st.at[rows(up_slot * 16, 16)], (UP, A1))
    down_row = me.x * 256 + me.zh * 128 + me.y * 32 + me.k * 16
    to_line_core(ZA, part[DOWN].pk, part[DOWN].w.at[rows(down_row, 16)], (DOWN, A1), me.zl)

    for n in (2, 1, 0):
        arrived(part[n].st.at[pl.ds(0, 192)], (n, A2))
        start = along(me, LAST[n]) * 160 + me.k * 80
        st = part[n].st[...]
        for g in range(2):
            part[n].w[rows(start, 80), g * 256 : g * 256 + 256] = dot(
                s.pick5[g, 0:80, 0:256], st
            ).astype(BF)
        pieces_on(LAST[n], part[n].w, [start], 80, (n, B1))

    arrived(part[OUT].st.at[pl.ds(0, 64)], (OUT, A1))
    pieces_on(YA, part[OUT].st, [(n * 4 + me.y) * 32 for n in range(2)], 32, (OUT, A2))
    arrived(part[GATE].st.at[pl.ds(0, 128)], (GATE, A1))
    pieces_on(ZA, part[GATE].st, [zi * 128], 128, (GATE, A2))
    arrived(part[UP].st.at[pl.ds(0, 128)], (UP, A1))
    pieces_on(YA, part[UP].st, [n * 256 + me.y * 64 for n in range(2)], 64, (UP, A2))
    arrived(part[DOWN].w.at[pl.ds(0, 64)], (DOWN, A1))
    pieces_on(
        XA, part[DOWN].w, [me.x * 256 + n * 128 + me.y * 32 for n in range(2)], 32, (DOWN, A2)
    )

    def columns(t):
        return pl.ds(pl.multiple_of(t * 256, 256), 256)

    def tile_of(name, b, t):
        if name == DOWN:
            return [rows(t * 256 + zh * 128 + b * 32, 32) for zh in range(2)]
        return [(rows(b * 160, 160), columns(t))]

    def tile_step(t):
        return 1 + 2 * lax.rem(t, 2)

    def start_tiles(name):
        b = along(me, LAST[name])
        ref = part[name].w
        for t in range(4):
            ahead = 1 + 2 * (t % 2)
            for at in tile_of(name, b, t):
                for stage, j in ((B1, ahead), (B2, 4 - ahead)):
                    target = device(*line_chip(me, LAST[name], j), me.k)
                    remote(ref.at[at], ref.at[at], (name, stage), target, t)

    def pass_tile(name, t):
        j = tile_step(t)
        b = around(along(me, LAST[name]), 4 - j)
        ref = part[name].w
        target = device(*line_chip(me, LAST[name], j), me.k)
        size = tile_bytes(name, 1)
        arrived(size, (name, B1), t)
        for at in tile_of(name, b, t):
            remote(ref.at[at], ref.at[at], (name, B2), target, t)

    def tile_bytes(name, count):
        if name == DOWN:
            return part[name].w.at[pl.ds(0, 64 * count)]
        return part[name].w.at[pl.ds(0, 160 * count), pl.ds(0, 256)]

    def out_rows(z):
        return [rows((2 * me.k + n) * 256 + lax.rem(z, 2) * 128 + lax.div(z, 2) * 64, 64) for n in range(2)]

    def start_out():
        for n in range(2):
            at = part[OUT].w.at[out_rows(me.z)[n]]
            for stage, j in ((B1, 1 + 2 * n), (B2, 3 - 2 * n)):
                remote(at, at, (OUT, stage), device(*line_chip(me, ZA, j), me.k), n)

    def pass_out():
        for n in range(2):
            at = part[OUT].w.at[out_rows(around(me.z, 3 - 2 * n))[n]]
            arrived(part[OUT].w.at[pl.ds(0, 64)], (OUT, B1), n)
            remote(at, at, (OUT, B2), device(*line_chip(me, ZA, 1 + 2 * n), me.k), n)

    def unpack5(name):
        start = along(me, LAST[name]) * 160
        st = part[name].st[...]
        for g in range(3):
            width = 384 if g < 2 else 256
            part[name].w[rows(start, 160), g * 384 : g * 384 + width] = dot(
                s.pick5[g], st[:, 0:width]
            ).astype(BF)

    for back in (1, 2):

        @pl.when(me.ctx < back)
        def _():
            s.tokens[back * TOK : back * TOK + TOK, :] = jnp.zeros((TOK, D), BF)

    @pl.when(me.ctx >= 2)
    def _():
        arrived(block(s.tokens, 2), (TK, 2))

    @pl.when((me.zl == 1) & (me.ctx >= 2))
    def _():
        remote(block(s.tokens, 2), block(s.tokens, 1), (TK, 1), (me.ctx - 1, me.fsdp))

    for n in (2, 1, 0):
        arrived(part[n].w.at[pl.ds(0, 240)], (n, B1))
        for b in range(4):
            at = part[n].w.at[rows(b * 160 + me.k * 80, 80)]
            remote(at, at, (n, C), sibling)

    arrived(part[OUT].st.at[pl.ds(0, 192)], (OUT, A2))
    st = part[OUT].st[...]
    left_cols = dot(s.pick8[0], st).astype(BF)
    right_cols = dot(s.pick8[1], st[:, 0:256]).astype(BF)
    for n in range(2):
        part[OUT].w[out_rows(me.z)[n], 0:384] = left_cols[n * 64 : n * 64 + 64, :]
        part[OUT].w[out_rows(me.z)[n], 384:640] = right_cols[n * 64 : n * 64 + 64, :]
    start_out()
    arrived(part[GATE].st.at[pl.ds(0, 384)], (GATE, A2))
    unpack5(GATE)
    start_tiles(GATE)
    arrived(part[UP].st.at[pl.ds(0, 384)], (UP, A2))
    unpack5(UP)
    start_tiles(UP)
    arrived(part[DOWN].w.at[pl.ds(0, 192)], (DOWN, A2))
    start_tiles(DOWN)

    s.xnz[2 * TOK :, :] = dot(first_norm(s.tokens[2 * TOK :, :]), s.orders[1]).astype(BF)

    boundary = starts[0]
    qi = lax.broadcasted_iota(jnp.int32, (TOK, TOK), 0)
    kj = lax.broadcasted_iota(jnp.int32, (TOK, TOK), 1)
    query_place = me.ctx * TOK + qi
    query_doc = (query_place >= boundary).astype(jnp.int32)
    for back in range(3):
        key_place = (me.ctx - back) * TOK + kj
        gap = query_place - key_place
        key_doc = (key_place >= boundary).astype(jnp.int32)
        allowed = (gap >= 0) & (gap < WINDOW) & (key_place >= 0) & (query_doc == key_doc)
        s.bias[:, back * TOK : back * TOK + TOK] = jnp.where(allowed, 0.0, masked_score)

    kv = s.kv
    cos = s.rope[0, 0]
    sin = s.rope[0, 1]
    for n in (1, 0):
        arrived(part[n].w.at[pl.ds(0, 320)], (n, C))
        field = dot(s.xn[n], part[n].w[...])
        for i in range(2):
            h = 2 * n + i
            s.qs[h * TOK : h * TOK + TOK, :] = (
                rotate(field[:, i * HEAD : i * HEAD + HEAD], cos, sin) * HEAD**-0.5
            ).astype(BF)

    def keys_values(back):
        at = slice(back * TOK, back * TOK + TOK)
        field = dot(s.xnz[at, :], part[2].w[...])
        kv[at, 0:HEAD] = rotate(field[:, 0:HEAD], s.rope[back, 0], s.rope[back, 1]).astype(BF)
        kv[at, HEAD:] = field[:, HEAD:].astype(BF)

    arrived(part[2].w.at[pl.ds(0, 320)], (2, C))
    keys_values(0)
    keys_values(2)

    @pl.when(me.ctx >= 1)
    def _():
        arrived(block(s.tokens, 1), (TK, 1))

    s.xnz[TOK : 2 * TOK, :] = dot(first_norm(s.tokens[TOK : 2 * TOK, :]), s.orders[1]).astype(BF)
    keys_values(1)

    def head_forward(h):
        hs = slice(h * TOK, h * TOK + TOK)
        scores = dot_nt(s.qs[hs, :], kv[:, 0:HEAD]) + s.bias[...]
        top = jnp.max(scores, axis=1, keepdims=True)
        e = jnp.exp(scores - top)
        p = (e * (1.0 / jnp.sum(e, axis=1, keepdims=True))).astype(BF)
        s.probs[hs, :] = p
        s.mixed[:, hs] = dot(p, kv[:, HEAD:]).astype(BF)

    pass_out()
    for h in range(HEADS):
        if h >= 2:
            for name in (GATE, UP, DOWN):
                pass_tile(name, h - 2)
        if h == 2:
            for n in range(2):
                arrived(part[OUT].w.at[pl.ds(0, 128)], (OUT, B2), n)
            half = part[OUT].w.at[rows(me.k * 512, 512)]
            remote(half, half, (OUT, C), sibling)
        head_forward(h)

    x = s.tokens[0:TOK, :].astype(F32)
    arrived(part[OUT].w.at[pl.ds(0, 512)], (OUT, C))
    x1 = x + dot(s.mixed[...], part[OUT].w[...])
    s.x1[...] = x1
    r1 = lax.rsqrt(jnp.mean(x1 * x1, axis=1, keepdims=True) + eps_norm)
    s.x2[0:TOK, :] = (x1 * r1).astype(BF)
    remote(block(s.x2, 0), block(s.x2, 1), X2, sibling)
    for t in (2, 3):
        for name in (GATE, UP, DOWN):
            pass_tile(name, t)
    arrived(block(s.dy2, 1), DY)
    s.x2z[0:TOK, :] = dot(s.x2[0:TOK, :], s.orders[1]).astype(BF)
    arrived(block(s.x2, 1), X2)
    s.x2z[TOK:, :] = dot(s.x2[TOK:, :], s.orders[1]).astype(BF)

    root = 0.7978845608028654

    def sum_at(name, t):
        if name == DOWN:
            return [rows(t * 64 + zh * 32, 32) for zh in range(2)]
        return [(pl.ds(0, 160), columns(t))]

    def start_sums(name, t):
        j = tile_step(t)
        b = along(me, LAST[name])
        size = 160 if name != DOWN else 256
        for stage, step, source, dst in (
            (E1, j, around(b, 2), part[name].rf),
            (E2, 4 - j, around(b, 4 - j), part[name].r1.at[pl.ds(0, size)]),
        ):
            target = device(*line_chip(me, LAST[name], step), me.k)
            for at, to in zip(tile_of(name, source, t), sum_at(name, t)):
                remote(part[name].g.at[at], dst.at[to], (name, stage), target, t)

    def pass_sums(name, t):
        j = tile_step(t)
        source = around(along(me, LAST[name]), j)
        size = 160 if name != DOWN else 256
        target = device(*line_chip(me, LAST[name], j), me.k)
        arrived(tile_bytes(name, 1), (name, E1), t)
        for at, to in zip(tile_of(name, source, t), sum_at(name, t)):
            part[name].sf[to] = (
                part[name].g[at].astype(F32) + part[name].rf[to].astype(F32)
            ).astype(BF)
            remote(
                part[name].sf.at[to],
                part[name].r1.at[pl.ds(size, size)].at[to],
                (name, E2),
                target,
                t,
            )

    def hidden_step(t, carry):
        for name in (GATE, UP, DOWN):
            arrived(tile_bytes(name, 2), (name, B2), t)
        ts = columns(t)
        w_g, w_u, w_d = part[GATE].w, part[UP].w, part[DOWN].w
        gate = dot(s.x2[...], w_g[:, ts])
        up = dot(s.x2z[...], w_u[:, ts])
        d_hidden = dot_nt(s.dy2[...], w_d[ts, :])
        square = gate * gate
        th = jnp.tanh(root * gate * (1.0 + 0.044715 * square))
        half = 0.5 * (1.0 + th)
        act = gate * half
        slope = half + 0.5 * gate * (1.0 - th * th) * (root * (1.0 + 0.134145 * square))
        hidden = (act * up).astype(BF)
        d_gate = (d_hidden * up * slope).astype(BF)
        d_up = (d_hidden * act).astype(BF)
        part[DOWN].g[ts, :] = dot_tn(hidden, s.dy2[...]).astype(BF)
        part[GATE].g[:, ts] = dot_tn(s.x2[...], d_gate).astype(BF)
        part[UP].g[:, ts] = dot_tn(s.x2z[...], d_up).astype(BF)
        for name in (GATE, UP, DOWN):
            start_sums(name, t)
        s.hidden[:, ts] = hidden
        s.d_gate[:, ts] = d_gate
        s.d_up[:, ts] = d_up
        return carry

    lax.fori_loop(0, 4, hidden_step, 0)

    def from_hidden(at):
        far = dot_nt(s.d_up[at, :], part[UP].w[...]).astype(BF)
        return dot_nt(s.d_gate[at, :], part[GATE].w[...]) + dot_nt(far, s.orders[1])

    s.esend[...] = from_hidden(slice(TOK, 2 * TOK)).astype(BF)
    remote(s.esend, s.erecv, EE, sibling)
    for t in (0, 1):
        for name in (GATE, UP, DOWN):
            pass_sums(name, t)
    e1 = from_hidden(slice(0, TOK))
    for t in (2, 3):
        for name in (GATE, UP, DOWN):
            pass_sums(name, t)
    s.osend[...] = dot(s.hidden[TOK:, :], part[DOWN].w[...]).astype(BF)
    remote(s.osend, s.orecv, OO, sibling)
    s.outp[...] = s.x1[...] + dot(s.hidden[0:TOK, :], part[DOWN].w[...])
    arrived(s.erecv, EE)
    e1 = e1 + s.erecv[...].astype(F32)
    x1 = s.x1[...]
    r1 = lax.rsqrt(jnp.mean(x1 * x1, axis=1, keepdims=True) + eps_norm)
    dx1 = (
        s.cin[...].astype(F32)
        + r1 * e1
        - x1 * (r1 * r1 * r1 * jnp.mean(x1 * e1, axis=1, keepdims=True))
    )
    s.dx1[...] = dx1
    da = dx1.astype(BF)

    def head_out(h, carry):
        hs = pl.ds(pl.multiple_of(h * TOK, TOK), TOK)
        part[OUT].g[hs, :] = dot_tn(s.mixed[:, hs], da).astype(BF)
        return carry

    lax.fori_loop(0, HEADS, head_out, 0)
    remote(part[OUT].g.at[rows((1 - me.k) * 512, 512)], part[OUT].r0, (OUT, D1), sibling)

    def head_backward(h, carry):
        hs = pl.ds(pl.multiple_of(h * TOK, TOK), TOK)
        dmix = dot_nt(da, part[OUT].w[hs, :]).astype(BF)
        s.dmix[hs, :] = dmix
        d_probs = dot_nt(dmix, kv[:, HEAD:])
        p = s.probs[hs, :].astype(F32)
        center = jnp.sum(p * d_probs, axis=1, keepdims=True)
        s.ds[hs, :] = (p * (d_probs - center)).astype(BF)
        return carry

    lax.fori_loop(0, HEADS, head_backward, 0)

    def to_blocks(n, starts_of, size):
        for j in (1, 3, 2):
            b = around(along(me, LAST[n]), j)
            for i, start in enumerate(starts_of(b)):
                remote(
                    part[n].gs.at[rows(start, size)],
                    part[n].r1.at[pl.ds(((j - 1) * len(starts_of(b)) + i) * size, size)],
                    (n, E1),
                    device(*line_chip(me, LAST[n], j), me.k),
                )

    def qkv_rows(b):
        return [b * 80]

    def out_half_rows(b):
        return [n * 256 + lax.rem(b, 2) * 128 + lax.div(b, 2) * 64 for n in range(2)]

    arrived(part[OUT].r0, (OUT, D1))
    part[OUT].gs[...] = (
        part[OUT].g[rows(me.k * 512, 512), :].astype(F32) + part[OUT].r0[...].astype(F32)
    ).astype(BF)
    to_blocks(OUT, out_half_rows, 64)

    def scatter(n, axis, starts_of, size):
        for j in (1, 3, 2):
            chip = line_chip(me, axis, j)
            starts_ = starts_of(*chip)
            for i, start in enumerate(starts_):
                remote(
                    part[n].gp.at[rows(start, size)],
                    part[n].ra.at[pl.ds(((j - 1) * len(starts_) + i) * size, size)],
                    (n, F1),
                    device(*chip, me.k),
                )

    def gathered(n, starts_of, size):
        starts_ = starts_of(me.x, me.y, me.z)
        total = size * len(starts_)
        arrived(part[n].ra, (n, F1))
        for i, start in enumerate(starts_):
            rows_here = part[n].gp[rows(start, size), :].astype(F32)
            for j in range(3):
                at = j * total + i * size
                rows_here = rows_here + part[n].ra[at : at + size, :].astype(F32)
            part[n].ga[i * size : i * size + size, :] = rows_here.astype(BF)

    def q0_rows(x, y, z):
        return [(n * 4 + y) * 32 for n in range(2)]

    def q1_rows(x, y, z):
        return [x * 64]

    def q2_rows(x, y, z):
        return [y * 64]

    def gate_rows(x, y, z):
        return [(n * 4 + y) * 32 for n in range(4)]

    def up_rows(x, y, z):
        return [n * 256 + y * 64 for n in range(2)]

    plane_of = {
        0: (YA, q0_rows, 32),
        1: (XA, q1_rows, 64),
        2: (YA, q2_rows, 64),
        OUT: (YA, q0_rows, 32),
        GATE: (YA, gate_rows, 32),
        UP: (YA, up_rows, 64),
        DOWN: (XA, q1_rows, 64),
    }

    for name in (GATE, UP, DOWN):
        for t in range(4):
            arrived(tile_bytes(name, 2), (name, E2), t)
        r1 = part[name].r1
        if name == DOWN:
            for n in range(8):
                at = slice(n * 32, n * 32 + 32)
                part[DOWN].gp[at, :] = (
                    part[DOWN].g[rows(n * 128 + me.y * 32, 32), :].astype(F32)
                    + r1[at, :].astype(F32)
                    + r1[256 + n * 32 : 256 + n * 32 + 32, :].astype(F32)
                ).astype(BF)
        else:
            total = (
                part[name].g[rows(along(me, LAST[name]) * 160, 160), :].astype(F32)
                + r1[0:160, :].astype(F32)
                + r1[160:320, :].astype(F32)
            ).astype(BF)
            part[name].gp[:, 0:256] = (
                dot_tn(s.pick5[0], total[:, 0:256])
                + dot_tn(s.pick5[1], total[:, 384:640])
                + dot_tn(s.pick5[2], total[:, 768:1024])
            ).astype(BF)
            part[name].gp[:, 256:384] = (
                dot_tn(s.pick5[0], total[:, 256:384]) + dot_tn(s.pick5[1], total[:, 640:768])
            ).astype(BF)
        scatter(name, *plane_of[name])

    for back in (2, 1, 0):
        at = slice(back * TOK, back * TOK + TOK)
        dk = dot_tn(s.ds[:, at], s.qs[...])
        s.dkv[at, 0:HEAD] = rotate(dk, s.rope[back, 0], -s.rope[back, 1]).astype(BF)
        s.dkv[at, HEAD:] = dot_tn(s.probs[:, at], s.dmix[...]).astype(BF)

    def swap_halves(n):
        for b in range(4):
            remote(
                part[n].g.at[rows(b * 160 + (1 - me.k) * 80, 80)],
                part[n].r0.at[pl.ds(b * 80, 80)],
                (n, D1),
                sibling,
            )

    part[2].g[...] = dot_tn(s.xnz[...], s.dkv[...]).astype(BF)
    swap_halves(2)

    def head_query(h, carry):
        hs = pl.ds(pl.multiple_of(h * TOK, TOK), TOK)
        dq = dot(s.ds[hs, :], kv[:, 0:HEAD]) * HEAD**-0.5
        s.dq[:, hs] = rotate(dq, cos, -sin).astype(BF)
        return carry

    lax.fori_loop(0, HEADS, head_query, 0)
    for n in (1, 0):
        part[n].g[...] = dot_tn(s.xn[n], s.dq[:, n * 512 : n * 512 + 512]).astype(BF)
        swap_halves(n)

    for n in (2, 1, 0):
        arrived(part[n].r0, (n, D1))
        for b in range(4):
            at = slice(b * 80, b * 80 + 80)
            part[n].gs[at, :] = (
                part[n].g[rows(b * 160 + me.k * 80, 80), :].astype(F32)
                + part[n].r0[at, :].astype(F32)
            ).astype(BF)
        to_blocks(n, qkv_rows, 80)
    @pl.when((me.zl == 0) & (me.ctx >= 2))
    def _():
        remote(block(s.dkv, 1), block(s.dkvr, 0), (DKV, 0), (me.ctx + 1, me.fsdp))
        remote(block(s.dkv, 2), block(s.dkvr, 2), (DKV, 2), (me.ctx - 2, me.fsdp))

    @pl.when(me.zl == 1)
    def _():
        remote(block(s.dkv, 1), block(s.dkvr, 1), (DKV, 1), (me.ctx - 1, me.fsdp))

    def owners_same(n, axis):
        home = part[n].rb.at[rows(along(me, axis) * 16, 16)]
        own_copy(part[n].ga.at[rows(along(me, axis) * 16, 16)], home, (n, F2))
        for j in (1, 3, 2):
            chip = line_chip(me, axis, j)
            remote(
                part[n].ga.at[rows(chip[axis] * 16, 16)],
                home,
                (n, F2),
                device(*chip, me.k),
            )

    def owners_low(n, axis):
        home = part[n].rb.at[rows(along(me, axis) * 16, 16)]
        for i in range(2):
            for core in range(2):
                if axis == ZA:
                    chip = (me.x, me.y, 2 * i + me.k)
                    here = chip[2] == me.z
                else:
                    chip = (2 * me.k + i, me.y, me.z)
                    here = chip[0] == me.x
                src = part[n].ga.at[pl.ds((i * 2 + core) * 16, 16)]
                mine = here & (me.k == core)

                @pl.when(mine)
                def _():
                    own_copy(src, home, (n, F2))

                @pl.when(jnp.logical_not(mine))
                def _():
                    remote(src, home, (n, F2), device(*chip, core))

    def owners_both(n, axis, slot_of):
        home = part[n].rb.at[rows((me.k * 4 + along(me, axis)) * 16, 16)]
        for j in (0, 1, 3, 2):
            chip = line_chip(me, axis, j)
            for flip in range(2):
                core = lax.rem(me.k + flip, 2)
                src = part[n].ga.at[rows(slot_of(chip[axis], core) * 16, 16)]
                if j == 0 and flip == 0:
                    own_copy(src, home, (n, F2))
                else:
                    remote(src, home, (n, F2), device(*chip, core))

    def spread_owners(n):
        gathered(n, *plane_of[n][1:])
        if n == 1:
            owners_same(1, ZA)
        elif n == 2:
            owners_same(2, XA)
        elif n == GATE:
            owners_both(n, ZA, lambda z, core: (lax.rem(z, 2) * 2 + lax.div(z, 2)) * 2 + core)
        elif n == UP:
            owners_both(n, XA, lambda place, core: core * 4 + place)
        else:
            owners_low(n, XA if n == OUT else ZA)

    for n in (2, 1, 0):
        arrived(part[n].r1, (n, E1))
        total = part[n].gs[rows(along(me, LAST[n]) * 80, 80), :].astype(F32)
        for j in range(3):
            total = total + part[n].r1[j * 80 : j * 80 + 80, :].astype(F32)
        total = total.astype(BF)
        part[n].gp[...] = (
            dot_tn(s.pick5[0, 0:80, 0:256], total[:, 0:256])
            + dot_tn(s.pick5[1, 0:80, 0:256], total[:, 256:512])
        ).astype(BF)
        scatter(n, *plane_of[n])

    arrived(part[OUT].r1, (OUT, E1))
    halves = []
    for i, start in enumerate(out_half_rows(me.z)):
        total = part[OUT].gs[rows(start, 64), :].astype(F32)
        for j in range(3):
            at = (j * 2 + i) * 64
            total = total + part[OUT].r1[at : at + 64, :].astype(F32)
        halves.append(total.astype(BF))
    total = jnp.concatenate(halves, axis=0)
    part[OUT].gp[:, 0:256] = (
        dot_tn(s.pick8[0], total[:, 0:256]) + dot_tn(s.pick8[1], total[:, 384:640])
    ).astype(BF)
    part[OUT].gp[:, 256:384] = dot_tn(s.pick8[0], total[:, 256:384]).astype(BF)
    scatter(OUT, *plane_of[OUT])

    for name in (GATE, UP, DOWN):
        spread_owners(name)

    @pl.when((me.zl == 1) & (me.ctx >= 2))
    def _():
        arrived(block(s.dkvr, 0), (DKV, 0))
        s.dkvs[...] = (s.dkv[2 * TOK :, :].astype(F32) + s.dkvr[0:TOK, :].astype(F32)).astype(BF)
        remote(s.dkvs, block(s.dkvr, 2), (DKV, 2), (me.ctx - 2, me.fsdp))

    e0 = dot_nt(s.dq[:, 0:512], part[0].w[...])
    field = dot_nt(s.dq[:, 512:1024], part[1].w[...])
    e0 = e0 + dot_nt(field.astype(BF), s.orders[0])
    s.e0[...] = e0
    arrived(s.orecv, OO)
    lo[...] = s.outp[...] + s.orecv[...].astype(F32)

    for n in (2, 1, 0, OUT):
        spread_owners(n)

    @pl.when(me.ctx < 6)
    def _():
        arrived(block(s.dkvr, 2), (DKV, 2))

    @pl.when(me.ctx >= 6)
    def _():
        s.dkvr[2 * TOK :, :] = jnp.zeros((TOK, 2 * HEAD), BF)

    @pl.when(me.zl == 0)
    def _():
        arrived(block(s.dkvr, 1), (DKV, 1))

    @pl.when(me.zl == 1)
    def _():
        s.dkvr[TOK : 2 * TOK, :] = jnp.zeros((TOK, 2 * HEAD), BF)

    dkv = (
        s.dkv[0:TOK, :].astype(F32)
        + s.dkvr[TOK : 2 * TOK, :].astype(F32)
        + s.dkvr[2 * TOK :, :].astype(F32)
    ).astype(BF)
    field = dot_nt(dkv, part[2].w[...])
    e0 = s.e0[...] + dot_nt(field.astype(BF), s.orders[1])
    x = s.tokens[0:TOK, :].astype(F32)
    r0 = lax.rsqrt(jnp.mean(x * x, axis=1, keepdims=True) + eps_norm)
    ig[...] = s.dx1[...] + r0 * e0 - x * (r0 * r0 * r0 * jnp.mean(x * e0, axis=1, keepdims=True))

    def line_total(n, out, first):
        base = first * 4
        total = part[n].rb[base : base + 16, :].astype(F32)
        for p in range(1, 4):
            total = total + part[n].rb[base + p * 16 : base + p * 16 + 16, :].astype(F32)
        out[first : first + 16, :] = total

    for n, out in ((GATE, sg), (UP, su), (DOWN, sd), (2, sq2), (1, sq1), (0, sq0), (OUT, so)):
        arrived(part[n].rb, (n, F2))
        line_total(n, out, 0)
        if n in (GATE, UP):
            line_total(n, out, 16)

    def left_or(condition, ref, name, low, high):
        @pl.when(condition)
        def _():
            left(ref.at[pl.ds(0, low)], name)

        @pl.when(jnp.logical_not(condition))
        def _():
            left(ref.at[pl.ds(0, high)], name)

    for n in range(7):
        p = part[n]
        home = {0: me.zl, OUT: xh, DOWN: me.zl}
        if n in home:
            left_or(home[n] == me.k, p.gp, (n, A1), 48, 64)
            left_or(home[n] == me.k, p.gp, (n, F2), 48, 64)
        elif n in (GATE, UP):
            left(p.st.at[pl.ds(0, 7 * 16)], (n, A1))
            left(p.rb.at[pl.ds(0, 7 * 16)], (n, F2))
        else:
            left(p.st.at[pl.ds(0, 48)], (n, A1))
            left(p.rb.at[pl.ds(0, 48)], (n, F2))
        left(p.ra, (n, F1))
    for n in range(3):
        left(part[n].st.at[pl.ds(0, 192)], (n, A2))
        left(part[n].w.at[pl.ds(0, 240)], (n, B1))
        left(part[n].w.at[pl.ds(0, 320)], (n, C))
        left(part[n].r0, (n, D1))
        left(part[n].r1, (n, E1))
    left(part[OUT].st.at[pl.ds(0, 192)], (OUT, A2))
    left(part[OUT].w.at[pl.ds(0, 128)], (OUT, B1))
    left(part[OUT].w.at[pl.ds(0, 256)], (OUT, B2))
    left(part[OUT].w.at[pl.ds(0, 512)], (OUT, C))
    left(part[OUT].r0, (OUT, D1))
    left(part[OUT].r1, (OUT, E1))
    for name in (GATE, UP, DOWN):
        if name == DOWN:
            left(part[name].w.at[pl.ds(0, 192)], (name, A2))
        else:
            left(part[name].st.at[pl.ds(0, 384)], (name, A2))
        block_rows = 256 if name == DOWN else 160
        left(part[name].w.at[pl.ds(0, block_rows)], (name, B1))
        left(part[name].w.at[pl.ds(0, 2 * block_rows)], (name, B2))
        left(part[name].w.at[pl.ds(0, block_rows)], (name, E1))
        left(part[name].w.at[pl.ds(0, 2 * block_rows)], (name, E2))
    left(s.cin, DY)
    left(s.esend, EE)
    left(s.osend, OO)
    left(s.osend, X2)

    @pl.when(me.ctx < 6)
    def _():
        left(block(s.tokens, 0), (TK, 2))

    @pl.when((me.zl == 0) | (me.ctx >= 2))
    def _():
        left(block(s.tokens, 0), (TK, 1))

    @pl.when((me.zl == 0) & (me.ctx >= 2))
    def _():
        left(s.dkvs, (DKV, 0))

    @pl.when(me.ctx >= 2)
    def _():
        left(s.dkvs, (DKV, 2))

    @pl.when(me.zl == 1)
    def _():
        left(s.dkvs, (DKV, 1))

    assert taken[0] <= SEMS


def whole_step(tokens, cotangent, starts, wq, wo, wgu, wd, gains):
    orders, pick5, pick8, rope = constants()
    scratch = scratch_list()
    vmem = pl.BlockSpec(memory_space=pltpu.VMEM)
    anywhere = pl.BlockSpec(memory_space=pl.ANY)
    smem = pl.BlockSpec(memory_space=pltpu.SMEM)
    shapes = [(TOK, D), (TOK, D)] + [(16, 256)] * 3 + [(16, 384), (32, 384), (32, 384), (16, 640)]
    return pl.pallas_call(
        functools.partial(step_kernel, scratch),
        name="whole_step",
        out_shape=[jax.ShapeDtypeStruct(shape, F32) for shape in shapes],
        in_specs=[anywhere, anywhere, smem] + [vmem] * 5 + [anywhere] * 4,
        out_specs=[vmem] * len(shapes),
        scratch_shapes=leaves(scratch)
        + [
            pltpu.SemaphoreType.DMA((12,)),
            pltpu.SemaphoreType.DMA((SEMS,)),
            pltpu.SemaphoreType.DMA((SEMS,)),
        ],
        compiler_params=pltpu.CompilerParams(
            collective_id=0, has_side_effects=True, vmem_limit_bytes=62 * 2**20
        ),
        cost_estimate=pl.CostEstimate(
            flops=12_000_000_000, bytes_accessed=8_000_000, transcendentals=2_000_000
        ),
    )(tokens, cotangent, starts, wq, wo, wgu, wd, gains, orders, pick5, pick8, rope)


def adamw(master, first, second, gradient, rate, decay):
    first_next = beta_one * first + (1.0 - beta_one) * gradient
    second_next = beta_two * second + (1.0 - beta_two) * gradient * gradient
    first_fixed = first_next * (1.0 / (1.0 - beta_one**STEP))
    second_fixed = second_next * (1.0 / (1.0 - beta_two**STEP))
    update = first_fixed / (jnp.sqrt(second_fixed) + eps_adam) + decay * master
    return master - rate * update, first_next, second_next


def update_kernel(*refs):
    inner = refs[41:65]
    sem = refs[65]
    copies = [
        pltpu.make_async_copy(src, dst, sem.at[n])
        for n, (src, dst) in enumerate(zip(refs[:24], inner))
    ]
    for one in copies:
        one.start()
    (sq0, sq1, sq2, so, sg, su, sd) = inner[2:9]
    (wq, qf, qs, wo, of, os_, wgu, gf, gs, wd, df, ds_, gains, nf, ns) = inner[9:]
    (oq, oqf, oqs, oo, oof, oos, og, ogf, ogs, od, odf, ods, on, onf, ons) = refs[26:41]
    for one in copies:
        one.wait()
    through = [
        pltpu.make_async_copy(inner[n], refs[24 + n].at[0], sem.at[24 + n]) for n in range(2)
    ]
    for one in through:
        one.start()

    rate = 1.5 * D**-0.5
    gain0 = column(gains[0:1, :])
    gain1 = column(gains[1:2, :])
    total0 = jnp.zeros((5, 1), F32)
    for n, share in enumerate((sq0, sq1, sq2)):
        for g in range(2):
            at = slice(n * 512 + g * 256, n * 512 + g * 256 + 256)
            raw = share[5 * g : 5 * g + 5, :]
            w = wq[:, at]
            total0 = total0 + jnp.sum(w.astype(BF).astype(F32) * raw, axis=1, keepdims=True)
            oq[:, at], oqf[:, at], oqs[:, at] = adamw(
                w, qf[:, at], qs[:, at], raw * gain0, rate, weight_decay
            )
    total1 = jnp.zeros((5, 1), F32)
    for n, share in enumerate((sg, su)):
        for c in range(2):
            for t in range(8):
                g, i = t // 3, t % 3
                base = n * FF + (t // 2) * 512 + c * 256 + (t % 2) * 128
                at = slice(base, base + 128)
                raw = share[c * 16 + 5 * g : c * 16 + 5 * g + 5, i * 128 : i * 128 + 128]
                w = wgu[:, at]
                total1 = total1 + jnp.sum(w.astype(BF).astype(F32) * raw, axis=1, keepdims=True)
                og[:, at], ogf[:, at], ogs[:, at] = adamw(
                    w, gf[:, at], gs[:, at], raw * gain1, rate, weight_decay
                )
    rate = 1.5 * OUT_FAN**-0.5
    for r, at in ((0, slice(0, 384)), (8, slice(384, 640))):
        raw = so[r : r + 8, 0 : at.stop - at.start]
        oo[:, at], oof[:, at], oos[:, at] = adamw(
            wo[:, at], of[:, at], os_[:, at], raw, rate, weight_decay
        )
    od[...], odf[...], ods[...] = adamw(
        wd[...], df[...], ds_[...], sd[...], 1.5 * FF**-0.5, weight_decay
    )
    i = lax.broadcasted_iota(jnp.int32, (5, 5), 0)
    j = lax.broadcasted_iota(jnp.int32, (5, 5), 1)
    for row, total in ((0, total0), (1, total1)):
        flat = jnp.sum(jnp.where(i == j, jnp.broadcast_to(total, (5, 5)), 0.0), axis=0, keepdims=True)
        at = slice(row, row + 1)
        on[at, :], onf[at, :], ons[at, :] = adamw(gains[at, :], nf[at, :], ns[at, :], flat, 0.5, 0.0)
    for one in through:
        one.wait()


def update(*arrays):
    vmem = pl.BlockSpec(memory_space=pltpu.VMEM)
    anywhere = pl.BlockSpec(memory_space=pl.ANY)
    outs = [jax.ShapeDtypeStruct((1, TOK, D), F32)] * 2 + [
        jax.ShapeDtypeStruct(a.shape, F32) for a in arrays[9:]
    ]
    return pl.pallas_call(
        update_kernel,
        name="update",
        out_shape=outs,
        in_specs=[anywhere] * len(arrays),
        out_specs=[anywhere] * 2 + [vmem] * (len(outs) - 2),
        scratch_shapes=[pltpu.VMEM(a.shape, F32) for a in arrays]
        + [pltpu.SemaphoreType.DMA((len(arrays) + 2,))],
        compiler_params=pltpu.CompilerParams(vmem_limit_bytes=60 * 2**20),
    )(*arrays)


def body(
    tokens,
    cotangent,
    starts,
    qkv_weight,
    qkv_first,
    qkv_second,
    out_weight,
    out_first,
    out_second,
    gate_up_weight,
    gate_up_first,
    gate_up_second,
    down_weight,
    down_first,
    down_second,
    norm_gains,
    gains_first,
    gains_second,
):
    results = whole_step(
        tokens, cotangent, starts, qkv_weight, out_weight, gate_up_weight, down_weight, norm_gains
    )
    return tuple(
        update(
            *results,
            qkv_weight,
            qkv_first,
            qkv_second,
            out_weight,
            out_first,
            out_second,
            gate_up_weight,
            gate_up_first,
            gate_up_second,
            down_weight,
            down_first,
            down_second,
            norm_gains,
            gains_first,
            gains_second,
        )
    )


def solution(mesh):
    act = P("fsdp", "ctx", None)
    row = P(("ctx", "fsdp"), None)
    gain = P(None, ("ctx", "fsdp"))
    return jax.shard_map(
        body,
        mesh=mesh,
        in_specs=(act, act, P("fsdp")) + (row,) * 12 + (gain,) * 3,
        out_specs=(act, act) + (row,) * 12 + (gain,) * 3,
        check_vma=False,
    )
```

```python
import functools

import jax
import jax.numpy as jnp
import numpy as np
from jax import lax
from jax.experimental import pallas as pl
from jax.experimental.pallas import tpu as pltpu
from jax.sharding import PartitionSpec as P

D = 640
HEADS = 4
HEAD = 256
FF = 2048
WINDOW = 512
STEP = 10
QW = 1024
OUT_FAN = 8
TOK = 256
LENGTH = 2048

eps_norm = 1e-06
beta_one = 0.9
beta_two = 0.95
eps_adam = 1e-08
weight_decay = 0.1
masked_score = -1e30

MESH = pl.DeviceIdType.MESH
BF = jnp.bfloat16
F32 = jnp.float32


class Place:
    def __init__(self):
        self.ctx = lax.axis_index("ctx")
        self.fsdp = lax.axis_index("fsdp")
        self.x = lax.div(self.ctx, 2)
        self.zl = lax.rem(self.ctx, 2)
        self.zh = lax.div(self.fsdp, 8)
        self.y = lax.div(lax.rem(self.fsdp, 8), 2)
        self.k = lax.rem(self.fsdp, 2)
        self.z = 2 * self.zh + self.zl


def device(x, y, z, k):
    return (2 * x + lax.rem(z, 2), 8 * lax.div(z, 2) + 2 * y + k)


def around(a, b):
    return lax.rem(a + b, 4)


def plane_chip(me, last, j):
    a, b = lax.rem(j, 4), lax.div(j, 4)
    if last == XA:
        return me.x, around(me.y, a), around(me.z, b)
    if last == YA:
        return around(me.x, a), me.y, around(me.z, b)
    return around(me.x, a), around(me.y, b), me.z


def line_chip(me, last, j):
    if last == XA:
        return around(me.x, j), me.y, me.z
    if last == YA:
        return me.x, around(me.y, j), me.z
    return me.x, me.y, around(me.z, j)


def along(me, last):
    return (me.x, me.y, me.z)[last]


def in_plane(last, x, y, z):
    if last == XA:
        return lax.rem(z, 2) * 8 + lax.div(z, 2) * 4 + y
    if last == YA:
        return 4 * x + z
    return 4 * x + y


def rows(start, size):
    return pl.ds(pl.multiple_of(start, 16), size)


def feature_order(last):
    order = np.zeros(D, np.int64)
    for x in range(4):
        for y in range(4):
            for z in range(4):
                for k in range(2):
                    dev = x * 32 + (z % 2) * 16 + (z // 2) * 8 + y * 2 + k
                    b, p = (y, 4 * x + z) if last == YA else (z, 4 * y + x)
                    for r in range(5):
                        order[b * 160 + k * 80 + p * 5 + r] = 5 * dev + r
    return order


def constants():
    orders = np.zeros((2, D, D), np.float32)
    for n, last in enumerate((YA, ZA)):
        orders[n, feature_order(last), np.arange(D)] = 1.0
    pick5 = np.zeros((3, 160, 512), np.float32)
    for g in range(3):
        for s in range(32):
            for r in range(5):
                pick5[g, s * 5 + r, s * 16 + g * 5 + r] = 1.0
    pick8 = np.zeros((2, 128, 256), np.float32)
    for g in range(2):
        for s in range(16):
            for r in range(8):
                pick8[g, s * 8 + r, s * 16 + g * 8 + r] = 1.0
    half = HEAD // 2
    frequency = np.float32(10000.0) ** (
        -(np.float32(2.0) * np.arange(half, dtype=np.float32)) / np.float32(HEAD)
    )
    angles = np.arange(LENGTH, dtype=np.float32)[:, None] * frequency.astype(np.float32)[None, :]
    rope = np.stack([np.cos(angles.astype(np.float64)), np.sin(angles.astype(np.float64))])
    return (
        jnp.asarray(orders, BF),
        jnp.asarray(pick5, BF),
        jnp.asarray(pick8, BF),
        jnp.asarray(rope.astype(np.float32)),
    )


def dot(a, b):
    return lax.dot_general(a, b, (((1,), (0,)), ((), ())), preferred_element_type=F32)


def dot_nt(a, b):
    return lax.dot_general(a, b, (((1,), (1,)), ((), ())), preferred_element_type=F32)


def dot_tn(a, b):
    return lax.dot_general(a, b, (((0,), (0,)), ((), ())), preferred_element_type=F32)


def rotate(u, cos, sin):
    a, b = u[:, :128], u[:, 128:]
    return jnp.concatenate([a * cos - b * sin, b * cos + a * sin], axis=1)


def column(row):
    n = row.shape[1]
    i = lax.broadcasted_iota(jnp.int32, (n, n), 0)
    j = lax.broadcasted_iota(jnp.int32, (n, n), 1)
    wide = jnp.broadcast_to(row.astype(BF).astype(F32), (n, n))
    return jnp.sum(jnp.where(i == j, wide, 0.0), axis=1, keepdims=True)


class Bag(dict):
    __getattr__ = dict.__getitem__


def scratch_list():
    def v(*shape, kind=BF):
        return pltpu.VMEM(shape, kind)

    qkv = [
        Bag(
            pk=v(16, 256),
            st=v(256, 256),
            w=v(640, 512),
            g=v(640, 512),
            r0=v(320, 512),
            gs=v(320, 512),
            r1=v(240, 512),
            gp=v(256, 256),
            ra=v(192, 256),
            ga=v(64, 256),
            rb=v(64, 256),
        )
        for n in range(3)
    ]
    out = Bag(
        pk=v(16, 384),
        st=v(256, 384),
        w=v(1024, 640),
        g=v(1024, 640),
        r0=v(512, 640),
        gs=v(512, 640),
        r1=v(384, 640),
        gp=v(256, 384),
        ra=v(192, 384),
        ga=v(64, 384),
        rb=v(64, 384),
    )
    gate_up = [
        Bag(
            pk=v(32, 384),
            st=v(512, 384),
            w=v(640, 1024),
            g=v(640, 1024),
            rf=v(160, 1024),
            sf=v(160, 1024),
            r1=v(320, 1024),
            gp=v(512, 384),
            ra=v(384, 384),
            ga=v(128, 384),
            rb=v(128, 384),
        )
        for n in range(2)
    ]
    down = Bag(
        pk=v(16, 640),
        w=v(1024, 640),
        g=v(1024, 640),
        rf=v(256, 640),
        sf=v(256, 640),
        r1=v(512, 640),
        gp=v(256, 640),
        ra=v(192, 640),
        ga=v(64, 640),
        rb=v(64, 640),
    )
    return Bag(
        part=qkv + [out] + gate_up + [down],
        tokens=v(3 * TOK, D),
        cin=v(TOK, D),
        orders=v(2, D, D),
        pick5=v(3, 160, 512),
        pick8=v(2, 128, 256),
        rope=v(3, 2, TOK, 128, kind=F32),
        pad=v(16, 384, kind=F32),
        xn=v(2, TOK, D),
        xnz=v(3 * TOK, D),
        qs=v(HEADS * TOK, HEAD),
        kv=v(3 * TOK, 2 * HEAD),
        bias=v(TOK, 3 * TOK, kind=F32),
        probs=v(HEADS * TOK, 3 * TOK),
        ds=v(HEADS * TOK, 3 * TOK),
        mixed=v(TOK, QW),
        dmix=v(HEADS * TOK, HEAD),
        x1=v(TOK, D, kind=F32),
        x2=v(2 * TOK, D),
        x2z=v(2 * TOK, D),
        dy2=v(2 * TOK, D),
        hidden=v(2 * TOK, FF // 2),
        d_gate=v(2 * TOK, FF // 2),
        d_up=v(2 * TOK, FF // 2),
        outp=v(TOK, D, kind=F32),
        e0=v(TOK, D, kind=F32),
        osend=v(TOK, D),
        orecv=v(TOK, D),
        esend=v(TOK, D),
        erecv=v(TOK, D),
        dx1=v(TOK, D, kind=F32),
        dq=v(TOK, QW),
        dkv=v(3 * TOK, 2 * HEAD),
        dkvr=v(3 * TOK, 2 * HEAD),
        dkvs=v(TOK, 2 * HEAD),
    )


def leaves(tree):
    if isinstance(tree, dict):
        return [leaf for branch in tree.values() for leaf in leaves(branch)]
    if isinstance(tree, list):
        return [leaf for branch in tree for leaf in leaves(branch)]
    return [tree]


def refill(tree, values):
    if isinstance(tree, dict):
        return Bag({key: refill(branch, values) for key, branch in tree.items()})
    if isinstance(tree, list):
        return [refill(branch, values) for branch in tree]
    return next(values)


OUT, GATE, UP, DOWN = 3, 4, 5, 6
XA, YA, ZA = range(3)
LAST = (XA, YA, ZA, ZA, XA, ZA, YA)
A1, A2, B1, B2, C, D1, E1, E2, F1, F2 = range(10)
DY, X2, EE, OO, TK, DKV = range(7, 13)
SEMS = 128


def wait_for(ref, sem):
    pltpu.make_async_copy(ref, ref, sem).wait()


def step_kernel(shape, *refs):
    (tok, cot, starts, wq, wo, wgu, wd, gains, orders_h, pick5_h, pick8_h, rope_h) = refs[:12]
    (lo, ig, sq0, sq1, sq2, so, sg, su, sd) = refs[12:21]
    s = refill(shape, iter(refs[21:-3]))
    local, sent, came = refs[-3:]
    me = Place()
    sems = {}
    taken = [0]

    def sem_of(name, size=1):
        if name not in sems:
            sems[name] = taken[0]
            taken[0] += size
        return sems[name]

    def remote(src, dst, name, target, tile=None):
        n = sem_of(name, 1 if tile is None else 4)
        pltpu.make_async_remote_copy(
            src_ref=src,
            dst_ref=dst,
            send_sem=sent.at[n],
            recv_sem=came.at[n if tile is None else n + tile],
            device_id=target,
            device_id_type=MESH,
        ).start()

    def own_copy(src, dst, name):
        pltpu.make_async_copy(src, dst, came.at[sem_of(name)]).start()

    def arrived(ref, name, tile=0):
        wait_for(ref, came.at[sem_of(name) + tile])

    def left(ref, name):
        wait_for(ref, sent.at[sem_of(name)])

    sibling = device(me.x, me.y, me.z, 1 - me.k)

    fetch = [
        (tok.at[0], s.tokens.at[pl.ds(0, TOK)]),
        (orders_h, s.orders),
        (pick5_h, s.pick5),
        (pick8_h, s.pick8),
        (cot.at[0], s.cin),
        (cot.at[0], s.dy2.at[pl.ds(0, TOK)]),
    ]
    for back in range(3):
        block = jnp.maximum(me.ctx - back, 0) * TOK
        fetch.append((rope_h.at[:, pl.ds(pl.multiple_of(block, TOK), TOK), :], s.rope.at[back]))
    fetches = [pltpu.make_async_copy(a, b, local.at[n]) for n, (a, b) in enumerate(fetch)]
    for one in fetches:
        one.start()

    barrier = pltpu.get_barrier_semaphore()
    for j in range(1, 4):
        for axis in range(3):
            for core in range(2):
                pl.semaphore_signal(
                    barrier,
                    inc=1,
                    device_id=device(*line_chip(me, axis, j), core),
                    device_id_type=MESH,
                )
    pl.semaphore_signal(barrier, inc=1, device_id=sibling, device_id_type=MESH)

    pad = s.pad
    pad[...] = jnp.zeros((16, 384), F32)
    wqb = wq[...].astype(BF).astype(F32) * column(gains[0:1, :])
    for n in range(3):
        for g in range(2):
            pad[5 * g : 5 * g + 5, 0:256] = wqb[:, n * 512 + g * 256 : n * 512 + g * 256 + 256]
        s.part[n].pk[...] = pad[:, 0:256].astype(BF)
    gain = column(gains[1:2, :])
    for n, name in enumerate((GATE, UP)):
        for c in range(2):
            for t in range(8):
                g, i = t // 3, t % 3
                base = n * FF + (t // 2) * 512 + c * 256 + (t % 2) * 128
                pad[5 * g : 5 * g + 5, i * 128 : i * 128 + 128] = (
                    wgu[:, base : base + 128].astype(BF).astype(F32) * gain
                )
            pad[10:15, 256:384] = jnp.zeros((5, 128), F32)
            s.part[name].pk[c * 16 : c * 16 + 16, :] = pad[...].astype(BF)
    pad[0:8, :] = wo[:, 0:384]
    pad[8:16, 0:256] = wo[:, 384:640]
    pad[8:16, 256:384] = jnp.zeros((8, 128), F32)
    s.part[OUT].pk[...] = pad[...].astype(BF)
    s.part[DOWN].pk[...] = wd[...].astype(BF)
    fetches[0].wait()
    pl.semaphore_wait(barrier, 19)

    def to_line(axis, src, dst, name, core):
        for j in (1, 3, 2):
            remote(src, dst, name, device(*line_chip(me, axis, j), core))

    def to_line_core(axis, src, dst, name, core):
        to_line(axis, src, dst, name, core)

        @pl.when(core == me.k)
        def _():
            own_copy(src, dst, name)

        @pl.when(core != me.k)
        def _():
            remote(src, dst, name, sibling)

    def to_line_both(axis, src, dst, name):
        for j in (1, 3, 2):
            for core in range(2):
                remote(
                    src.at[pl.ds(core * 16, 16)], dst, name, device(*line_chip(me, axis, j), core)
                )
        own_copy(src.at[rows(me.k * 16, 16)], dst, name)
        remote(src.at[rows((1 - me.k) * 16, 16)], dst, name, sibling)

    xh, xl = lax.div(me.x, 2), lax.rem(me.x, 2)
    zi = me.zl * 2 + me.zh
    part = s.part
    place = part[2].st.at[rows((4 * me.y + me.x) * 16, 16)]
    own_copy(part[2].pk, place, (2, A1))
    to_line(XA, part[2].pk, place, (2, A1), me.k)
    place = part[1].st.at[rows((4 * me.x + me.z) * 16, 16)]
    own_copy(part[1].pk, place, (1, A1))
    to_line(ZA, part[1].pk, place, (1, A1), me.k)
    low_slot = (me.zh * 4 + me.y) * 2 + me.k
    to_line_core(ZA, part[0].pk, part[0].st.at[rows(low_slot * 16, 16)], (0, A1), me.zl)

    def block(ref, back):
        return ref.at[pl.ds(back * TOK, TOK)]

    @pl.when(me.ctx < 6)
    def _():
        remote(block(s.tokens, 0), block(s.tokens, 2), (TK, 2), (me.ctx + 2, me.fsdp))

    @pl.when(me.zl == 0)
    def _():
        remote(block(s.tokens, 0), block(s.tokens, 1), (TK, 1), (me.ctx + 1, me.fsdp))

    def first_norm(rows_in):
        field = rows_in.astype(F32)
        r = lax.rsqrt(jnp.mean(field * field, axis=1, keepdims=True) + eps_norm)
        return (field * r).astype(BF)

    xn = first_norm(s.tokens[0:TOK, :])
    s.xn[0] = xn
    for n in range(1, len(fetches)):
        fetches[n].wait()
    s.xn[1] = dot(xn, s.orders[0]).astype(BF)
    s.xnz[0:TOK, :] = dot(xn, s.orders[1]).astype(BF)

    def pieces_on(axis, ref, starts_, size, name):
        for j in (1, 3, 2):
            for start in starts_:
                at = ref.at[rows(start, size)]
                remote(at, at, name, device(*line_chip(me, axis, j), me.k))

    arrived(part[2].st.at[pl.ds(0, 64)], (2, A1))
    pieces_on(YA, part[2].st, [me.y * 64], 64, (2, A2))
    arrived(part[1].st.at[pl.ds(0, 64)], (1, A1))
    pieces_on(XA, part[1].st, [me.x * 64], 64, (1, A2))
    arrived(part[0].st.at[pl.ds(0, 64)], (0, A1))
    pieces_on(YA, part[0].st, [(zh * 4 + me.y) * 32 for zh in range(2)], 32, (0, A2))
    remote(s.cin, block(s.dy2, 1), DY, sibling)
    out_slot = (xl * 4 + me.y) * 2 + me.k
    to_line_core(XA, part[OUT].pk, part[OUT].st.at[rows(out_slot * 16, 16)], (OUT, A1), xh)
    gate_slot = (zi * 4 + me.y) * 2 + me.k
    to_line_both(YA, part[GATE].pk, part[GATE].st.at[rows(gate_slot * 16, 16)], (GATE, A1))
    up_slot = me.k * 16 + me.y * 4 + me.x
    to_line_both(XA, part[UP].pk, part[UP].st.at[rows(up_slot * 16, 16)], (UP, A1))
    down_row = me.x * 256 + me.zh * 128 + me.y * 32 + me.k * 16
    to_line_core(ZA, part[DOWN].pk, part[DOWN].w.at[rows(down_row, 16)], (DOWN, A1), me.zl)

    for n in (2, 1, 0):
        arrived(part[n].st.at[pl.ds(0, 192)], (n, A2))
        start = along(me, LAST[n]) * 160 + me.k * 80
        st = part[n].st[...]
        for g in range(2):
            part[n].w[rows(start, 80), g * 256 : g * 256 + 256] = dot(
                s.pick5[g, 0:80, 0:256], st
            ).astype(BF)
        pieces_on(LAST[n], part[n].w, [start], 80, (n, B1))

    arrived(part[OUT].st.at[pl.ds(0, 64)], (OUT, A1))
    pieces_on(YA, part[OUT].st, [(n * 4 + me.y) * 32 for n in range(2)], 32, (OUT, A2))
    arrived(part[GATE].st.at[pl.ds(0, 128)], (GATE, A1))
    pieces_on(ZA, part[GATE].st, [zi * 128], 128, (GATE, A2))
    arrived(part[UP].st.at[pl.ds(0, 128)], (UP, A1))
    pieces_on(YA, part[UP].st, [n * 256 + me.y * 64 for n in range(2)], 64, (UP, A2))
    arrived(part[DOWN].w.at[pl.ds(0, 64)], (DOWN, A1))
    pieces_on(
        XA, part[DOWN].w, [me.x * 256 + n * 128 + me.y * 32 for n in range(2)], 32, (DOWN, A2)
    )

    def columns(t):
        return pl.ds(pl.multiple_of(t * 256, 256), 256)

    def tile_of(name, b, t):
        if name == DOWN:
            return [rows(t * 256 + zh * 128 + b * 32, 32) for zh in range(2)]
        return [(rows(b * 160, 160), columns(t))]

    def tile_step(t):
        return 1 + 2 * lax.rem(t, 2)

    def start_tiles(name):
        b = along(me, LAST[name])
        ref = part[name].w
        for t in range(4):
            ahead = 1 + 2 * (t % 2)
            for at in tile_of(name, b, t):
                for stage, j in ((B1, ahead), (B2, 4 - ahead)):
                    target = device(*line_chip(me, LAST[name], j), me.k)
                    remote(ref.at[at], ref.at[at], (name, stage), target, t)

    def pass_tile(name, t):
        j = tile_step(t)
        b = around(along(me, LAST[name]), 4 - j)
        ref = part[name].w
        target = device(*line_chip(me, LAST[name], j), me.k)
        size = tile_bytes(name, 1)
        arrived(size, (name, B1), t)
        for at in tile_of(name, b, t):
            remote(ref.at[at], ref.at[at], (name, B2), target, t)

    def tile_bytes(name, count):
        if name == DOWN:
            return part[name].w.at[pl.ds(0, 64 * count)]
        return part[name].w.at[pl.ds(0, 160 * count), pl.ds(0, 256)]

    def out_rows(z):
        return [rows((2 * me.k + n) * 256 + lax.rem(z, 2) * 128 + lax.div(z, 2) * 64, 64) for n in range(2)]

    def start_out():
        for n in range(2):
            at = part[OUT].w.at[out_rows(me.z)[n]]
            for stage, j in ((B1, 1 + 2 * n), (B2, 3 - 2 * n)):
                remote(at, at, (OUT, stage), device(*line_chip(me, ZA, j), me.k), n)

    def pass_out():
        for n in range(2):
            at = part[OUT].w.at[out_rows(around(me.z, 3 - 2 * n))[n]]
            arrived(part[OUT].w.at[pl.ds(0, 64)], (OUT, B1), n)
            remote(at, at, (OUT, B2), device(*line_chip(me, ZA, 1 + 2 * n), me.k), n)

    def unpack5(name):
        start = along(me, LAST[name]) * 160
        st = part[name].st[...]
        for g in range(3):
            width = 384 if g < 2 else 256
            part[name].w[rows(start, 160), g * 384 : g * 384 + width] = dot(
                s.pick5[g], st[:, 0:width]
            ).astype(BF)

    for back in (1, 2):

        @pl.when(me.ctx < back)
        def _():
            s.tokens[back * TOK : back * TOK + TOK, :] = jnp.zeros((TOK, D), BF)

    @pl.when(me.ctx >= 2)
    def _():
        arrived(block(s.tokens, 2), (TK, 2))

    @pl.when((me.zl == 1) & (me.ctx >= 2))
    def _():
        remote(block(s.tokens, 2), block(s.tokens, 1), (TK, 1), (me.ctx - 1, me.fsdp))

    for n in (2, 1, 0):
        arrived(part[n].w.at[pl.ds(0, 240)], (n, B1))
        for b in range(4):
            at = part[n].w.at[rows(b * 160 + me.k * 80, 80)]
            remote(at, at, (n, C), sibling)

    arrived(part[OUT].st.at[pl.ds(0, 192)], (OUT, A2))
    st = part[OUT].st[...]
    left_cols = dot(s.pick8[0], st).astype(BF)
    right_cols = dot(s.pick8[1], st[:, 0:256]).astype(BF)
    for n in range(2):
        part[OUT].w[out_rows(me.z)[n], 0:384] = left_cols[n * 64 : n * 64 + 64, :]
        part[OUT].w[out_rows(me.z)[n], 384:640] = right_cols[n * 64 : n * 64 + 64, :]
    start_out()
    arrived(part[GATE].st.at[pl.ds(0, 384)], (GATE, A2))
    unpack5(GATE)
    start_tiles(GATE)
    arrived(part[UP].st.at[pl.ds(0, 384)], (UP, A2))
    unpack5(UP)
    start_tiles(UP)
    arrived(part[DOWN].w.at[pl.ds(0, 192)], (DOWN, A2))
    start_tiles(DOWN)

    s.xnz[2 * TOK :, :] = dot(first_norm(s.tokens[2 * TOK :, :]), s.orders[1]).astype(BF)

    boundary = starts[0]
    qi = lax.broadcasted_iota(jnp.int32, (TOK, TOK), 0)
    kj = lax.broadcasted_iota(jnp.int32, (TOK, TOK), 1)
    query_place = me.ctx * TOK + qi
    query_doc = (query_place >= boundary).astype(jnp.int32)
    for back in range(3):
        key_place = (me.ctx - back) * TOK + kj
        gap = query_place - key_place
        key_doc = (key_place >= boundary).astype(jnp.int32)
        allowed = (gap >= 0) & (gap < WINDOW) & (key_place >= 0) & (query_doc == key_doc)
        s.bias[:, back * TOK : back * TOK + TOK] = jnp.where(allowed, 0.0, masked_score)

    kv = s.kv
    cos = s.rope[0, 0]
    sin = s.rope[0, 1]
    for n in (1, 0):
        arrived(part[n].w.at[pl.ds(0, 320)], (n, C))
        field = dot(s.xn[n], part[n].w[...])
        for i in range(2):
            h = 2 * n + i
            s.qs[h * TOK : h * TOK + TOK, :] = (
                rotate(field[:, i * HEAD : i * HEAD + HEAD], cos, sin) * HEAD**-0.5
            ).astype(BF)

    def keys_values(back):
        at = slice(back * TOK, back * TOK + TOK)
        field = dot(s.xnz[at, :], part[2].w[...])
        kv[at, 0:HEAD] = rotate(field[:, 0:HEAD], s.rope[back, 0], s.rope[back, 1]).astype(BF)
        kv[at, HEAD:] = field[:, HEAD:].astype(BF)

    arrived(part[2].w.at[pl.ds(0, 320)], (2, C))
    keys_values(0)
    keys_values(2)

    @pl.when(me.ctx >= 1)
    def _():
        arrived(block(s.tokens, 1), (TK, 1))

    s.xnz[TOK : 2 * TOK, :] = dot(first_norm(s.tokens[TOK : 2 * TOK, :]), s.orders[1]).astype(BF)
    keys_values(1)

    def head_forward(h):
        hs = slice(h * TOK, h * TOK + TOK)
        scores = dot_nt(s.qs[hs, :], kv[:, 0:HEAD]) + s.bias[...]
        top = jnp.max(scores, axis=1, keepdims=True)
        e = jnp.exp(scores - top)
        p = (e * (1.0 / jnp.sum(e, axis=1, keepdims=True))).astype(BF)
        s.probs[hs, :] = p
        s.mixed[:, hs] = dot(p, kv[:, HEAD:]).astype(BF)

    pass_out()
    for h in range(HEADS):
        if h >= 2:
            for name in (GATE, UP, DOWN):
                pass_tile(name, h - 2)
        if h == 2:
            for n in range(2):
                arrived(part[OUT].w.at[pl.ds(0, 128)], (OUT, B2), n)
            half = part[OUT].w.at[rows(me.k * 512, 512)]
            remote(half, half, (OUT, C), sibling)
        head_forward(h)

    x = s.tokens[0:TOK, :].astype(F32)
    arrived(part[OUT].w.at[pl.ds(0, 512)], (OUT, C))
    x1 = x + dot(s.mixed[...], part[OUT].w[...])
    s.x1[...] = x1
    r1 = lax.rsqrt(jnp.mean(x1 * x1, axis=1, keepdims=True) + eps_norm)
    s.x2[0:TOK, :] = (x1 * r1).astype(BF)
    remote(block(s.x2, 0), block(s.x2, 1), X2, sibling)
    for t in (2, 3):
        for name in (GATE, UP, DOWN):
            pass_tile(name, t)
    arrived(block(s.dy2, 1), DY)
    s.x2z[0:TOK, :] = dot(s.x2[0:TOK, :], s.orders[1]).astype(BF)
    arrived(block(s.x2, 1), X2)
    s.x2z[TOK:, :] = dot(s.x2[TOK:, :], s.orders[1]).astype(BF)

    root = 0.7978845608028654

    def sum_at(name, t):
        if name == DOWN:
            return [rows(t * 64 + zh * 32, 32) for zh in range(2)]
        return [(pl.ds(0, 160), columns(t))]

    def start_sums(name, t):
        j = tile_step(t)
        b = along(me, LAST[name])
        size = 160 if name != DOWN else 256
        for stage, step, source, dst in (
            (E1, j, around(b, 2), part[name].rf),
            (E2, 4 - j, around(b, 4 - j), part[name].r1.at[pl.ds(0, size)]),
        ):
            target = device(*line_chip(me, LAST[name], step), me.k)
            for at, to in zip(tile_of(name, source, t), sum_at(name, t)):
                remote(part[name].g.at[at], dst.at[to], (name, stage), target, t)

    def pass_sums(name, t):
        j = tile_step(t)
        source = around(along(me, LAST[name]), j)
        size = 160 if name != DOWN else 256
        target = device(*line_chip(me, LAST[name], j), me.k)
        arrived(tile_bytes(name, 1), (name, E1), t)
        for at, to in zip(tile_of(name, source, t), sum_at(name, t)):
            part[name].sf[to] = (
                part[name].g[at].astype(F32) + part[name].rf[to].astype(F32)
            ).astype(BF)
            remote(
                part[name].sf.at[to],
                part[name].r1.at[pl.ds(size, size)].at[to],
                (name, E2),
                target,
                t,
            )

    def hidden_step(t, carry):
        for name in (GATE, UP, DOWN):
            arrived(tile_bytes(name, 2), (name, B2), t)
        ts = columns(t)
        w_g, w_u, w_d = part[GATE].w, part[UP].w, part[DOWN].w
        gate = dot(s.x2[...], w_g[:, ts])
        up = dot(s.x2z[...], w_u[:, ts])
        d_hidden = dot_nt(s.dy2[...], w_d[ts, :])
        square = gate * gate
        th = jnp.tanh(root * gate * (1.0 + 0.044715 * square))
        half = 0.5 * (1.0 + th)
        act = gate * half
        slope = half + 0.5 * gate * (1.0 - th * th) * (root * (1.0 + 0.134145 * square))
        hidden = (act * up).astype(BF)
        d_gate = (d_hidden * up * slope).astype(BF)
        d_up = (d_hidden * act).astype(BF)
        part[DOWN].g[ts, :] = dot_tn(hidden, s.dy2[...]).astype(BF)
        part[GATE].g[:, ts] = dot_tn(s.x2[...], d_gate).astype(BF)
        part[UP].g[:, ts] = dot_tn(s.x2z[...], d_up).astype(BF)
        for name in (GATE, UP, DOWN):
            start_sums(name, t)
        s.hidden[:, ts] = hidden
        s.d_gate[:, ts] = d_gate
        s.d_up[:, ts] = d_up
        return carry

    lax.fori_loop(0, 4, hidden_step, 0)

    def from_hidden(at):
        far = dot_nt(s.d_up[at, :], part[UP].w[...]).astype(BF)
        return dot_nt(s.d_gate[at, :], part[GATE].w[...]) + dot_nt(far, s.orders[1])

    s.esend[...] = from_hidden(slice(TOK, 2 * TOK)).astype(BF)
    remote(s.esend, s.erecv, EE, sibling)
    for t in (0, 1):
        for name in (GATE, UP, DOWN):
            pass_sums(name, t)
    e1 = from_hidden(slice(0, TOK))
    for t in (2, 3):
        for name in (GATE, UP, DOWN):
            pass_sums(name, t)
    s.osend[...] = dot(s.hidden[TOK:, :], part[DOWN].w[...]).astype(BF)
    remote(s.osend, s.orecv, OO, sibling)
    s.outp[...] = s.x1[...] + dot(s.hidden[0:TOK, :], part[DOWN].w[...])
    arrived(s.erecv, EE)
    e1 = e1 + s.erecv[...].astype(F32)
    x1 = s.x1[...]
    r1 = lax.rsqrt(jnp.mean(x1 * x1, axis=1, keepdims=True) + eps_norm)
    dx1 = (
        s.cin[...].astype(F32)
        + r1 * e1
        - x1 * (r1 * r1 * r1 * jnp.mean(x1 * e1, axis=1, keepdims=True))
    )
    s.dx1[...] = dx1
    da = dx1.astype(BF)

    def head_out(h, carry):
        hs = pl.ds(pl.multiple_of(h * TOK, TOK), TOK)
        part[OUT].g[hs, :] = dot_tn(s.mixed[:, hs], da).astype(BF)
        return carry

    lax.fori_loop(0, HEADS, head_out, 0)
    remote(part[OUT].g.at[rows((1 - me.k) * 512, 512)], part[OUT].r0, (OUT, D1), sibling)

    def head_backward(h, carry):
        hs = pl.ds(pl.multiple_of(h * TOK, TOK), TOK)
        dmix = dot_nt(da, part[OUT].w[hs, :]).astype(BF)
        s.dmix[hs, :] = dmix
        d_probs = dot_nt(dmix, kv[:, HEAD:])
        p = s.probs[hs, :].astype(F32)
        center = jnp.sum(p * d_probs, axis=1, keepdims=True)
        s.ds[hs, :] = (p * (d_probs - center)).astype(BF)
        return carry

    lax.fori_loop(0, HEADS, head_backward, 0)

    def to_blocks(n, starts_of, size):
        for j in (1, 3, 2):
            b = around(along(me, LAST[n]), j)
            for i, start in enumerate(starts_of(b)):
                remote(
                    part[n].gs.at[rows(start, size)],
                    part[n].r1.at[pl.ds(((j - 1) * len(starts_of(b)) + i) * size, size)],
                    (n, E1),
                    device(*line_chip(me, LAST[n], j), me.k),
                )

    def qkv_rows(b):
        return [b * 80]

    def out_half_rows(b):
        return [n * 256 + lax.rem(b, 2) * 128 + lax.div(b, 2) * 64 for n in range(2)]

    arrived(part[OUT].r0, (OUT, D1))
    part[OUT].gs[...] = (
        part[OUT].g[rows(me.k * 512, 512), :].astype(F32) + part[OUT].r0[...].astype(F32)
    ).astype(BF)
    to_blocks(OUT, out_half_rows, 64)

    def scatter(n, axis, starts_of, size):
        for j in (1, 3, 2):
            chip = line_chip(me, axis, j)
            starts_ = starts_of(*chip)
            for i, start in enumerate(starts_):
                remote(
                    part[n].gp.at[rows(start, size)],
                    part[n].ra.at[pl.ds(((j - 1) * len(starts_) + i) * size, size)],
                    (n, F1),
                    device(*chip, me.k),
                )

    def gathered(n, starts_of, size):
        starts_ = starts_of(me.x, me.y, me.z)
        total = size * len(starts_)
        arrived(part[n].ra, (n, F1))
        for i, start in enumerate(starts_):
            rows_here = part[n].gp[rows(start, size), :].astype(F32)
            for j in range(3):
                at = j * total + i * size
                rows_here = rows_here + part[n].ra[at : at + size, :].astype(F32)
            part[n].ga[i * size : i * size + size, :] = rows_here.astype(BF)

    def q0_rows(x, y, z):
        return [(n * 4 + y) * 32 for n in range(2)]

    def q1_rows(x, y, z):
        return [x * 64]

    def q2_rows(x, y, z):
        return [y * 64]

    def gate_rows(x, y, z):
        return [(n * 4 + y) * 32 for n in range(4)]

    def up_rows(x, y, z):
        return [n * 256 + y * 64 for n in range(2)]

    plane_of = {
        0: (YA, q0_rows, 32),
        1: (XA, q1_rows, 64),
        2: (YA, q2_rows, 64),
        OUT: (YA, q0_rows, 32),
        GATE: (YA, gate_rows, 32),
        UP: (YA, up_rows, 64),
        DOWN: (XA, q1_rows, 64),
    }

    for name in (GATE, UP, DOWN):
        for t in range(4):
            arrived(tile_bytes(name, 2), (name, E2), t)
        r1 = part[name].r1
        if name == DOWN:
            for n in range(8):
                at = slice(n * 32, n * 32 + 32)
                part[DOWN].gp[at, :] = (
                    part[DOWN].g[rows(n * 128 + me.y * 32, 32), :].astype(F32)
                    + r1[at, :].astype(F32)
                    + r1[256 + n * 32 : 256 + n * 32 + 32, :].astype(F32)
                ).astype(BF)
        else:
            total = (
                part[name].g[rows(along(me, LAST[name]) * 160, 160), :].astype(F32)
                + r1[0:160, :].astype(F32)
                + r1[160:320, :].astype(F32)
            ).astype(BF)
            part[name].gp[:, 0:256] = (
                dot_tn(s.pick5[0], total[:, 0:256])
                + dot_tn(s.pick5[1], total[:, 384:640])
                + dot_tn(s.pick5[2], total[:, 768:1024])
            ).astype(BF)
            part[name].gp[:, 256:384] = (
                dot_tn(s.pick5[0], total[:, 256:384]) + dot_tn(s.pick5[1], total[:, 640:768])
            ).astype(BF)
        scatter(name, *plane_of[name])

    for back in (2, 1, 0):
        at = slice(back * TOK, back * TOK + TOK)
        dk = dot_tn(s.ds[:, at], s.qs[...])
        s.dkv[at, 0:HEAD] = rotate(dk, s.rope[back, 0], -s.rope[back, 1]).astype(BF)
        s.dkv[at, HEAD:] = dot_tn(s.probs[:, at], s.dmix[...]).astype(BF)

    def swap_halves(n):
        for b in range(4):
            remote(
                part[n].g.at[rows(b * 160 + (1 - me.k) * 80, 80)],
                part[n].r0.at[pl.ds(b * 80, 80)],
                (n, D1),
                sibling,
            )

    part[2].g[...] = dot_tn(s.xnz[...], s.dkv[...]).astype(BF)
    swap_halves(2)

    def head_query(h, carry):
        hs = pl.ds(pl.multiple_of(h * TOK, TOK), TOK)
        dq = dot(s.ds[hs, :], kv[:, 0:HEAD]) * HEAD**-0.5
        s.dq[:, hs] = rotate(dq, cos, -sin).astype(BF)
        return carry

    lax.fori_loop(0, HEADS, head_query, 0)
    for n in (1, 0):
        part[n].g[...] = dot_tn(s.xn[n], s.dq[:, n * 512 : n * 512 + 512]).astype(BF)
        swap_halves(n)

    for n in (2, 1, 0):
        arrived(part[n].r0, (n, D1))
        for b in range(4):
            at = slice(b * 80, b * 80 + 80)
            part[n].gs[at, :] = (
                part[n].g[rows(b * 160 + me.k * 80, 80), :].astype(F32)
                + part[n].r0[at, :].astype(F32)
            ).astype(BF)
        to_blocks(n, qkv_rows, 80)
    @pl.when((me.zl == 0) & (me.ctx >= 2))
    def _():
        remote(block(s.dkv, 1), block(s.dkvr, 0), (DKV, 0), (me.ctx + 1, me.fsdp))
        remote(block(s.dkv, 2), block(s.dkvr, 2), (DKV, 2), (me.ctx - 2, me.fsdp))

    @pl.when(me.zl == 1)
    def _():
        remote(block(s.dkv, 1), block(s.dkvr, 1), (DKV, 1), (me.ctx - 1, me.fsdp))

    def owners_same(n, axis):
        home = part[n].rb.at[rows(along(me, axis) * 16, 16)]
        own_copy(part[n].ga.at[rows(along(me, axis) * 16, 16)], home, (n, F2))
        for j in (1, 3, 2):
            chip = line_chip(me, axis, j)
            remote(
                part[n].ga.at[rows(chip[axis] * 16, 16)],
                home,
                (n, F2),
                device(*chip, me.k),
            )

    def owners_low(n, axis):
        home = part[n].rb.at[rows(along(me, axis) * 16, 16)]
        for i in range(2):
            for core in range(2):
                if axis == ZA:
                    chip = (me.x, me.y, 2 * i + me.k)
                    here = chip[2] == me.z
                else:
                    chip = (2 * me.k + i, me.y, me.z)
                    here = chip[0] == me.x
                src = part[n].ga.at[pl.ds((i * 2 + core) * 16, 16)]
                mine = here & (me.k == core)

                @pl.when(mine)
                def _():
                    own_copy(src, home, (n, F2))

                @pl.when(jnp.logical_not(mine))
                def _():
                    remote(src, home, (n, F2), device(*chip, core))

    def owners_both(n, axis, slot_of):
        home = part[n].rb.at[rows((me.k * 4 + along(me, axis)) * 16, 16)]
        for j in (0, 1, 3, 2):
            chip = line_chip(me, axis, j)
            for flip in range(2):
                core = lax.rem(me.k + flip, 2)
                src = part[n].ga.at[rows(slot_of(chip[axis], core) * 16, 16)]
                if j == 0 and flip == 0:
                    own_copy(src, home, (n, F2))
                else:
                    remote(src, home, (n, F2), device(*chip, core))

    def spread_owners(n):
        gathered(n, *plane_of[n][1:])
        if n == 1:
            owners_same(1, ZA)
        elif n == 2:
            owners_same(2, XA)
        elif n == GATE:
            owners_both(n, ZA, lambda z, core: (lax.rem(z, 2) * 2 + lax.div(z, 2)) * 2 + core)
        elif n == UP:
            owners_both(n, XA, lambda place, core: core * 4 + place)
        else:
            owners_low(n, XA if n == OUT else ZA)

    for n in (2, 1, 0):
        arrived(part[n].r1, (n, E1))
        total = part[n].gs[rows(along(me, LAST[n]) * 80, 80), :].astype(F32)
        for j in range(3):
            total = total + part[n].r1[j * 80 : j * 80 + 80, :].astype(F32)
        total = total.astype(BF)
        part[n].gp[...] = (
            dot_tn(s.pick5[0, 0:80, 0:256], total[:, 0:256])
            + dot_tn(s.pick5[1, 0:80, 0:256], total[:, 256:512])
        ).astype(BF)
        scatter(n, *plane_of[n])

    arrived(part[OUT].r1, (OUT, E1))
    halves = []
    for i, start in enumerate(out_half_rows(me.z)):
        total = part[OUT].gs[rows(start, 64), :].astype(F32)
        for j in range(3):
            at = (j * 2 + i) * 64
            total = total + part[OUT].r1[at : at + 64, :].astype(F32)
        halves.append(total.astype(BF))
    total = jnp.concatenate(halves, axis=0)
    part[OUT].gp[:, 0:256] = (
        dot_tn(s.pick8[0], total[:, 0:256]) + dot_tn(s.pick8[1], total[:, 384:640])
    ).astype(BF)
    part[OUT].gp[:, 256:384] = dot_tn(s.pick8[0], total[:, 256:384]).astype(BF)
    scatter(OUT, *plane_of[OUT])

    for name in (GATE, UP, DOWN):
        spread_owners(name)

    @pl.when((me.zl == 1) & (me.ctx >= 2))
    def _():
        arrived(block(s.dkvr, 0), (DKV, 0))
        s.dkvs[...] = (s.dkv[2 * TOK :, :].astype(F32) + s.dkvr[0:TOK, :].astype(F32)).astype(BF)
        remote(s.dkvs, block(s.dkvr, 2), (DKV, 2), (me.ctx - 2, me.fsdp))

    e0 = dot_nt(s.dq[:, 0:512], part[0].w[...])
    field = dot_nt(s.dq[:, 512:1024], part[1].w[...])
    e0 = e0 + dot_nt(field.astype(BF), s.orders[0])
    s.e0[...] = e0
    arrived(s.orecv, OO)
    lo[...] = s.outp[...] + s.orecv[...].astype(F32)

    for n in (2, 1, 0, OUT):
        spread_owners(n)

    @pl.when(me.ctx < 6)
    def _():
        arrived(block(s.dkvr, 2), (DKV, 2))

    @pl.when(me.ctx >= 6)
    def _():
        s.dkvr[2 * TOK :, :] = jnp.zeros((TOK, 2 * HEAD), BF)

    @pl.when(me.zl == 0)
    def _():
        arrived(block(s.dkvr, 1), (DKV, 1))

    @pl.when(me.zl == 1)
    def _():
        s.dkvr[TOK : 2 * TOK, :] = jnp.zeros((TOK, 2 * HEAD), BF)

    dkv = (
        s.dkv[0:TOK, :].astype(F32)
        + s.dkvr[TOK : 2 * TOK, :].astype(F32)
        + s.dkvr[2 * TOK :, :].astype(F32)
    ).astype(BF)
    field = dot_nt(dkv, part[2].w[...])
    e0 = s.e0[...] + dot_nt(field.astype(BF), s.orders[1])
    x = s.tokens[0:TOK, :].astype(F32)
    r0 = lax.rsqrt(jnp.mean(x * x, axis=1, keepdims=True) + eps_norm)
    ig[...] = s.dx1[...] + r0 * e0 - x * (r0 * r0 * r0 * jnp.mean(x * e0, axis=1, keepdims=True))

    def line_total(n, out, first):
        base = first * 4
        total = part[n].rb[base : base + 16, :].astype(F32)
        for p in range(1, 4):
            total = total + part[n].rb[base + p * 16 : base + p * 16 + 16, :].astype(F32)
        out[first : first + 16, :] = total

    for n, out in ((GATE, sg), (UP, su), (DOWN, sd), (2, sq2), (1, sq1), (0, sq0), (OUT, so)):
        arrived(part[n].rb, (n, F2))
        line_total(n, out, 0)
        if n in (GATE, UP):
            line_total(n, out, 16)

    def left_or(condition, ref, name, low, high):
        @pl.when(condition)
        def _():
            left(ref.at[pl.ds(0, low)], name)

        @pl.when(jnp.logical_not(condition))
        def _():
            left(ref.at[pl.ds(0, high)], name)

    for n in range(7):
        p = part[n]
        home = {0: me.zl, OUT: xh, DOWN: me.zl}
        if n in home:
            left_or(home[n] == me.k, p.gp, (n, A1), 48, 64)
            left_or(home[n] == me.k, p.gp, (n, F2), 48, 64)
        elif n in (GATE, UP):
            left(p.st.at[pl.ds(0, 7 * 16)], (n, A1))
            left(p.rb.at[pl.ds(0, 7 * 16)], (n, F2))
        else:
            left(p.st.at[pl.ds(0, 48)], (n, A1))
            left(p.rb.at[pl.ds(0, 48)], (n, F2))
        left(p.ra, (n, F1))
    for n in range(3):
        left(part[n].st.at[pl.ds(0, 192)], (n, A2))
        left(part[n].w.at[pl.ds(0, 240)], (n, B1))
        left(part[n].w.at[pl.ds(0, 320)], (n, C))
        left(part[n].r0, (n, D1))
        left(part[n].r1, (n, E1))
    left(part[OUT].st.at[pl.ds(0, 192)], (OUT, A2))
    left(part[OUT].w.at[pl.ds(0, 128)], (OUT, B1))
    left(part[OUT].w.at[pl.ds(0, 256)], (OUT, B2))
    left(part[OUT].w.at[pl.ds(0, 512)], (OUT, C))
    left(part[OUT].r0, (OUT, D1))
    left(part[OUT].r1, (OUT, E1))
    for name in (GATE, UP, DOWN):
        if name == DOWN:
            left(part[name].w.at[pl.ds(0, 192)], (name, A2))
        else:
            left(part[name].st.at[pl.ds(0, 384)], (name, A2))
        block_rows = 256 if name == DOWN else 160
        left(part[name].w.at[pl.ds(0, block_rows)], (name, B1))
        left(part[name].w.at[pl.ds(0, 2 * block_rows)], (name, B2))
        left(part[name].w.at[pl.ds(0, block_rows)], (name, E1))
        left(part[name].w.at[pl.ds(0, 2 * block_rows)], (name, E2))
    left(s.cin, DY)
    left(s.esend, EE)
    left(s.osend, OO)
    left(s.osend, X2)

    @pl.when(me.ctx < 6)
    def _():
        left(block(s.tokens, 0), (TK, 2))

    @pl.when((me.zl == 0) | (me.ctx >= 2))
    def _():
        left(block(s.tokens, 0), (TK, 1))

    @pl.when((me.zl == 0) & (me.ctx >= 2))
    def _():
        left(s.dkvs, (DKV, 0))

    @pl.when(me.ctx >= 2)
    def _():
        left(s.dkvs, (DKV, 2))

    @pl.when(me.zl == 1)
    def _():
        left(s.dkvs, (DKV, 1))

    assert taken[0] <= SEMS


def whole_step(tokens, cotangent, starts, wq, wo, wgu, wd, gains):
    orders, pick5, pick8, rope = constants()
    scratch = scratch_list()
    vmem = pl.BlockSpec(memory_space=pltpu.VMEM)
    anywhere = pl.BlockSpec(memory_space=pl.ANY)
    smem = pl.BlockSpec(memory_space=pltpu.SMEM)
    shapes = [(TOK, D), (TOK, D)] + [(16, 256)] * 3 + [(16, 384), (32, 384), (32, 384), (16, 640)]
    return pl.pallas_call(
        functools.partial(step_kernel, scratch),
        name="whole_step",
        out_shape=[jax.ShapeDtypeStruct(shape, F32) for shape in shapes],
        in_specs=[anywhere, anywhere, smem] + [vmem] * 5 + [anywhere] * 4,
        out_specs=[vmem] * len(shapes),
        scratch_shapes=leaves(scratch)
        + [
            pltpu.SemaphoreType.DMA((12,)),
            pltpu.SemaphoreType.DMA((SEMS,)),
            pltpu.SemaphoreType.DMA((SEMS,)),
        ],
        compiler_params=pltpu.CompilerParams(
            collective_id=0, has_side_effects=True, vmem_limit_bytes=62 * 2**20
        ),
        cost_estimate=pl.CostEstimate(
            flops=12_000_000_000, bytes_accessed=8_000_000, transcendentals=2_000_000
        ),
    )(tokens, cotangent, starts, wq, wo, wgu, wd, gains, orders, pick5, pick8, rope)


def adamw(master, first, second, gradient, rate, decay):
    first_next = beta_one * first + (1.0 - beta_one) * gradient
    second_next = beta_two * second + (1.0 - beta_two) * gradient * gradient
    first_fixed = first_next * (1.0 / (1.0 - beta_one**STEP))
    second_fixed = second_next * (1.0 / (1.0 - beta_two**STEP))
    update = first_fixed / (jnp.sqrt(second_fixed) + eps_adam) + decay * master
    return master - rate * update, first_next, second_next


def update_kernel(*refs):
    inner = refs[41:65]
    sem = refs[65]
    copies = [
        pltpu.make_async_copy(src, dst, sem.at[n])
        for n, (src, dst) in enumerate(zip(refs[:24], inner))
    ]
    for one in copies:
        one.start()
    (sq0, sq1, sq2, so, sg, su, sd) = inner[2:9]
    (wq, qf, qs, wo, of, os_, wgu, gf, gs, wd, df, ds_, gains, nf, ns) = inner[9:]
    (oq, oqf, oqs, oo, oof, oos, og, ogf, ogs, od, odf, ods, on, onf, ons) = refs[26:41]
    for one in copies[:2]:
        one.wait()
    through = [
        pltpu.make_async_copy(inner[n], refs[24 + n].at[0], sem.at[24 + n]) for n in range(2)
    ]
    for one in through:
        one.start()
    for one in copies[2:]:
        one.wait()

    rate = 1.5 * D**-0.5
    gain0 = column(gains[0:1, :])
    gain1 = column(gains[1:2, :])
    total0 = jnp.zeros((5, 1), F32)
    for n, share in enumerate((sq0, sq1, sq2)):
        for g in range(2):
            at = slice(n * 512 + g * 256, n * 512 + g * 256 + 256)
            raw = share[5 * g : 5 * g + 5, :]
            w = wq[:, at]
            total0 = total0 + jnp.sum(w.astype(BF).astype(F32) * raw, axis=1, keepdims=True)
            oq[:, at], oqf[:, at], oqs[:, at] = adamw(
                w, qf[:, at], qs[:, at], raw * gain0, rate, weight_decay
            )
    total1 = jnp.zeros((5, 1), F32)
    for n, share in enumerate((sg, su)):
        for c in range(2):
            for t in range(8):
                g, i = t // 3, t % 3
                base = n * FF + (t // 2) * 512 + c * 256 + (t % 2) * 128
                at = slice(base, base + 128)
                raw = share[c * 16 + 5 * g : c * 16 + 5 * g + 5, i * 128 : i * 128 + 128]
                w = wgu[:, at]
                total1 = total1 + jnp.sum(w.astype(BF).astype(F32) * raw, axis=1, keepdims=True)
                og[:, at], ogf[:, at], ogs[:, at] = adamw(
                    w, gf[:, at], gs[:, at], raw * gain1, rate, weight_decay
                )
    rate = 1.5 * OUT_FAN**-0.5
    for r, at in ((0, slice(0, 384)), (8, slice(384, 640))):
        raw = so[r : r + 8, 0 : at.stop - at.start]
        oo[:, at], oof[:, at], oos[:, at] = adamw(
            wo[:, at], of[:, at], os_[:, at], raw, rate, weight_decay
        )
    od[...], odf[...], ods[...] = adamw(
        wd[...], df[...], ds_[...], sd[...], 1.5 * FF**-0.5, weight_decay
    )
    i = lax.broadcasted_iota(jnp.int32, (5, 5), 0)
    j = lax.broadcasted_iota(jnp.int32, (5, 5), 1)
    for row, total in ((0, total0), (1, total1)):
        flat = jnp.sum(jnp.where(i == j, jnp.broadcast_to(total, (5, 5)), 0.0), axis=0, keepdims=True)
        at = slice(row, row + 1)
        on[at, :], onf[at, :], ons[at, :] = adamw(gains[at, :], nf[at, :], ns[at, :], flat, 0.5, 0.0)
    for one in through:
        one.wait()


def update(*arrays):
    vmem = pl.BlockSpec(memory_space=pltpu.VMEM)
    anywhere = pl.BlockSpec(memory_space=pl.ANY)
    outs = [jax.ShapeDtypeStruct((1, TOK, D), F32)] * 2 + [
        jax.ShapeDtypeStruct(a.shape, F32) for a in arrays[9:]
    ]
    return pl.pallas_call(
        update_kernel,
        name="update",
        out_shape=outs,
        in_specs=[anywhere] * len(arrays),
        out_specs=[anywhere] * 2 + [vmem] * (len(outs) - 2),
        scratch_shapes=[pltpu.VMEM(a.shape, F32) for a in arrays]
        + [pltpu.SemaphoreType.DMA((len(arrays) + 2,))],
        compiler_params=pltpu.CompilerParams(vmem_limit_bytes=60 * 2**20),
    )(*arrays)


def body(
    tokens,
    cotangent,
    starts,
    qkv_weight,
    qkv_first,
    qkv_second,
    out_weight,
    out_first,
    out_second,
    gate_up_weight,
    gate_up_first,
    gate_up_second,
    down_weight,
    down_first,
    down_second,
    norm_gains,
    gains_first,
    gains_second,
):
    results = whole_step(
        tokens, cotangent, starts, qkv_weight, out_weight, gate_up_weight, down_weight, norm_gains
    )
    return tuple(
        update(
            *results,
            qkv_weight,
            qkv_first,
            qkv_second,
            out_weight,
            out_first,
            out_second,
            gate_up_weight,
            gate_up_first,
            gate_up_second,
            down_weight,
            down_first,
            down_second,
            norm_gains,
            gains_first,
            gains_second,
        )
    )


def solution(mesh):
    act = P("fsdp", "ctx", None)
    row = P(("ctx", "fsdp"), None)
    gain = P(None, ("ctx", "fsdp"))
    return jax.shard_map(
        body,
        mesh=mesh,
        in_specs=(act, act, P("fsdp")) + (row,) * 12 + (gain,) * 3,
        out_specs=(act, act) + (row,) * 12 + (gain,) * 3,
        check_vma=False,
    )
```
